256 devices in a mesh: dp: 16 (over x, y), seq: 16 (over z, core).
Axes of the slice: x: 4, y: 4, z: 8, core: 2. Of those that a mesh axis runs over, the one named last changes fastest.
Arguments:
- layer_input: bfloat16 [16, 2048, 4096], P('dp', 'seq'), may hold values from -6 to 6
- queries: bfloat16 [16, 2048, 2048], P('dp', 'seq'), may hold values from -12.5 to 12.5
- keys: bfloat16 [16, 2048, 512], P('dp', 'seq'), may hold values from -5 to 5
- values: bfloat16 [16, 2048, 512], P('dp', 'seq'), may hold values from -6 to 6
- output_grads: bfloat16 [16, 2048, 2048], P('dp', 'seq'), may hold values from -6 to 6
- block_links: int32 [16, 16, 8], P('dp'), may hold values from 0 to 15, as said below
- segment_ids: int32 [16, 2048], P('dp'), may hold values from 0 to 2, never falling along the last dimension, each value on 1 to 1024 neighbouring positions
Outputs:
- query_grads: bfloat16 [16, 2048, 2048], P('dp', 'seq')
- key_grads: bfloat16 [16, 2048, 512], P('dp', 'seq')
- value_grads: bfloat16 [16, 2048, 512], P('dp', 'seq')
- key_weight_grads: float32 [4096, 512], P(('dp', 'seq'))
- value_weight_grads: float32 [4096, 512], P(('dp', 'seq'))
The draws below stay inside these ranges and needn't reach their ends.
Inputs may be any that keep to these rules, and one draw needn't show every extreme that they name: `block_links`: each row of 8 entries names distinct key blocks of its sequence, among them the row's own block, the two blocks beside it (block 15 counting as beside block 0) and block 0.
All inputs are finite; a program needn't handle non-finite values.
Results may differ from the reference program's by a relative error of at most 0.018.
Values may be sent and summed in bfloat16 or wider, within the bound.
No kernel may reach another device: no remote copies, remote signals or barrier semaphores. Data moves between devices by JAX's collectives and lax.ppermute only.
A program may use at most 128 MiB of HBM per device.

```python
import math
import jax
import jax.numpy as jnp
import numpy as np
from jax import lax

D = 4096
HEADS = 16
KV_HEADS = 4
HEAD_DIM = 128
BLOCK = 128
LINKS = 8
DOCS = 16
SEQ = 2048
NQB = 16
GROUP = 4
QW = 2048
KW = 512


def draw_keys(key, part):
    key = jax.random.fold_in(key, 2)
    array_shape = (DOCS, NQB, BLOCK, KV_HEADS, HEAD_DIM)
    entries = jnp.clip(jax.random.normal(key, array_shape, jnp.float32), -4.0, 4.0)
    return entries.reshape(DOCS, SEQ, KW).astype(jnp.bfloat16)


def draw_queries(key, part):
    key = jax.random.fold_in(key, 3)
    array_shape = (DOCS, NQB, BLOCK, HEADS, HEAD_DIM)
    entries = jnp.clip(jax.random.normal(key, array_shape, jnp.float32), -4.0, 4.0)
    return entries.reshape(DOCS, SEQ, QW).astype(jnp.bfloat16)


def draw_block_links(key, part):
    key = jax.random.fold_in(key, 1)
    priority = jax.random.randint(key, (DOCS, NQB, NQB), 0, 65536)
    column_index = jnp.arange(NQB)[None, None, :]
    row_index = jnp.arange(NQB)[None, :, None]
    forced = (column_index == row_index) | (column_index == (row_index + 1) % NQB) | (column_index == (row_index + NQB - 1) % NQB) | (column_index == 0)
    ranking = priority * NQB + column_index + jnp.where(forced, 1073741824, 0)
    chosen = jnp.argsort(-ranking, axis=-1)[..., :LINKS]
    return jnp.sort(chosen, axis=-1).astype(jnp.int32)


def strengthened(values, stream_key, source, target, parts, factor):
    def block_of(position):
        return (jnp.arange(values.shape[position]) // (values.shape[position] // parts)).reshape((-1,) + (1,) * (values.ndim - 1 - position))

    near = jax.random.permutation(stream_key, parts)[block_of(target)]
    other_side = (block_of(target) + parts // 2) % parts
    return jnp.where((block_of(source) == near) | (block_of(source) == other_side), factor * values, values)


def levels(stream_key, shape, cuts, low, top_value):
    def one(axis_at, parts):
        draws = jax.random.uniform(jax.random.fold_in(jax.random.fold_in(stream_key, 6), axis_at), (parts,), jnp.float32, low / len(cuts), top_value / len(cuts))
        return jnp.repeat(jnp.exp(draws), shape[axis_at] // parts).reshape((-1,) + (1,) * (len(shape) - axis_at - 1))

    loudness = one(*cuts[0])
    for cut in cuts[1:]:
        loudness = loudness * one(*cut)
    return loudness


def profile(amount, total, reach, skew):
    weights = [(1 << 20) // math.isqrt(rank ** skew) + 1 for rank in range(2, amount + 1)]
    rest, holding = total - reach - (amount - 1), [1] * (amount - 1)
    while rest > 0:
        candidates = [i for i in range(amount - 1) if holding[i] < reach]
        mass, remaining = sum([weights[i] for i in candidates]), rest
        for i in candidates:
            extra = min(reach - holding[i], max(1, remaining * weights[i] // mass), rest)
            holding[i] = holding[i] + extra
            rest = rest - extra
    return np.array([reach] + holding)


def ragged_sizes(key, count, total, reach, slope):
    if count == 2:
        one = jax.random.randint(key, (), max(1, total - reach), min(reach, total - 1) + 1)
        return jnp.stack([one, total - one])
    sizes = jnp.asarray(profile(count, total, reach, slope), jnp.int32)
    couples = (count - 1) // 2
    source_of, sink = sizes[1:1 + 2 * couples:2], sizes[2:2 + 2 * couples:2]
    slack = jnp.minimum(source_of - 1, reach - sink)
    passed = jax.random.randint(jax.random.fold_in(key, 1), (couples,), 0, 1 << 20) % (slack + 1)
    sizes = sizes.at[1:1 + 2 * couples:2].set(source_of - passed).at[2:2 + 2 * couples:2].set(sink + passed)
    return sizes[jax.random.permutation(jax.random.fold_in(key, 2), count)]


def scatter_about(own_key, shape, spread, reach, cuts=(), dtype=jnp.bfloat16):
    result = jax.random.normal(own_key, shape, jnp.float32) * spread
    if len(cuts) > 0:
        result = levels(own_key, shape, cuts, -0.22, 0.18) * result
    return jnp.clip(result, min=-reach, max=reach).astype(dtype)


def bell_draw_with(own_key, dims, spread, limit, cuts, heavy, held_as=jnp.bfloat16):
    values = spread * jax.random.normal(own_key, dims, jnp.float32)
    if cuts:
        values = values * levels(own_key, dims, cuts, -0.22, 0.18)
    return jnp.clip(strengthened(values, jax.random.fold_in(own_key, 3), *heavy), -limit, limit).astype(held_as)


def setup_inputs(seed: int = 0) -> dict:
    key_list = jax.random.split(jax.random.key(seed), 8)
    return {
        "layer_input": bell_draw_with(key_list[0], (DOCS, SEQ, D), 1.0, 6.0, ((0, 16), (1, 16)), (1, 2, 16, 2.0)),
        "queries": draw_queries(jax.random.fold_in(key_list[7], 71), 0),
        "keys": draw_keys(jax.random.fold_in(key_list[7], 71), 0),
        "values": scatter_about(key_list[3], (DOCS, SEQ, KW), 1.0, 6.0, ((0, 16), (1, 16))),
        "output_grads": scatter_about(key_list[4], (DOCS, SEQ, QW), 1.0, 6.0, ((0, 16), (1, 16))),
        "block_links": draw_block_links(jax.random.fold_in(key_list[7], 71), 0),
        "segment_ids": jax.vmap(lambda own: jnp.searchsorted(jnp.cumsum(ragged_sizes(own, 3, SEQ, SEQ // 2, 0)), jnp.arange(SEQ), side="right"))(jax.random.split(key_list[6], DOCS)).reshape((DOCS, SEQ)).astype(jnp.int32),
    }


def product(einsum_form, first_operand, second_operand):
    return jnp.einsum(einsum_form, first_operand.astype(jnp.float32), second_operand.astype(jnp.float32), precision=lax.Precision.HIGHEST)

def block_grads(query_blocks, key_tiles, grad_blocks, allowed, keep_rows, score_scale):
    head_width = query_blocks.shape[-1]
    key_part = key_tiles[..., :head_width]
    value_part = key_tiles[..., head_width:]
    scores = product('brhe,bce->bhrc', query_blocks, key_part) * score_scale
    scores = jnp.where(allowed[:, None], scores, -1e+30)
    highest = lax.optimization_barrier(jnp.max(scores, axis=-1, keepdims=True))
    log_totals = highest + jnp.log(lax.optimization_barrier(jnp.sum(jnp.exp(scores - highest), axis=-1, keepdims=True)))
    probs = jnp.exp(scores - log_totals) * keep_rows[:, None, None, None]
    attention = probs.astype(jnp.bfloat16)
    attended = product('bhrc,bce->brhe', attention, value_part)
    delta_rows = lax.optimization_barrier(jnp.sum(grad_blocks.astype(jnp.float32) * attended, axis=-1))
    prob_grads = product('brhe,bce->bhrc', grad_blocks, value_part)
    score_grads = (probs * (prob_grads - jnp.transpose(delta_rows, (0, 2, 1))[..., None])).astype(jnp.bfloat16)
    query_part = product('bhrc,bce->brhe', score_grads, key_part) * score_scale
    key_grads = product('bhrc,brhe->bce', score_grads, query_blocks) * score_scale
    value_grads = product('bhrc,brhe->bce', attention, grad_blocks)
    return (query_part, jnp.concatenate([key_grads, value_grads], axis=-1))

def sequence_grads(query_rows, pair_rows, grad_rows, segment_rows, link_rows, score_scale):
    length = query_rows.shape[0]
    block_count = link_rows.shape[0]
    block_rows = length // block_count
    heads_here = query_rows.shape[1]
    head_width = query_rows.shape[2]
    link_count = link_rows.shape[1]
    steps_count = block_count // 4

    def to_steps(array):
        return array.reshape((steps_count, 4, block_rows) + array.shape[1:])
    tile_pairs = pair_rows.reshape(block_count, block_rows, 2 * head_width)
    tile_segments = segment_rows.reshape(block_count, block_rows)
    keep_all = (jnp.arange(block_count) != 0).astype(jnp.float32).reshape(steps_count, 4)

    def one_step(totals, pieces):
        query_part, grad_part, link_part, segment_part, keep_part = pieces
        gathered = jnp.take(tile_pairs, link_part, axis=0).reshape(4, link_count * block_rows, 2 * head_width)
        gathered_segments = jnp.take(tile_segments, link_part, axis=0).reshape(4, link_count * block_rows)
        allowed = segment_part[:, :, None] == gathered_segments[:, None, :]
        query_part_grads, pair_part_grads = block_grads(query_part, gathered, grad_part, allowed, keep_part, score_scale)
        totals = totals.at[link_part.reshape(-1)].add(pair_part_grads.reshape(4 * link_count, block_rows, 2 * head_width))
        return (totals, query_part_grads)
    initial = jnp.zeros((block_count, block_rows, 2 * head_width), jnp.float32)
    totals, query_steps = lax.scan(one_step, initial, (to_steps(query_rows), to_steps(grad_rows), link_rows.reshape(steps_count, 4, link_count), tile_segments.reshape(steps_count, 4, block_rows), keep_all))
    first_allowed = (segment_rows[:block_rows][:, None] == segment_rows[None, :])[None]
    first_query, first_pair = block_grads(query_rows[:block_rows][None], pair_rows[None], grad_rows[:block_rows][None], first_allowed, jnp.ones((1,), jnp.float32), score_scale)
    query_all = jnp.concatenate([first_query[0], query_steps.reshape(length, heads_here, head_width)[block_rows:]], axis=0)
    pair_all = totals.reshape(length, 2 * head_width) + first_pair[0]
    return (query_all, pair_all)

def reference(layer_input, queries, keys, values, output_grads, block_links, segment_ids):
    score_scale = 1.0 / math.sqrt(HEAD_DIM)

    def one_document(pieces):
        query_doc, key_doc, value_doc, grad_doc, link_doc, segment_doc = pieces
        query_groups = jnp.transpose(query_doc.reshape(SEQ, KV_HEADS, GROUP, HEAD_DIM), (1, 0, 2, 3))
        grad_groups = jnp.transpose(grad_doc.reshape(SEQ, KV_HEADS, GROUP, HEAD_DIM), (1, 0, 2, 3))
        pair_groups = jnp.transpose(jnp.concatenate([key_doc.reshape(SEQ, KV_HEADS, HEAD_DIM), value_doc.reshape(SEQ, KV_HEADS, HEAD_DIM)], axis=-1), (1, 0, 2))

        def one_group(group_pieces):
            query_rows, grad_rows, pair_rows = group_pieces
            return sequence_grads(query_rows, pair_rows, grad_rows, segment_doc, link_doc, score_scale)
        query_part, pair_part = lax.map(one_group, (query_groups, grad_groups, pair_groups))
        query_out = jnp.transpose(query_part, (1, 0, 2, 3)).reshape(SEQ, QW).astype(jnp.bfloat16)
        key_out = jnp.transpose(pair_part[..., :HEAD_DIM], (1, 0, 2)).reshape(SEQ, KW).astype(jnp.bfloat16)
        value_out = jnp.transpose(pair_part[..., HEAD_DIM:], (1, 0, 2)).reshape(SEQ, KW).astype(jnp.bfloat16)
        return (query_out, key_out, value_out)
    query_grads, key_grads, value_grads = lax.map(one_document, (queries, keys, values, output_grads, block_links, segment_ids))
    flat_input = layer_input.reshape(DOCS * SEQ, D)
    contract = (((0,), (0,)), ((), ()))
    key_weight_grads = lax.dot_general(flat_input, key_grads.reshape(DOCS * SEQ, KW), contract, preferred_element_type=jnp.float32)
    value_weight_grads = lax.dot_general(flat_input, value_grads.reshape(DOCS * SEQ, KW), contract, preferred_element_type=jnp.float32)
    return (query_grads, key_grads, value_grads, key_weight_grads, value_weight_grads)
```

```python
import math

import jax
import jax.numpy as jnp
from jax import lax
from jax.experimental import pallas as pl
from jax.experimental.pallas import tpu as pltpu
from jax.sharding import Mesh, PartitionSpec as P

NX, NY, NZ, NC = 4, 4, 8, 2
HEAD = 128
BLOCK = 128
BLOCKS = NZ * NC
LINKS = 8
KV_HEADS = 4
MIB = 1 << 20
SCALE = 1.0 / math.sqrt(HEAD)
LOG2E = math.log2(math.e)
MASKED = -1e30


def dot(a, b):
    return lax.dot_general(
        a, b, (((1,), (0,)), ((), ())), preferred_element_type=jnp.float32
    )


def attention_kernel(
    links_ref, core_ref, rows_ref, other_ref, seg_cols_ref, seg_rows_ref,
    dq_ref, own_ref, away_ref, pair_ref, keys_t_ref, total_ref,
):
    core = core_ref[0]

    def load_pairs(i, carry):
        for block, pair in ((2 * i + core, rows_ref[i, :, 4 * HEAD:]), (2 * i + 1 - core, other_ref[i])):
            pair_ref[block] = pair
            keys_t_ref[block] = pair[:, :HEAD].T
        return carry

    lax.fori_loop(0, NZ, load_pairs, 0)
    total_ref[...] = jnp.zeros_like(total_ref)

    def query_block(i, key_blocks):
        block = 2 * i + core
        rows = rows_ref[i]
        queries = jnp.concatenate([rows[:, :HEAD], rows[:, HEAD : 2 * HEAD]], axis=0)
        grads = jnp.concatenate([rows[:, 2 * HEAD : 3 * HEAD], rows[:, 3 * HEAD : 4 * HEAD]], axis=0)
        queries_t, grads_t = queries.T, grads.T
        seg = seg_rows_ref[pl.ds(block, 1), :]
        scores = []
        highest = None
        for j in key_blocks:
            allowed = seg_cols_ref[j] == seg
            s = dot(pair_ref[j, :, :HEAD], queries_t) * (SCALE * LOG2E)
            s = jnp.where(jnp.concatenate([allowed, allowed], axis=1), s, MASKED)
            top = jnp.max(s, axis=0, keepdims=True)
            highest = top if highest is None else jnp.maximum(highest, top)
            scores.append(s)
        weights = []
        norm = None
        for s in scores:
            e = jnp.exp2(s - highest)
            part = jnp.sum(e, axis=0, keepdims=True)
            norm = part if norm is None else norm + part
            weights.append(e)
        inverse = 1.0 / norm
        probs, prob_grads = [], []
        delta = None
        for j, e in zip(key_blocks, weights):
            p = e * inverse
            attention = p.astype(jnp.bfloat16)
            g = dot(pair_ref[j, :, HEAD:], grads_t)
            part = jnp.sum(attention.astype(jnp.float32) * g, axis=0, keepdims=True)
            delta = part if delta is None else delta + part
            total_ref[j, :, HEAD:] += dot(attention, grads)
            probs.append(p)
            prob_grads.append(g)
        dq_t = None
        for j, p, g in zip(key_blocks, probs, prob_grads):
            score_grads = (p * (g - delta)).astype(jnp.bfloat16)
            total_ref[j, :, :HEAD] += dot(score_grads, queries)
            part = dot(keys_t_ref[j], score_grads)
            dq_t = part if dq_t is None else dq_t + part
        dq = (dq_t * SCALE).T
        dq_ref[i, :, :HEAD] = dq[:BLOCK].astype(jnp.bfloat16)
        dq_ref[i, :, HEAD:] = dq[BLOCK:].astype(jnp.bfloat16)

    def linked(i, carry):
        query_block(i, [links_ref[2 * i + core, t] for t in range(LINKS)])
        return carry

    @pl.when(core == 0)
    def _():
        query_block(0, list(range(BLOCKS)))

    lax.fori_loop(1 - core, NZ, linked, 0)

    def store(i, carry):
        for ref, block in ((own_ref, 2 * i + core), (away_ref, 2 * i + 1 - core)):
            ref[i, :, :HEAD] = total_ref[block, :, :HEAD] * SCALE
            ref[i, :, HEAD:] = total_ref[block, :, HEAD:]
        return carry

    lax.fori_loop(0, NZ, store, 0)


def attention_grads(links, core, rows, other, seg_cols, seg_rows):
    vmem = pl.BlockSpec(memory_space=pltpu.VMEM)
    smem = pl.BlockSpec(memory_space=pltpu.SMEM)
    return pl.pallas_call(
        attention_kernel,
        out_shape=(
            jax.ShapeDtypeStruct((NZ, BLOCK, 2 * HEAD), jnp.bfloat16),
            jax.ShapeDtypeStruct((NZ, BLOCK, 2 * HEAD), jnp.float32),
            jax.ShapeDtypeStruct((NZ, BLOCK, 2 * HEAD), jnp.float32),
        ),
        in_specs=[smem, smem, vmem, vmem, vmem, vmem],
        out_specs=(vmem, vmem, vmem),
        scratch_shapes=[
            pltpu.VMEM((BLOCKS, BLOCK, 2 * HEAD), jnp.bfloat16),
            pltpu.VMEM((BLOCKS, HEAD, BLOCK), jnp.bfloat16),
            pltpu.VMEM((BLOCKS, BLOCK, 2 * HEAD), jnp.float32),
        ],
        compiler_params=pltpu.CompilerParams(vmem_limit_bytes=48 * MIB),
        cost_estimate=pl.CostEstimate(
            flops=4_000_000_000, bytes_accessed=8 * MIB, transcendentals=2_500_000
        ),
    )(links, core, rows, other, seg_cols, seg_rows)


def weight_kernel(place_ref, grads_ref, own_ref, other_ref, out_ref, total_ref):
    step = pl.program_id(0)
    x, core = place_ref[0], place_ref[1]

    @pl.when(step == 0)
    def _():
        total_ref[...] = jnp.zeros_like(total_ref)

    total = total_ref[...]
    for s in range(NX):
        source = (lax.rem(x - s + NX, NX) * NY + step) * NC
        grads = jnp.concatenate([grads_ref[source + core], grads_ref[source + 1 - core]], axis=0)
        inputs = jnp.concatenate([own_ref[0, s], other_ref[0, s]], axis=0)
        total = total + dot(grads.T, inputs)
    total_ref[...] = total

    @pl.when(step == NY - 1)
    def _():
        out_ref[...] = total_ref[...].T.astype(jnp.bfloat16)


def weight_grads_part(place, grads, own, other):
    width = own.shape[-1]
    return pl.pallas_call(
        weight_kernel,
        grid=(NY,),
        out_shape=jax.ShapeDtypeStruct((width, HEAD), jnp.bfloat16),
        in_specs=[
            pl.BlockSpec(memory_space=pltpu.SMEM),
            pl.BlockSpec(memory_space=pltpu.VMEM),
            pl.BlockSpec((1, NX, BLOCK, width), lambda i: (i, 0, 0, 0)),
            pl.BlockSpec((1, NX, BLOCK, width), lambda i: (i, 0, 0, 0)),
        ],
        out_specs=pl.BlockSpec((width, HEAD), lambda i: (0, 0)),
        scratch_shapes=[pltpu.VMEM((HEAD, width), jnp.float32)],
        compiler_params=pltpu.CompilerParams(vmem_limit_bytes=32 * MIB),
        cost_estimate=pl.CostEstimate(
            flops=1_100_000_000, bytes_accessed=9 * MIB, transcendentals=0
        ),
    )(place, grads, own, other)


def ring(size, shift):
    return [(i, (i + shift) % size) for i in range(size)]


def swap_cores(a):
    return lax.ppermute(a, "c", [(0, 1), (1, 0)])


def local(layer_input, queries, keys, values, output_grads, block_links, segment_ids):
    x, core = lax.axis_index("x"), lax.axis_index("c")
    bf16 = jnp.bfloat16

    inputs = layer_input[0]
    width = inputs.shape[1] // NX
    pieces = []
    for s in range(NX):
        piece = lax.dynamic_slice_in_dim(inputs, lax.rem(x + s, NX) * width, width, axis=1)
        pieces.append(piece if s == 0 else lax.ppermute(piece, "x", ring(NX, s)))
    inputs_own = lax.all_gather(jnp.stack(pieces), "y", axis=0)

    def by_chip(a):
        return jnp.transpose(a.reshape(BLOCK, NZ, 2 * HEAD), (1, 0, 2))

    def by_key_head(a):
        heads = jnp.transpose(a.reshape(BLOCK, KV_HEADS, HEAD), (1, 0, 2))
        return jnp.repeat(heads, NZ // KV_HEADS, axis=0)

    outgoing = jnp.concatenate(
        [by_chip(queries[0]), by_chip(output_grads[0]), by_key_head(keys[0]), by_key_head(values[0])],
        axis=-1,
    )
    rows = lax.all_to_all(outgoing, "z", split_axis=0, concat_axis=0, tiled=True)
    other = swap_cores(rows[..., 4 * HEAD :])

    seg_rows = segment_ids[0].reshape(BLOCKS, BLOCK)
    seg_cols = jnp.broadcast_to(seg_rows[:, :, None], (BLOCKS, BLOCK, BLOCK))
    dq, own, away = attention_grads(
        block_links[0], core.reshape(1).astype(jnp.int32), rows, other, seg_cols, seg_rows
    )

    pair = (own + swap_cores(away)).astype(bf16)
    pair = lax.all_to_all(pair, "z", split_axis=0, concat_axis=0, tiled=True)
    pair = pair.reshape(KV_HEADS, NZ // KV_HEADS, BLOCK, 2, HEAD).astype(jnp.float32)
    pair = jnp.sum(pair, axis=1).astype(bf16)
    key_grads = jnp.transpose(pair[:, :, 0], (1, 0, 2)).reshape(BLOCK, KV_HEADS * HEAD)
    value_grads = jnp.transpose(pair[:, :, 1], (1, 0, 2)).reshape(BLOCK, KV_HEADS * HEAD)

    dq = lax.all_to_all(dq, "z", split_axis=0, concat_axis=0, tiled=True)
    query_grads = jnp.transpose(dq, (1, 0, 2)).reshape(BLOCK, NZ * 2 * HEAD)

    chunks = jnp.transpose(pair, (0, 2, 1, 3)).reshape(1, NY * NC, BLOCK, HEAD)
    chunks = jnp.broadcast_to(chunks, (NX, NY * NC, BLOCK, HEAD)).reshape(-1, BLOCK, HEAD)
    grads = lax.all_to_all(chunks, ("x", "y", "c"), split_axis=0, concat_axis=0, tiled=True)
    inputs_other = swap_cores(inputs_own)
    place = jnp.stack([x, core]).astype(jnp.int32)
    part = weight_grads_part(place, grads, inputs_own, inputs_other)

    part = part.reshape(NY * NZ * NC, -1, HEAD)
    part = lax.all_to_all(part, ("y", "z", "c"), split_axis=0, concat_axis=0, tiled=True)
    part = part.reshape(NY, NZ, NC, -1, HEAD).astype(jnp.float32)
    part = jnp.transpose(jnp.sum(part, axis=1), (1, 2, 0, 3))
    part = part.reshape(NC, -1, NY * HEAD)
    return query_grads[None], key_grads[None], value_grads[None], part[0], part[1]


def solution(mesh):
    chips = Mesh(mesh.devices.reshape(NX, NY, NZ, NC), ("x", "y", "z", "c"))
    dp, seq = ("x", "y"), ("z", "c")
    by_position = P(dp, seq, None)
    return jax.shard_map(
        local,
        mesh=chips,
        in_specs=(by_position,) * 5 + (P(dp, None, None), P(dp, None)),
        out_specs=(by_position,) * 3 + (P(dp + seq, None),) * 2,
        check_vma=False,
    )
```

```python
import math

import jax
import jax.numpy as jnp
from jax import lax
from jax.experimental import pallas as pl
from jax.experimental.pallas import tpu as pltpu
from jax.sharding import Mesh, PartitionSpec as P

NX, NY, NZ, NC = 4, 4, 8, 2
HEAD = 128
BLOCK = 128
BLOCKS = NZ * NC
LINKS = 8
KV_HEADS = 4
MIB = 1 << 20
SCALE = 1.0 / math.sqrt(HEAD)
LOG2E = math.log2(math.e)
MASKED = -1e30


def dot(a, b):
    return lax.dot_general(
        a, b, (((1,), (0,)), ((), ())), preferred_element_type=jnp.float32
    )


def attention_kernel(
    links_ref, place_ref, rows_ref, other_ref, seg_cols_ref, seg_rows_ref,
    dq_ref, own_ref, away_ref, pair_ref, keys_t_ref, total_ref,
):
    z, core = place_ref[1], place_ref[2]

    def load_pairs(i, carry):
        for block, pair in ((2 * i + core, rows_ref[i, :, 4 * HEAD:]), (2 * i + 1 - core, other_ref[i])):
            pair_ref[block] = pair
            keys_t_ref[block] = pair[:, :HEAD].T
        return carry

    lax.fori_loop(0, NZ, load_pairs, 0)
    total_ref[...] = jnp.zeros_like(total_ref)

    def query_block(i, key_blocks):
        block = 2 * i + core
        rows = rows_ref[i]
        queries = jnp.concatenate([rows[:, :HEAD], rows[:, HEAD : 2 * HEAD]], axis=0)
        grads = jnp.concatenate([rows[:, 2 * HEAD : 3 * HEAD], rows[:, 3 * HEAD : 4 * HEAD]], axis=0)
        queries_t, grads_t = queries.T, grads.T
        seg = seg_rows_ref[pl.ds(block, 1), :]
        scores = []
        highest = None
        for j in key_blocks:
            allowed = seg_cols_ref[j] == seg
            s = dot(pair_ref[j, :, :HEAD], queries_t) * (SCALE * LOG2E)
            s = jnp.where(jnp.concatenate([allowed, allowed], axis=1), s, MASKED)
            top = jnp.max(s, axis=0, keepdims=True)
            highest = top if highest is None else jnp.maximum(highest, top)
            scores.append(s)
        weights = []
        norm = None
        for s in scores:
            e = jnp.exp2(s - highest)
            part = jnp.sum(e, axis=0, keepdims=True)
            norm = part if norm is None else norm + part
            weights.append(e)
        inverse = 1.0 / norm
        probs, prob_grads = [], []
        delta = None
        for j, e in zip(key_blocks, weights):
            p = e * inverse
            attention = p.astype(jnp.bfloat16)
            g = dot(pair_ref[j, :, HEAD:], grads_t)
            part = jnp.sum(attention.astype(jnp.float32) * g, axis=0, keepdims=True)
            delta = part if delta is None else delta + part
            total_ref[j, :, HEAD:] += dot(attention, grads)
            probs.append(p)
            prob_grads.append(g)
        dq_t = None
        for j, p, g in zip(key_blocks, probs, prob_grads):
            score_grads = (p * (g - delta)).astype(jnp.bfloat16)
            total_ref[j, :, :HEAD] += dot(score_grads, queries)
            part = dot(keys_t_ref[j], score_grads)
            dq_t = part if dq_t is None else dq_t + part
        dq = (dq_t * SCALE).T
        slot = lax.rem(i - z + NZ, NZ)
        dq_ref[slot, :, :HEAD] = dq[:BLOCK].astype(jnp.bfloat16)
        dq_ref[slot, :, HEAD:] = dq[BLOCK:].astype(jnp.bfloat16)

    def linked(i, carry):
        query_block(i, [links_ref[2 * i + core, t] for t in range(LINKS)])
        return carry

    @pl.when(core == 0)
    def _():
        query_block(0, list(range(BLOCKS)))

    lax.fori_loop(1 - core, NZ, linked, 0)

    def store(i, carry):
        for ref, block in ((own_ref, 2 * i + core), (away_ref, 2 * i + 1 - core)):
            ref[i, :, :HEAD] = total_ref[block, :, :HEAD] * SCALE
            ref[i, :, HEAD:] = total_ref[block, :, HEAD:]
        return carry

    lax.fori_loop(0, NZ, store, 0)


def attention_grads(links, place, rows, other, seg_cols, seg_rows):
    vmem = pl.BlockSpec(memory_space=pltpu.VMEM)
    smem = pl.BlockSpec(memory_space=pltpu.SMEM)
    return pl.pallas_call(
        attention_kernel,
        out_shape=(
            jax.ShapeDtypeStruct((NZ, BLOCK, 2 * HEAD), jnp.bfloat16),
            jax.ShapeDtypeStruct((NZ, BLOCK, 2 * HEAD), jnp.float32),
            jax.ShapeDtypeStruct((NZ, BLOCK, 2 * HEAD), jnp.float32),
        ),
        in_specs=[smem, smem, vmem, vmem, vmem, vmem],
        out_specs=(vmem, vmem, vmem),
        scratch_shapes=[
            pltpu.VMEM((BLOCKS, BLOCK, 2 * HEAD), jnp.bfloat16),
            pltpu.VMEM((BLOCKS, HEAD, BLOCK), jnp.bfloat16),
            pltpu.VMEM((BLOCKS, BLOCK, 2 * HEAD), jnp.float32),
        ],
        compiler_params=pltpu.CompilerParams(vmem_limit_bytes=48 * MIB),
        cost_estimate=pl.CostEstimate(
            flops=4_000_000_000, bytes_accessed=8 * MIB, transcendentals=2_500_000
        ),
    )(links, place, rows, other, seg_cols, seg_rows)


PARTS = tuple((shift, first) for shift in (0, -1, 1, 2) for first in (0, NX // 2))


def weight_kernel(place_ref, grads_ref, *refs):
    count = len(PARTS)
    out_ref, own_ref, other_ref, sems = refs[2 * count :]
    copies = []
    for p in range(count):
        for side, held in enumerate((own_ref, other_ref)):
            copy = pltpu.make_async_copy(refs[side * count + p], held.at[p], sems.at[side, p])
            copy.start()
            copies.append(copy)
    x, y, core = place_ref[0], place_ref[3], place_ref[2]
    total = None
    for p, (shift, first) in enumerate(PARTS):
        copies[2 * p].wait()
        copies[2 * p + 1].wait()
        for s in range(NX // 2):
            source = (lax.rem(x - first - s + NX, NX) * NY + lax.rem(y + shift + NY, NY)) * NC
            grads = jnp.concatenate([grads_ref[source + core], grads_ref[source + 1 - core]], axis=0)
            inputs = jnp.concatenate([own_ref[p, s], other_ref[p, s]], axis=0)
            part = dot(grads.T, inputs)
            total = part if total is None else total + part
    out_ref[...] = total.T.astype(jnp.bfloat16)


def weight_grads_part(place, grads, own, other):
    shape = own[0].shape
    vmem = pl.BlockSpec(memory_space=pltpu.VMEM)
    held = pltpu.VMEM((len(PARTS),) + shape, jnp.bfloat16)
    return pl.pallas_call(
        weight_kernel,
        out_shape=jax.ShapeDtypeStruct((shape[-1], HEAD), jnp.bfloat16),
        in_specs=[pl.BlockSpec(memory_space=pltpu.SMEM), vmem]
        + [pl.BlockSpec(memory_space=pl.ANY)] * (2 * len(PARTS)),
        out_specs=vmem,
        scratch_shapes=[held, held, pltpu.SemaphoreType.DMA((2, len(PARTS)))],
        compiler_params=pltpu.CompilerParams(vmem_limit_bytes=24 * MIB),
        cost_estimate=pl.CostEstimate(
            flops=1_100_000_000, bytes_accessed=9 * MIB, transcendentals=0
        ),
    )(place, grads, *own, *other)


def pack_kernel(queries_ref, grads_ref, keys_ref, values_ref, out_ref):
    for i in range(NZ):
        heads = slice(2 * HEAD * i, 2 * HEAD * (i + 1))
        shared = slice(HEAD * (i * KV_HEADS // NZ), HEAD * (i * KV_HEADS // NZ + 1))
        out_ref[i, :, : 2 * HEAD] = queries_ref[:, heads]
        out_ref[i, :, 2 * HEAD : 4 * HEAD] = grads_ref[:, heads]
        out_ref[i, :, 4 * HEAD : 5 * HEAD] = keys_ref[:, shared]
        out_ref[i, :, 5 * HEAD :] = values_ref[:, shared]


def packed(queries, grads, keys, values):
    vmem = pl.BlockSpec(memory_space=pltpu.VMEM)
    return pl.pallas_call(
        pack_kernel,
        out_shape=jax.ShapeDtypeStruct((NZ, BLOCK, 6 * HEAD), jnp.bfloat16),
        in_specs=[vmem] * 4,
        out_specs=vmem,
        compiler_params=pltpu.CompilerParams(vmem_limit_bytes=16 * MIB),
        cost_estimate=pl.CostEstimate(flops=0, bytes_accessed=3 * MIB, transcendentals=0),
    )(queries, grads, keys, values)


def pair_kernel(partials_ref, keys_ref, values_ref, chunks_ref):
    for g in range(KV_HEADS):
        pair = partials_ref[2 * g].astype(jnp.float32) + partials_ref[2 * g + 1].astype(jnp.float32)
        pair = pair.astype(jnp.bfloat16)
        for kind, ref in enumerate((keys_ref, values_ref)):
            part = pair[:, kind * HEAD : (kind + 1) * HEAD]
            ref[:, g * HEAD : (g + 1) * HEAD] = part
            for x in range(NX):
                chunks_ref[(x * NY + g) * NC + kind] = part


def pair_grads(partials):
    vmem = pl.BlockSpec(memory_space=pltpu.VMEM)
    out = jax.ShapeDtypeStruct((BLOCK, KV_HEADS * HEAD), jnp.bfloat16)
    return pl.pallas_call(
        pair_kernel,
        out_shape=(out, out, jax.ShapeDtypeStruct((NX * NY * NC, BLOCK, HEAD), jnp.bfloat16)),
        in_specs=[vmem],
        out_specs=(vmem, vmem, vmem),
        compiler_params=pltpu.CompilerParams(vmem_limit_bytes=16 * MIB),
        cost_estimate=pl.CostEstimate(flops=0, bytes_accessed=2 * MIB, transcendentals=0),
    )(partials)


def join_kernel(place_ref, *refs):
    out_ref = refs[-1]
    z = place_ref[1]
    for s in range(NZ):
        column = lax.rem(z - s + NZ, NZ) * (2 * HEAD)
        out_ref[:, pl.ds(pl.multiple_of(column, 2 * HEAD), 2 * HEAD)] = refs[s][...]


def joined(place, pieces):
    vmem = pl.BlockSpec(memory_space=pltpu.VMEM)
    return pl.pallas_call(
        join_kernel,
        out_shape=jax.ShapeDtypeStruct((BLOCK, NZ * 2 * HEAD), jnp.bfloat16),
        in_specs=[pl.BlockSpec(memory_space=pltpu.SMEM)] + [vmem] * NZ,
        out_specs=vmem,
        compiler_params=pltpu.CompilerParams(vmem_limit_bytes=16 * MIB),
        cost_estimate=pl.CostEstimate(flops=0, bytes_accessed=MIB, transcendentals=0),
    )(place, *pieces)


def ring(size, shift):
    return [(i, (i + shift) % size) for i in range(size)]


def swap_cores(a):
    return lax.ppermute(a, "c", [(0, 1), (1, 0)])


def local(layer_input, queries, keys, values, output_grads, block_links, segment_ids):
    x, y, z, core = (lax.axis_index(axis) for axis in ("x", "y", "z", "c"))
    place = jnp.stack([x, z, core, y]).astype(jnp.int32)
    bf16 = jnp.bfloat16

    inputs = layer_input[0]
    width = inputs.shape[1] // NX
    pieces = []
    for s in range(NX):
        piece = lax.dynamic_slice_in_dim(inputs, lax.rem(x + s, NX) * width, width, axis=1)
        pieces.append(piece if s == 0 else lax.ppermute(piece, "x", ring(NX, s)))
    half = NX // 2
    mine = (jnp.stack(pieces[:half]), jnp.stack(pieces[half:]))
    before, after = (
        tuple(lax.ppermute(a, "y", ring(NY, shift)) for a in mine) for shift in (1, -1)
    )

    outgoing = packed(queries[0], output_grads[0], keys[0], values[0])
    rows = lax.all_to_all(outgoing, "z", split_axis=0, concat_axis=0, tiled=True)
    rows, mine = lax.optimization_barrier((rows, mine))
    other = swap_cores(rows[..., 4 * HEAD :])

    seg_rows = segment_ids[0].reshape(BLOCKS, BLOCK)
    seg_cols = jnp.broadcast_to(seg_rows[:, :, None], (BLOCKS, BLOCK, BLOCK))
    dq, own, away = attention_grads(
        block_links[0], place, rows, other, seg_cols, seg_rows
    )

    dq, own, away, before, after = lax.optimization_barrier((dq, own, away, before, after))
    far = (
        lax.ppermute(before[0], "y", ring(NY, 1)),
        lax.ppermute(after[1], "y", ring(NY, -1)),
    )
    inputs_own = mine + before + after
    inputs_other = tuple(swap_cores(a) for a in inputs_own)

    pair = (own + swap_cores(away)).astype(bf16)
    pair = lax.all_to_all(pair, "z", split_axis=0, concat_axis=0, tiled=True)
    dq, pair, inputs_other, far = lax.optimization_barrier((dq, pair, inputs_other, far))
    far_other = tuple(swap_cores(a) for a in far)
    key_grads, value_grads, chunks = pair_grads(pair)

    grads = lax.all_to_all(chunks, ("x", "y", "c"), split_axis=0, concat_axis=0, tiled=True)
    dq = (dq[0],) + tuple(lax.ppermute(dq[s], "z", ring(NZ, s)) for s in range(1, NZ))
    grads, dq, far_other = lax.optimization_barrier((grads, dq, far_other))
    query_grads = joined(place, dq)
    part = weight_grads_part(place, grads, inputs_own + far, inputs_other + far_other)

    part = part.reshape(NY * NZ * NC, -1, HEAD)
    part = lax.all_to_all(part, ("y", "z", "c"), split_axis=0, concat_axis=0, tiled=True)
    part = part.reshape(NY, NZ, NC, -1, HEAD).astype(jnp.float32)
    part = jnp.transpose(jnp.sum(part, axis=1), (1, 2, 0, 3))
    part = part.reshape(NC, -1, NY * HEAD)
    return query_grads[None], key_grads[None], value_grads[None], part[0], part[1]


def solution(mesh):
    chips = Mesh(mesh.devices.reshape(NX, NY, NZ, NC), ("x", "y", "z", "c"))
    dp, seq = ("x", "y"), ("z", "c")
    by_position = P(dp, seq, None)
    return jax.shard_map(
        local,
        mesh=chips,
        in_specs=(by_position,) * 5 + (P(dp, None, None), P(dp, None)),
        out_specs=(by_position,) * 3 + (P(dp + seq, None),) * 2,
        check_vma=False,
    )
```

```python
import math

import jax
import jax.numpy as jnp
from jax import lax
from jax.experimental import pallas as pl
from jax.experimental.pallas import tpu as pltpu
from jax.sharding import Mesh, PartitionSpec as P

NX, NY, NZ, NC = 4, 4, 8, 2
HEAD = 128
BLOCK = 128
BLOCKS = NZ * NC
LINKS = 8
KV_HEADS = 4
MIB = 1 << 20
SCALE = 1.0 / math.sqrt(HEAD)
LOG2E = math.log2(math.e)
MASKED = -1e30


def placed(arrays, space):
    return tuple(pltpu.with_memory_space_constraint(a, space) for a in arrays)


def dot(a, b):
    return lax.dot_general(
        a, b, (((1,), (0,)), ((), ())), preferred_element_type=jnp.float32
    )


def attention_kernel(
    links_ref, place_ref, rows_ref, other_ref, seg_cols_ref, seg_rows_ref,
    dq_ref, own_ref, away_ref, pair_ref, keys_t_ref, total_ref, near_ref, near_t_ref,
):
    z, core = place_ref[1], place_ref[2]

    def at(block):
        return pl.ds(pl.multiple_of(block * BLOCK, BLOCK), BLOCK)

    def load_pairs(i, carry):
        for block, pair in ((2 * i + core, rows_ref[i, :, 4 * HEAD:]), (2 * i + 1 - core, other_ref[i])):
            pair_ref[at(block), :] = pair
            keys_t_ref[:, at(block)] = pair[:, :HEAD].T
        return carry

    lax.fori_loop(0, NZ, load_pairs, 0)
    total_ref[...] = jnp.zeros_like(total_ref)

    def query_block(i, key_blocks, pairs, keys_t):
        rows = rows_ref[i]
        queries = jnp.concatenate([rows[:, :HEAD], rows[:, HEAD : 2 * HEAD]], axis=0)
        grads = jnp.concatenate([rows[:, 2 * HEAD : 3 * HEAD], rows[:, 3 * HEAD : 4 * HEAD]], axis=0)
        queries_t, grads_t = queries.T, grads.T
        seg = seg_rows_ref[pl.ds(2 * i + core, 1), :]
        allowed = jnp.concatenate([seg_cols_ref[j] == seg for j in key_blocks], axis=0)
        scores = dot(pairs[:, :HEAD], queries_t) * (SCALE * LOG2E)
        scores = jnp.where(jnp.concatenate([allowed, allowed], axis=1), scores, MASKED)
        weights = jnp.exp2(scores - jnp.max(scores, axis=0, keepdims=True))
        probs = weights * (1.0 / jnp.sum(weights, axis=0, keepdims=True))
        attention = probs.astype(jnp.bfloat16)
        prob_grads = dot(pairs[:, HEAD:], grads_t)
        delta = jnp.sum(attention.astype(jnp.float32) * prob_grads, axis=0, keepdims=True)
        score_grads = (probs * (prob_grads - delta)).astype(jnp.bfloat16)
        value_part = dot(attention, grads)
        key_part = dot(score_grads, queries)
        for t, j in enumerate(key_blocks):
            here = slice(t * BLOCK, (t + 1) * BLOCK)
            total_ref[at(j), :HEAD] += key_part[here]
            total_ref[at(j), HEAD:] += value_part[here]
        dq = (dot(keys_t, score_grads) * SCALE).T
        slot = lax.rem(i - z + NZ, NZ)
        dq_ref[slot, :, :HEAD] = dq[:BLOCK].astype(jnp.bfloat16)
        dq_ref[slot, :, HEAD:] = dq[BLOCK:].astype(jnp.bfloat16)

    def linked(i, carry):
        key_blocks = [links_ref[2 * i + core, t] for t in range(LINKS)]
        for t, j in enumerate(key_blocks):
            here = slice(t * BLOCK, (t + 1) * BLOCK)
            near_ref[here, :] = pair_ref[at(j), :]
            near_t_ref[:, here] = keys_t_ref[:, at(j)]
        query_block(i, key_blocks, near_ref[...], near_t_ref[...])
        return carry

    @pl.when(core == 0)
    def _():
        query_block(0, list(range(BLOCKS)), pair_ref[...], keys_t_ref[...])

    lax.fori_loop(1 - core, NZ, linked, 0)

    def store(i, carry):
        for ref, block in ((own_ref, 2 * i + core), (away_ref, 2 * i + 1 - core)):
            ref[i, :, :HEAD] = total_ref[at(block), :HEAD] * SCALE
            ref[i, :, HEAD:] = total_ref[at(block), HEAD:]
        return carry

    lax.fori_loop(0, NZ, store, 0)


def attention_grads(links, place, rows, other, seg_cols, seg_rows):
    vmem = pl.BlockSpec(memory_space=pltpu.VMEM)
    smem = pl.BlockSpec(memory_space=pltpu.SMEM)
    return pl.pallas_call(
        attention_kernel,
        out_shape=(
            jax.ShapeDtypeStruct((NZ, BLOCK, 2 * HEAD), jnp.bfloat16),
            jax.ShapeDtypeStruct((NZ, BLOCK, 2 * HEAD), jnp.float32),
            jax.ShapeDtypeStruct((NZ, BLOCK, 2 * HEAD), jnp.float32),
        ),
        in_specs=[smem, smem, vmem, vmem, vmem, vmem],
        out_specs=(vmem, vmem, vmem),
        scratch_shapes=[
            pltpu.VMEM((BLOCKS * BLOCK, 2 * HEAD), jnp.bfloat16),
            pltpu.VMEM((HEAD, BLOCKS * BLOCK), jnp.bfloat16),
            pltpu.VMEM((BLOCKS * BLOCK, 2 * HEAD), jnp.float32),
            pltpu.VMEM((LINKS * BLOCK, 2 * HEAD), jnp.bfloat16),
            pltpu.VMEM((HEAD, LINKS * BLOCK), jnp.bfloat16),
        ],
        compiler_params=pltpu.CompilerParams(vmem_limit_bytes=32 * MIB),
        cost_estimate=pl.CostEstimate(
            flops=4_000_000_000, bytes_accessed=8 * MIB, transcendentals=2_500_000
        ),
    )(links, place, rows, other, seg_cols, seg_rows)


PARTS = tuple((shift, first) for shift in (0, -1, 1, 2) for first in (0, NX // 2))


def weight_kernel(place_ref, grads_ref, *refs):
    out_ref = refs[-1]
    x, y, core = place_ref[0], place_ref[3], place_ref[2]
    total = None
    for p, (shift, first) in enumerate(PARTS):
        for s in range(NX // 2):
            source = (lax.rem(x - first - s + NX, NX) * NY + lax.rem(y + shift + NY, NY)) * NC
            grads = jnp.concatenate([grads_ref[source + core], grads_ref[source + 1 - core]], axis=0)
            inputs = jnp.concatenate([refs[p][s], refs[len(PARTS) + p][s]], axis=0)
            part = dot(grads.T, inputs)
            total = part if total is None else total + part
    out_ref[...] = total.T.astype(jnp.bfloat16)


def weight_grads_part(place, grads, own, other):
    vmem = pl.BlockSpec(memory_space=pltpu.VMEM)
    return pl.pallas_call(
        weight_kernel,
        out_shape=jax.ShapeDtypeStruct((own[0].shape[-1], HEAD), jnp.bfloat16),
        in_specs=[pl.BlockSpec(memory_space=pltpu.SMEM)] + [vmem] * (1 + 2 * len(PARTS)),
        out_specs=vmem,
        compiler_params=pltpu.CompilerParams(vmem_limit_bytes=16 * MIB),
        cost_estimate=pl.CostEstimate(
            flops=1_100_000_000, bytes_accessed=9 * MIB, transcendentals=0
        ),
    )(place, grads, *placed(own, pltpu.VMEM), *placed(other, pltpu.VMEM))


def pack_kernel(queries_ref, grads_ref, keys_ref, values_ref, out_ref, sem):
    copies = []
    for i in range(NZ):
        heads = pl.ds(2 * HEAD * i, 2 * HEAD)
        shared = pl.ds(HEAD * (i * KV_HEADS // NZ), HEAD)
        for ref, source, first, size in (
            (queries_ref, heads, 0, 2), (grads_ref, heads, 2, 2), (keys_ref, shared, 4, 1), (values_ref, shared, 5, 1)
        ):
            target = out_ref.at[i, :, pl.ds(first * HEAD, size * HEAD)]
            copies.append(pltpu.make_async_copy(ref.at[:, source], target, sem.at[len(copies)]))
    for copy in copies:
        copy.start()
    for copy in copies:
        copy.wait()


def packed(queries, grads, keys, values):
    return pl.pallas_call(
        pack_kernel,
        out_shape=jax.ShapeDtypeStruct((NZ, BLOCK, 6 * HEAD), jnp.bfloat16),
        in_specs=[pl.BlockSpec(memory_space=pltpu.HBM)] * 4,
        out_specs=pl.BlockSpec(memory_space=pltpu.VMEM),
        scratch_shapes=[pltpu.SemaphoreType.DMA((4 * NZ,))],
        compiler_params=pltpu.CompilerParams(vmem_limit_bytes=16 * MIB),
        cost_estimate=pl.CostEstimate(flops=0, bytes_accessed=3 * MIB, transcendentals=0),
    )(*placed((queries, grads, keys, values), pltpu.HBM))


def pair_kernel(partials_ref, keys_ref, values_ref, chunks_ref):
    for g in range(KV_HEADS):
        pair = partials_ref[2 * g].astype(jnp.float32) + partials_ref[2 * g + 1].astype(jnp.float32)
        pair = pair.astype(jnp.bfloat16)
        for kind, ref in enumerate((keys_ref, values_ref)):
            part = pair[:, kind * HEAD : (kind + 1) * HEAD]
            ref[:, g * HEAD : (g + 1) * HEAD] = part
            for x in range(NX):
                chunks_ref[(x * NY + g) * NC + kind] = part


def pair_grads(partials):
    vmem = pl.BlockSpec(memory_space=pltpu.VMEM)
    out = jax.ShapeDtypeStruct((BLOCK, KV_HEADS * HEAD), jnp.bfloat16)
    return pl.pallas_call(
        pair_kernel,
        out_shape=(out, out, jax.ShapeDtypeStruct((NX * NY * NC, BLOCK, HEAD), jnp.bfloat16)),
        in_specs=[vmem],
        out_specs=(vmem, vmem, vmem),
        compiler_params=pltpu.CompilerParams(vmem_limit_bytes=16 * MIB),
        cost_estimate=pl.CostEstimate(flops=0, bytes_accessed=2 * MIB, transcendentals=0),
    )(partials)


def join_kernel(place_ref, *refs):
    out_ref = refs[-1]
    z = place_ref[1]
    for s in range(NZ):
        column = lax.rem(z - s + NZ, NZ) * (2 * HEAD)
        out_ref[:, pl.ds(pl.multiple_of(column, 2 * HEAD), 2 * HEAD)] = refs[s][...]


def joined(place, pieces):
    vmem = pl.BlockSpec(memory_space=pltpu.VMEM)
    return pl.pallas_call(
        join_kernel,
        out_shape=jax.ShapeDtypeStruct((BLOCK, NZ * 2 * HEAD), jnp.bfloat16),
        in_specs=[pl.BlockSpec(memory_space=pltpu.SMEM)] + [vmem] * NZ,
        out_specs=vmem,
        compiler_params=pltpu.CompilerParams(vmem_limit_bytes=16 * MIB),
        cost_estimate=pl.CostEstimate(flops=0, bytes_accessed=MIB, transcendentals=0),
    )(place, *pieces)


def ring(size, shift):
    return [(i, (i + shift) % size) for i in range(size)]


def swap_cores(a):
    return lax.ppermute(a, "c", [(0, 1), (1, 0)])


def local(layer_input, queries, keys, values, output_grads, block_links, segment_ids):
    x, y, z, core = (lax.axis_index(axis) for axis in ("x", "y", "z", "c"))
    place = jnp.stack([x, z, core, y]).astype(jnp.int32)
    bf16 = jnp.bfloat16

    inputs = layer_input[0]
    width = inputs.shape[1] // NX
    pieces = [
        lax.dynamic_slice_in_dim(inputs, lax.rem(x + s, NX) * width, width, axis=1)
        for s in range(NX)
    ]
    pieces, queries = lax.optimization_barrier((pieces, queries))
    pieces = [a if s == 0 else lax.ppermute(a, "x", ring(NX, s)) for s, a in enumerate(pieces)]
    half = NX // 2
    mine = (jnp.stack(pieces[:half]), jnp.stack(pieces[half:]))
    before, after = (
        tuple(lax.ppermute(a, "y", ring(NY, shift)) for a in mine) for shift in (1, -1)
    )

    outgoing = packed(queries[0], output_grads[0], keys[0], values[0])
    rows = lax.all_to_all(outgoing, "z", split_axis=0, concat_axis=0, tiled=True)
    rows, mine, before, after = lax.optimization_barrier((rows, mine, before, after))
    other = swap_cores(rows[..., 4 * HEAD :])

    seg_rows = segment_ids[0].reshape(BLOCKS, BLOCK)
    seg_cols = jnp.broadcast_to(seg_rows[:, :, None], (BLOCKS, BLOCK, BLOCK))
    dq, own, away = attention_grads(
        block_links[0], place, rows, other, seg_cols, seg_rows
    )

    dq, own, away, mine, before, after = lax.optimization_barrier(
        (dq, own, away, mine, before, after)
    )
    far = (
        lax.ppermute(before[0], "y", ring(NY, 1)),
        lax.ppermute(after[1], "y", ring(NY, -1)),
    )
    inputs_own = mine + before + after
    inputs_other = tuple(swap_cores(a) for a in inputs_own)

    pair = (own + swap_cores(away)).astype(bf16)
    pair = lax.all_to_all(pair, "z", split_axis=0, concat_axis=0, tiled=True)
    dq, pair, inputs_other, far = lax.optimization_barrier((dq, pair, inputs_other, far))
    far_other = tuple(swap_cores(a) for a in far)
    key_grads, value_grads, chunks = pair_grads(pair)

    grads = lax.all_to_all(chunks, ("x", "y", "c"), split_axis=0, concat_axis=0, tiled=True)
    early, late = (1, 7, 2, 6), (3, 5, 4)
    dq = [dq[s] for s in range(NZ)]
    for s in early:
        dq[s] = lax.ppermute(dq[s], "z", ring(NZ, s))
    grads, dq, far_other = lax.optimization_barrier((grads, dq, far_other))
    part = weight_grads_part(place, grads, inputs_own + far, inputs_other + far_other)

    part, dq = lax.optimization_barrier((part, dq))
    part = part.reshape(NY * NZ * NC, -1, HEAD)
    part = lax.all_to_all(part, ("y", "z", "c"), split_axis=0, concat_axis=0, tiled=True)
    for s in late:
        dq[s] = lax.ppermute(dq[s], "z", ring(NZ, s))
    part, dq = lax.optimization_barrier((part, dq))
    query_grads = joined(place, dq)
    part = part.reshape(NY, NZ, NC, -1, HEAD).astype(jnp.float32)
    part = jnp.transpose(jnp.sum(part, axis=1), (1, 2, 0, 3))
    part = part.reshape(NC, -1, NY * HEAD)
    return query_grads[None], key_grads[None], value_grads[None], part[0], part[1]


def solution(mesh):
    chips = Mesh(mesh.devices.reshape(NX, NY, NZ, NC), ("x", "y", "z", "c"))
    dp, seq = ("x", "y"), ("z", "c")
    by_position = P(dp, seq, None)
    return jax.shard_map(
        local,
        mesh=chips,
        in_specs=(by_position,) * 5 + (P(dp, None, None), P(dp, None)),
        out_specs=(by_position,) * 3 + (P(dp + seq, None),) * 2,
        check_vma=False,
    )
```

```python
import math

import jax
import jax.numpy as jnp
from jax import lax
from jax.experimental import pallas as pl
from jax.experimental.pallas import tpu as pltpu
from jax.sharding import Mesh, PartitionSpec as P

NX, NY, NZ, NC = 4, 4, 8, 2
HEAD = 128
BLOCK = 128
BLOCKS = NZ * NC
LINKS = 8
KV_HEADS = 4
MIB = 1 << 20
SCALE = 1.0 / math.sqrt(HEAD)
LOG2E = math.log2(math.e)
MASKED = -1e30


def placed(arrays, space):
    return tuple(pltpu.with_memory_space_constraint(a, space) for a in arrays)


def dot(a, b):
    return lax.dot_general(
        a, b, (((1,), (0,)), ((), ())), preferred_element_type=jnp.float32
    )


def dot_nt(a, b):
    return lax.dot_general(
        a, b, (((1,), (1,)), ((), ())), preferred_element_type=jnp.float32
    )


def attention_kernel(
    links_ref, place_ref, rows_ref, other_ref, seg_cols_ref, seg_rows_ref, *refs
):
    dq_refs, refs = refs[:NZ], refs[NZ:]
    own_ref, away_ref, pair_ref, keys_t_ref, total_ref, near_ref, near_t_ref, dq_ref = refs
    z, core = place_ref[1], place_ref[2]

    def at(block):
        return pl.ds(pl.multiple_of(block * BLOCK, BLOCK), BLOCK)

    def load_pairs(i, carry):
        for block, pair in ((2 * i + core, rows_ref[i, :, 4 * HEAD:]), (2 * i + 1 - core, other_ref[i])):
            pair_ref[at(block), :] = pair
            keys_t_ref[:, at(block)] = pair[:, :HEAD].T
        return carry

    lax.fori_loop(0, NZ, load_pairs, 0)
    total_ref[...] = jnp.zeros_like(total_ref)

    def query_block(i, key_blocks, pairs, keys_t):
        rows = rows_ref[i]
        queries = jnp.concatenate([rows[:, :HEAD], rows[:, HEAD : 2 * HEAD]], axis=0)
        grads = jnp.concatenate([rows[:, 2 * HEAD : 3 * HEAD], rows[:, 3 * HEAD : 4 * HEAD]], axis=0)
        seg = seg_rows_ref[pl.ds(2 * i + core, 1), :]
        allowed = jnp.concatenate([seg_cols_ref[j] == seg for j in key_blocks], axis=0)
        scores = dot_nt(pairs[:, :HEAD], queries) * (SCALE * LOG2E)
        scores = jnp.where(jnp.concatenate([allowed, allowed], axis=1), scores, MASKED)
        weights = jnp.exp2(scores - jnp.max(scores, axis=0, keepdims=True))
        probs = weights * (1.0 / jnp.sum(weights, axis=0, keepdims=True))
        attention = probs.astype(jnp.bfloat16)
        prob_grads = dot_nt(pairs[:, HEAD:], grads)
        delta = jnp.sum(attention.astype(jnp.float32) * prob_grads, axis=0, keepdims=True)
        score_grads = (probs * (prob_grads - delta)).astype(jnp.bfloat16)
        value_part = dot(attention, grads)
        key_part = dot(score_grads, queries)
        for t, j in enumerate(key_blocks):
            here = slice(t * BLOCK, (t + 1) * BLOCK)
            total_ref[at(j), :HEAD] += key_part[here]
            total_ref[at(j), HEAD:] += value_part[here]
        dq = (dot(keys_t, score_grads) * SCALE).astype(jnp.bfloat16).T
        slot = lax.rem(i - z + NZ, NZ)
        dq_ref[slot, :, :HEAD] = dq[:BLOCK]
        dq_ref[slot, :, HEAD:] = dq[BLOCK:]

    def linked(i, carry):
        key_blocks = [links_ref[2 * i + core, t] for t in range(LINKS)]
        for t, j in enumerate(key_blocks):
            here = slice(t * BLOCK, (t + 1) * BLOCK)
            near_ref[here, :] = pair_ref[at(j), :]
            near_t_ref[:, here] = keys_t_ref[:, at(j)]
        query_block(i, key_blocks, near_ref[...], near_t_ref[...])
        return carry

    @pl.when(core == 0)
    def _():
        query_block(0, list(range(BLOCKS)), pair_ref[...], keys_t_ref[...])

    lax.fori_loop(1 - core, NZ, linked, 0)

    def store(i, carry):
        for ref, block in ((own_ref, 2 * i + core), (away_ref, 2 * i + 1 - core)):
            ref[i, :, :HEAD] = total_ref[at(block), :HEAD] * SCALE
            ref[i, :, HEAD:] = total_ref[at(block), HEAD:]
        return carry

    lax.fori_loop(0, NZ, store, 0)
    for s, ref in enumerate(dq_refs):
        ref[...] = dq_ref[s]


def attention_grads(links, place, rows, other, seg_cols, seg_rows):
    vmem = pl.BlockSpec(memory_space=pltpu.VMEM)
    smem = pl.BlockSpec(memory_space=pltpu.SMEM)
    return pl.pallas_call(
        attention_kernel,
        out_shape=(jax.ShapeDtypeStruct((BLOCK, 2 * HEAD), jnp.bfloat16),) * NZ
        + (
            jax.ShapeDtypeStruct((NZ, BLOCK, 2 * HEAD), jnp.float32),
            jax.ShapeDtypeStruct((NZ, BLOCK, 2 * HEAD), jnp.float32),
        ),
        in_specs=[smem, smem, vmem, vmem, vmem, vmem],
        out_specs=(vmem,) * (NZ + 2),
        scratch_shapes=[
            pltpu.VMEM((BLOCKS * BLOCK, 2 * HEAD), jnp.bfloat16),
            pltpu.VMEM((HEAD, BLOCKS * BLOCK), jnp.bfloat16),
            pltpu.VMEM((BLOCKS * BLOCK, 2 * HEAD), jnp.float32),
            pltpu.VMEM((LINKS * BLOCK, 2 * HEAD), jnp.bfloat16),
            pltpu.VMEM((HEAD, LINKS * BLOCK), jnp.bfloat16),
            pltpu.VMEM((NZ, BLOCK, 2 * HEAD), jnp.bfloat16),
        ],
        compiler_params=pltpu.CompilerParams(vmem_limit_bytes=32 * MIB),
        cost_estimate=pl.CostEstimate(
            flops=4_000_000_000, bytes_accessed=8 * MIB, transcendentals=2_500_000
        ),
    )(links, place, rows, other, seg_cols, seg_rows)


PARTS = tuple((shift, first) for shift in (0, -1, 1, 2) for first in (0, NX // 2))


def weight_kernel(place_ref, grads_ref, *refs):
    count = len(PARTS)
    out_ref, held_ref, sems = refs[2 * count :]
    copies = []
    for p in range(count):
        for side in range(NC):
            target = held_ref.at[p, :, pl.ds(side * BLOCK, BLOCK), :]
            copies.append(pltpu.make_async_copy(refs[side * count + p], target, sems.at[p, side]))
    for copy in copies:
        copy.start()
    x, y, core = place_ref[0], place_ref[3], place_ref[2]
    total = None
    for p, (shift, first) in enumerate(PARTS):
        copies[2 * p].wait()
        copies[2 * p + 1].wait()
        for s in range(NX // 2):
            source = (lax.rem(x - first - s + NX, NX) * NY + lax.rem(y + shift + NY, NY)) * NC
            grads = jnp.concatenate([grads_ref[source + core], grads_ref[source + 1 - core]], axis=0)
            part = dot(grads.T, held_ref[p, s])
            total = part if total is None else total + part
    out_ref[...] = total.T.astype(jnp.bfloat16)


def weight_grads_part(place, grads, own, other):
    half, rows, width = own[0].shape
    vmem = pl.BlockSpec(memory_space=pltpu.VMEM)
    return pl.pallas_call(
        weight_kernel,
        out_shape=jax.ShapeDtypeStruct((width, HEAD), jnp.bfloat16),
        in_specs=[pl.BlockSpec(memory_space=pltpu.SMEM), vmem]
        + [pl.BlockSpec(memory_space=pltpu.HBM)] * (2 * len(PARTS)),
        out_specs=vmem,
        scratch_shapes=[
            pltpu.VMEM((len(PARTS), half, NC * rows, width), jnp.bfloat16),
            pltpu.SemaphoreType.DMA((len(PARTS), NC)),
        ],
        compiler_params=pltpu.CompilerParams(vmem_limit_bytes=24 * MIB),
        cost_estimate=pl.CostEstimate(
            flops=1_100_000_000, bytes_accessed=9 * MIB, transcendentals=0
        ),
    )(place, grads, *placed(own, pltpu.HBM), *placed(other, pltpu.HBM))


def pack_kernel(queries_ref, grads_ref, keys_ref, values_ref, out_ref, sem):
    copies = []
    for i in range(NZ):
        heads = pl.ds(2 * HEAD * i, 2 * HEAD)
        shared = pl.ds(HEAD * (i * KV_HEADS // NZ), HEAD)
        for ref, source, first, size in (
            (queries_ref, heads, 0, 2), (grads_ref, heads, 2, 2), (keys_ref, shared, 4, 1), (values_ref, shared, 5, 1)
        ):
            target = out_ref.at[i, :, pl.ds(first * HEAD, size * HEAD)]
            copies.append(pltpu.make_async_copy(ref.at[:, source], target, sem.at[len(copies)]))
    for copy in copies:
        copy.start()
    for copy in copies:
        copy.wait()


def packed(queries, grads, keys, values):
    return pl.pallas_call(
        pack_kernel,
        out_shape=jax.ShapeDtypeStruct((NZ, BLOCK, 6 * HEAD), jnp.bfloat16),
        in_specs=[pl.BlockSpec(memory_space=pltpu.HBM)] * 4,
        out_specs=pl.BlockSpec(memory_space=pltpu.VMEM),
        scratch_shapes=[pltpu.SemaphoreType.DMA((4 * NZ,))],
        compiler_params=pltpu.CompilerParams(vmem_limit_bytes=16 * MIB),
        cost_estimate=pl.CostEstimate(flops=0, bytes_accessed=3 * MIB, transcendentals=0),
    )(*placed((queries, grads, keys, values), pltpu.HBM))


def pair_kernel(partials_ref, keys_ref, values_ref, chunks_ref):
    for g in range(KV_HEADS):
        pair = partials_ref[2 * g].astype(jnp.float32) + partials_ref[2 * g + 1].astype(jnp.float32)
        pair = pair.astype(jnp.bfloat16)
        for kind, ref in enumerate((keys_ref, values_ref)):
            part = pair[:, kind * HEAD : (kind + 1) * HEAD]
            ref[:, g * HEAD : (g + 1) * HEAD] = part
            for x in range(NX):
                chunks_ref[(x * NY + g) * NC + kind] = part


def pair_grads(partials):
    vmem = pl.BlockSpec(memory_space=pltpu.VMEM)
    out = jax.ShapeDtypeStruct((BLOCK, KV_HEADS * HEAD), jnp.bfloat16)
    return pl.pallas_call(
        pair_kernel,
        out_shape=(out, out, jax.ShapeDtypeStruct((NX * NY * NC, BLOCK, HEAD), jnp.bfloat16)),
        in_specs=[vmem],
        out_specs=(vmem, vmem, vmem),
        compiler_params=pltpu.CompilerParams(vmem_limit_bytes=16 * MIB),
        cost_estimate=pl.CostEstimate(flops=0, bytes_accessed=2 * MIB, transcendentals=0),
    )(partials)


def join_kernel(place_ref, *refs):
    out_ref = refs[-1]
    z = place_ref[1]
    for s in range(NZ):
        column = lax.rem(z - s + NZ, NZ) * (2 * HEAD)
        out_ref[:, pl.ds(pl.multiple_of(column, 2 * HEAD), 2 * HEAD)] = refs[s][...]


def joined(place, pieces):
    vmem = pl.BlockSpec(memory_space=pltpu.VMEM)
    return pl.pallas_call(
        join_kernel,
        out_shape=jax.ShapeDtypeStruct((BLOCK, NZ * 2 * HEAD), jnp.bfloat16),
        in_specs=[pl.BlockSpec(memory_space=pltpu.SMEM)] + [vmem] * NZ,
        out_specs=vmem,
        compiler_params=pltpu.CompilerParams(vmem_limit_bytes=16 * MIB),
        cost_estimate=pl.CostEstimate(flops=0, bytes_accessed=MIB, transcendentals=0),
    )(place, *pieces)


def ring(size, shift):
    return [(i, (i + shift) % size) for i in range(size)]


def swap_cores(a):
    return lax.ppermute(a, "c", [(0, 1), (1, 0)])


def local(layer_input, queries, keys, values, output_grads, block_links, segment_ids):
    x, y, z, core = (lax.axis_index(axis) for axis in ("x", "y", "z", "c"))
    place = jnp.stack([x, z, core, y]).astype(jnp.int32)
    bf16 = jnp.bfloat16

    inputs = layer_input[0]
    width = inputs.shape[1] // NX
    pieces = [
        lax.dynamic_slice_in_dim(inputs, lax.rem(x + s, NX) * width, width, axis=1)
        for s in range(NX)
    ]
    pieces, queries = lax.optimization_barrier((pieces, queries))
    pieces = [a if s == 0 else lax.ppermute(a, "x", ring(NX, s)) for s, a in enumerate(pieces)]
    half = NX // 2
    mine = (jnp.stack(pieces[:half]), jnp.stack(pieces[half:]))
    before, after = (
        tuple(lax.ppermute(a, "y", ring(NY, shift)) for a in mine) for shift in (1, -1)
    )

    outgoing = packed(queries[0], output_grads[0], keys[0], values[0])
    rows = lax.all_to_all(outgoing, "z", split_axis=0, concat_axis=0, tiled=True)
    seg_rows = segment_ids[0].reshape(BLOCKS, BLOCK)
    seg_cols = jnp.broadcast_to(seg_rows[:, :, None], (BLOCKS, BLOCK, BLOCK))
    rows, mine, before, after, seg_cols = lax.optimization_barrier(
        (rows, mine, before, after, seg_cols)
    )
    other = swap_cores(rows[..., 4 * HEAD :])
    *dq, own, away = attention_grads(block_links[0], place, rows, other, seg_cols, seg_rows)

    dq, own, away, mine, before, after = lax.optimization_barrier(
        (dq, own, away, mine, before, after)
    )
    far = (
        lax.ppermute(before[0], "y", ring(NY, 1)),
        lax.ppermute(after[1], "y", ring(NY, -1)),
    )
    inputs_own = mine + before + after
    inputs_other = tuple(swap_cores(a) for a in inputs_own)

    pair = (own + swap_cores(away)).astype(bf16)
    pair = lax.all_to_all(pair, "z", split_axis=0, concat_axis=0, tiled=True)
    for s in (1, 7):
        dq[s] = lax.ppermute(dq[s], "z", ring(NZ, s))
    dq, pair, inputs_other, far = lax.optimization_barrier((dq, pair, inputs_other, far))
    far_other = tuple(swap_cores(a) for a in far)
    key_grads, value_grads, chunks = pair_grads(pair)

    grads = lax.all_to_all(chunks, ("x", "y", "c"), split_axis=0, concat_axis=0, tiled=True)
    for s in (4, 3, 5, 2, 6):
        dq[s] = lax.ppermute(dq[s], "z", ring(NZ, s))
    grads, dq, far_other = lax.optimization_barrier((grads, dq, far_other))
    part = weight_grads_part(place, grads, inputs_own + far, inputs_other + far_other)

    query_grads = joined(place, dq)
    part = part.reshape(NY * NZ * NC, -1, HEAD)
    part = lax.all_to_all(part, ("y", "z", "c"), split_axis=0, concat_axis=0, tiled=True)
    part = part.reshape(NY, NZ, NC, -1, HEAD).astype(jnp.float32)
    part = jnp.transpose(jnp.sum(part, axis=1), (1, 2, 0, 3))
    part = part.reshape(NC, -1, NY * HEAD)
    return query_grads[None], key_grads[None], value_grads[None], part[0], part[1]


def solution(mesh):
    chips = Mesh(mesh.devices.reshape(NX, NY, NZ, NC), ("x", "y", "z", "c"))
    dp, seq = ("x", "y"), ("z", "c")
    by_position = P(dp, seq, None)
    return jax.shard_map(
        local,
        mesh=chips,
        in_specs=(by_position,) * 5 + (P(dp, None, None), P(dp, None)),
        out_specs=(by_position,) * 3 + (P(dp + seq, None),) * 2,
        check_vma=False,
    )
```

```python
import math

import jax
import jax.numpy as jnp
from jax import lax
from jax.experimental import pallas as pl
from jax.experimental.pallas import tpu as pltpu
from jax.sharding import Mesh, PartitionSpec as P

NX, NY, NZ, NC = 4, 4, 8, 2
HEAD = 128
BLOCK = 128
BLOCKS = NZ * NC
LINKS = 8
KV_HEADS = 4
MIB = 1 << 20
SCALE = 1.0 / math.sqrt(HEAD)
LOG2E = math.log2(math.e)
MASKED = -1e30


def placed(arrays, space):
    return tuple(pltpu.with_memory_space_constraint(a, space) for a in arrays)


def dot(a, b):
    return lax.dot_general(
        a, b, (((1,), (0,)), ((), ())), preferred_element_type=jnp.float32
    )


def dot_nt(a, b):
    return lax.dot_general(
        a, b, (((1,), (1,)), ((), ())), preferred_element_type=jnp.float32
    )


def attention_kernel(
    links_ref, place_ref, rows_ref, other_ref, seg_cols_ref, seg_rows_ref, *refs
):
    dq_refs, refs = refs[:NZ], refs[NZ:]
    own_ref, away_ref, pair_ref, keys_t_ref, total_ref, near_ref, near_t_ref, dq_ref, sems = refs
    z, core = place_ref[1], place_ref[2]

    def at(block):
        return pl.ds(pl.multiple_of(block * BLOCK, BLOCK), BLOCK)

    def load_pairs(i, carry):
        for block, pair in ((2 * i + core, rows_ref[i, :, 4 * HEAD:]), (2 * i + 1 - core, other_ref[i])):
            pair_ref[at(block), :] = pair
            keys_t_ref[:, at(block)] = pair[:, :HEAD].T
        return carry

    lax.fori_loop(0, NZ, load_pairs, 0)
    total_ref[...] = jnp.zeros_like(total_ref)

    def query_block(i, key_blocks, pairs, keys_t):
        rows = rows_ref[i]
        queries = jnp.concatenate([rows[:, :HEAD], rows[:, HEAD : 2 * HEAD]], axis=0)
        grads = jnp.concatenate([rows[:, 2 * HEAD : 3 * HEAD], rows[:, 3 * HEAD : 4 * HEAD]], axis=0)
        seg = seg_rows_ref[pl.ds(2 * i + core, 1), :]
        allowed = jnp.concatenate([seg_cols_ref[j] == seg for j in key_blocks], axis=0)
        scores = dot_nt(pairs[:, :HEAD], queries) * (SCALE * LOG2E)
        scores = jnp.where(jnp.concatenate([allowed, allowed], axis=1), scores, MASKED)
        weights = jnp.exp2(scores - jnp.max(scores, axis=0, keepdims=True))
        probs = weights * (1.0 / jnp.sum(weights, axis=0, keepdims=True))
        attention = probs.astype(jnp.bfloat16)
        prob_grads = dot_nt(pairs[:, HEAD:], grads)
        delta = jnp.sum(attention.astype(jnp.float32) * prob_grads, axis=0, keepdims=True)
        score_grads = (probs * (prob_grads - delta)).astype(jnp.bfloat16)
        value_part = dot(attention, grads)
        key_part = dot(score_grads, queries)
        for t, j in enumerate(key_blocks):
            here = slice(t * BLOCK, (t + 1) * BLOCK)
            total_ref[at(j), :HEAD] += key_part[here]
            total_ref[at(j), HEAD:] += value_part[here]
        dq = (dot(keys_t, score_grads) * SCALE).astype(jnp.bfloat16).T
        slot = lax.rem(i - z + NZ, NZ)
        dq_ref[slot, :, :HEAD] = dq[:BLOCK]
        dq_ref[slot, :, HEAD:] = dq[BLOCK:]

    def linked(i, carry):
        key_blocks = [links_ref[2 * i + core, t] for t in range(LINKS)]
        for t, j in enumerate(key_blocks):
            here = slice(t * BLOCK, (t + 1) * BLOCK)
            near_ref[here, :] = pair_ref[at(j), :]
            near_t_ref[:, here] = keys_t_ref[:, at(j)]
        query_block(i, key_blocks, near_ref[...], near_t_ref[...])
        return carry

    @pl.when(core == 0)
    def _():
        query_block(0, list(range(BLOCKS)), pair_ref[...], keys_t_ref[...])

    lax.fori_loop(1 - core, NZ, linked, 0)

    copies = [pltpu.make_async_copy(dq_ref.at[s], dq_refs[s], sems.at[s]) for s in range(NZ)]
    for copy in copies:
        copy.start()

    def store(i, carry):
        for ref, block in ((own_ref, 2 * i + core), (away_ref, 2 * i + 1 - core)):
            ref[i, :, :HEAD] = total_ref[at(block), :HEAD] * SCALE
            ref[i, :, HEAD:] = total_ref[at(block), HEAD:]
        return carry

    lax.fori_loop(0, NZ, store, 0)
    for copy in copies:
        copy.wait()


def attention_grads(links, place, rows, other, seg_cols, seg_rows):
    vmem = pl.BlockSpec(memory_space=pltpu.VMEM)
    smem = pl.BlockSpec(memory_space=pltpu.SMEM)
    return pl.pallas_call(
        attention_kernel,
        out_shape=(pltpu.HBM((BLOCK, 2 * HEAD), jnp.bfloat16),) * NZ
        + (
            jax.ShapeDtypeStruct((NZ, BLOCK, 2 * HEAD), jnp.float32),
            jax.ShapeDtypeStruct((NZ, BLOCK, 2 * HEAD), jnp.float32),
        ),
        in_specs=[smem, smem, vmem, vmem, vmem, vmem],
        out_specs=(pl.BlockSpec(memory_space=pltpu.HBM),) * NZ + (vmem, vmem),
        scratch_shapes=[
            pltpu.VMEM((BLOCKS * BLOCK, 2 * HEAD), jnp.bfloat16),
            pltpu.VMEM((HEAD, BLOCKS * BLOCK), jnp.bfloat16),
            pltpu.VMEM((BLOCKS * BLOCK, 2 * HEAD), jnp.float32),
            pltpu.VMEM((LINKS * BLOCK, 2 * HEAD), jnp.bfloat16),
            pltpu.VMEM((HEAD, LINKS * BLOCK), jnp.bfloat16),
            pltpu.VMEM((NZ, BLOCK, 2 * HEAD), jnp.bfloat16),
            pltpu.SemaphoreType.DMA((NZ,)),
        ],
        compiler_params=pltpu.CompilerParams(vmem_limit_bytes=32 * MIB),
        cost_estimate=pl.CostEstimate(
            flops=4_000_000_000, bytes_accessed=8 * MIB, transcendentals=2_500_000
        ),
    )(links, place, rows, other, seg_cols, seg_rows)


PARTS = tuple((shift, first) for shift in (0, -1, 1, 2) for first in (0, NX // 2))


def weight_kernel(place_ref, grads_ref, *refs):
    count = len(PARTS)
    out_ref, held_ref, sems = refs[2 * count :]
    copies = []
    for p in range(count):
        for side in range(NC):
            target = held_ref.at[p, :, pl.ds(side * BLOCK, BLOCK), :]
            copies.append(pltpu.make_async_copy(refs[side * count + p], target, sems.at[p, side]))
    for copy in copies:
        copy.start()
    x, y, core = place_ref[0], place_ref[3], place_ref[2]
    total = None
    for p, (shift, first) in enumerate(PARTS):
        copies[2 * p].wait()
        copies[2 * p + 1].wait()
        for s in range(NX // 2):
            source = (lax.rem(x - first - s + NX, NX) * NY + lax.rem(y + shift + NY, NY)) * NC
            grads = jnp.concatenate([grads_ref[source + core], grads_ref[source + 1 - core]], axis=0)
            part = dot(grads.T, held_ref[p, s])
            total = part if total is None else total + part
    out_ref[...] = total.T.astype(jnp.bfloat16)


def weight_grads_part(place, grads, own, other):
    half, rows, width = own[0].shape
    vmem = pl.BlockSpec(memory_space=pltpu.VMEM)
    return pl.pallas_call(
        weight_kernel,
        out_shape=jax.ShapeDtypeStruct((width, HEAD), jnp.bfloat16),
        in_specs=[pl.BlockSpec(memory_space=pltpu.SMEM), vmem]
        + [pl.BlockSpec(memory_space=pltpu.HBM)] * (2 * len(PARTS)),
        out_specs=vmem,
        scratch_shapes=[
            pltpu.VMEM((len(PARTS), half, NC * rows, width), jnp.bfloat16),
            pltpu.SemaphoreType.DMA((len(PARTS), NC)),
        ],
        compiler_params=pltpu.CompilerParams(vmem_limit_bytes=24 * MIB),
        cost_estimate=pl.CostEstimate(
            flops=1_100_000_000, bytes_accessed=9 * MIB, transcendentals=0
        ),
    )(place, grads, *placed(own, pltpu.HBM), *placed(other, pltpu.HBM))


def pack_kernel(queries_ref, grads_ref, keys_ref, values_ref, out_ref, sem):
    copies = []
    for i in range(NZ):
        heads = pl.ds(2 * HEAD * i, 2 * HEAD)
        shared = pl.ds(HEAD * (i * KV_HEADS // NZ), HEAD)
        for ref, source, first, size in (
            (queries_ref, heads, 0, 2), (grads_ref, heads, 2, 2), (keys_ref, shared, 4, 1), (values_ref, shared, 5, 1)
        ):
            target = out_ref.at[i, :, pl.ds(first * HEAD, size * HEAD)]
            copies.append(pltpu.make_async_copy(ref.at[:, source], target, sem.at[len(copies)]))
    for copy in copies:
        copy.start()
    for copy in copies:
        copy.wait()


def packed(queries, grads, keys, values):
    return pl.pallas_call(
        pack_kernel,
        out_shape=pltpu.HBM((NZ, BLOCK, 6 * HEAD), jnp.bfloat16),
        in_specs=[pl.BlockSpec(memory_space=pltpu.HBM)] * 4,
        out_specs=pl.BlockSpec(memory_space=pltpu.HBM),
        scratch_shapes=[pltpu.SemaphoreType.DMA((4 * NZ,))],
        compiler_params=pltpu.CompilerParams(vmem_limit_bytes=16 * MIB),
        cost_estimate=pl.CostEstimate(flops=0, bytes_accessed=3 * MIB, transcendentals=0),
    )(*placed((queries, grads, keys, values), pltpu.HBM))


def pair_kernel(partials_ref, keys_ref, values_ref, chunks_ref):
    for g in range(KV_HEADS):
        pair = partials_ref[2 * g].astype(jnp.float32) + partials_ref[2 * g + 1].astype(jnp.float32)
        pair = pair.astype(jnp.bfloat16)
        for kind, ref in enumerate((keys_ref, values_ref)):
            part = pair[:, kind * HEAD : (kind + 1) * HEAD]
            ref[:, g * HEAD : (g + 1) * HEAD] = part
            for x in range(NX):
                chunks_ref[(x * NY + g) * NC + kind] = part


def pair_grads(partials):
    vmem = pl.BlockSpec(memory_space=pltpu.VMEM)
    out = jax.ShapeDtypeStruct((BLOCK, KV_HEADS * HEAD), jnp.bfloat16)
    return pl.pallas_call(
        pair_kernel,
        out_shape=(out, out, jax.ShapeDtypeStruct((NX * NY * NC, BLOCK, HEAD), jnp.bfloat16)),
        in_specs=[vmem],
        out_specs=(vmem, vmem, vmem),
        compiler_params=pltpu.CompilerParams(vmem_limit_bytes=16 * MIB),
        cost_estimate=pl.CostEstimate(flops=0, bytes_accessed=2 * MIB, transcendentals=0),
    )(partials)


def join_kernel(place_ref, *refs):
    out_ref = refs[-1]
    z = place_ref[1]
    for s in range(NZ):
        column = lax.rem(z - s + NZ, NZ) * (2 * HEAD)
        out_ref[:, pl.ds(pl.multiple_of(column, 2 * HEAD), 2 * HEAD)] = refs[s][...]


def joined(place, pieces):
    vmem = pl.BlockSpec(memory_space=pltpu.VMEM)
    return pl.pallas_call(
        join_kernel,
        out_shape=jax.ShapeDtypeStruct((BLOCK, NZ * 2 * HEAD), jnp.bfloat16),
        in_specs=[pl.BlockSpec(memory_space=pltpu.SMEM)] + [vmem] * NZ,
        out_specs=vmem,
        compiler_params=pltpu.CompilerParams(vmem_limit_bytes=16 * MIB),
        cost_estimate=pl.CostEstimate(flops=0, bytes_accessed=MIB, transcendentals=0),
    )(place, *pieces)


def ring(size, shift):
    return [(i, (i + shift) % size) for i in range(size)]


def swap_cores(a):
    return lax.ppermute(a, "c", [(0, 1), (1, 0)])


def local(layer_input, queries, keys, values, output_grads, block_links, segment_ids):
    x, y, z, core = (lax.axis_index(axis) for axis in ("x", "y", "z", "c"))
    place = jnp.stack([x, z, core, y]).astype(jnp.int32)
    bf16 = jnp.bfloat16

    inputs = layer_input[0]
    width = inputs.shape[1] // NX
    pieces = [
        lax.dynamic_slice_in_dim(inputs, lax.rem(x + s, NX) * width, width, axis=1)
        for s in range(NX)
    ]
    pieces = [a if s == 0 else lax.ppermute(a, "x", ring(NX, s)) for s, a in enumerate(pieces)]
    half = NX // 2
    mine = (jnp.stack(pieces[:half]), jnp.stack(pieces[half:]))
    before, after = lax.ppermute(mine[0], "y", ring(NY, 1)), lax.ppermute(mine[1], "y", ring(NY, -1))

    outgoing = packed(queries[0], output_grads[0], keys[0], values[0])
    rows = lax.all_to_all(outgoing, "z", split_axis=0, concat_axis=0, tiled=True)
    seg_rows = segment_ids[0].reshape(BLOCKS, BLOCK)
    seg_cols = jnp.broadcast_to(seg_rows[:, :, None], (BLOCKS, BLOCK, BLOCK))
    rows, mine, before, after, seg_cols = lax.optimization_barrier(
        (rows, mine, before, after, seg_cols)
    )
    other = swap_cores(rows[..., 4 * HEAD :])
    before = (before, lax.ppermute(mine[1], "y", ring(NY, 1)))
    after = (lax.ppermute(mine[0], "y", ring(NY, -1)), after)
    *dq, own, away = attention_grads(block_links[0], place, rows, other, seg_cols, seg_rows)

    dq, own, away, mine, before, after = lax.optimization_barrier(
        (dq, own, away, mine, before, after)
    )
    far = (
        lax.ppermute(before[0], "y", ring(NY, 1)),
        lax.ppermute(after[1], "y", ring(NY, -1)),
    )
    inputs_own = mine + before + after
    inputs_other = tuple(swap_cores(a) for a in inputs_own)

    pair = (own + swap_cores(away)).astype(bf16)
    pair = lax.all_to_all(pair, "z", split_axis=0, concat_axis=0, tiled=True)
    dq, pair, inputs_other, far = lax.optimization_barrier((dq, pair, inputs_other, far))
    far_other = tuple(swap_cores(a) for a in far)
    key_grads, value_grads, chunks = pair_grads(pair)

    grads = lax.all_to_all(chunks, ("x", "y", "c"), split_axis=0, concat_axis=0, tiled=True)
    for s in (1, 7, 2, 6, 3, 5, 4):
        dq[s] = lax.ppermute(dq[s], "z", ring(NZ, s))
    grads, dq, far_other = lax.optimization_barrier((grads, dq, far_other))
    part = weight_grads_part(place, grads, inputs_own + far, inputs_other + far_other)

    query_grads = joined(place, dq)
    part = part.reshape(NY * NZ * NC, -1, HEAD)
    part = lax.all_to_all(part, ("y", "z", "c"), split_axis=0, concat_axis=0, tiled=True)
    part = part.reshape(NY, NZ, NC, -1, HEAD).astype(jnp.float32)
    part = jnp.transpose(jnp.sum(part, axis=1), (1, 2, 0, 3))
    part = part.reshape(NC, -1, NY * HEAD)
    return query_grads[None], key_grads[None], value_grads[None], part[0], part[1]


def solution(mesh):
    chips = Mesh(mesh.devices.reshape(NX, NY, NZ, NC), ("x", "y", "z", "c"))
    dp, seq = ("x", "y"), ("z", "c")
    by_position = P(dp, seq, None)
    return jax.shard_map(
        local,
        mesh=chips,
        in_specs=(by_position,) * 5 + (P(dp, None, None), P(dp, None)),
        out_specs=(by_position,) * 3 + (P(dp + seq, None),) * 2,
        check_vma=False,
    )
```

```python
import math

import jax
import jax.numpy as jnp
from jax import lax
from jax.experimental import pallas as pl
from jax.experimental.pallas import tpu as pltpu
from jax.sharding import Mesh, PartitionSpec as P

NX, NY, NZ, NC = 4, 4, 8, 2
HEAD = 128
BLOCK = 128
BLOCKS = NZ * NC
LINKS = 8
KV_HEADS = 4
SIDE = NZ // 2 - 1
MIB = 1 << 20
SCALE = 1.0 / math.sqrt(HEAD)
LOG2E = math.log2(math.e)
MASKED = -1e30


def placed(arrays, space):
    return tuple(pltpu.with_memory_space_constraint(a, space) for a in arrays)


def dot(a, b):
    return lax.dot_general(
        a, b, (((1,), (0,)), ((), ())), preferred_element_type=jnp.float32
    )


def dot_nt(a, b):
    return lax.dot_general(
        a, b, (((1,), (1,)), ((), ())), preferred_element_type=jnp.float32
    )


def attention_kernel(
    links_ref, place_ref, rows_ref, other_ref, seg_cols_ref, seg_rows_ref, *refs
):
    (keep_ref, across_ref, *ship_refs, give_ref), refs = refs[: SIDE + 3], refs[SIDE + 3 :]
    own_ref, away_ref, pair_ref, keys_t_ref, total_ref, near_ref, near_t_ref, dq_ref, sems = refs
    z, core = place_ref[1], place_ref[2]

    def at(block):
        return pl.ds(pl.multiple_of(block * BLOCK, BLOCK), BLOCK)

    def load_pairs(i, carry):
        for block, pair in ((2 * i + core, rows_ref[i, :, 4 * HEAD:]), (2 * i + 1 - core, other_ref[i])):
            pair_ref[at(block), :] = pair
            keys_t_ref[:, at(block)] = pair[:, :HEAD].T
        return carry

    lax.fori_loop(0, NZ, load_pairs, 0)
    total_ref[...] = jnp.zeros_like(total_ref)

    def query_block(i, key_blocks, pairs, keys_t):
        rows = rows_ref[i]
        queries = jnp.concatenate([rows[:, :HEAD], rows[:, HEAD : 2 * HEAD]], axis=0)
        grads = jnp.concatenate([rows[:, 2 * HEAD : 3 * HEAD], rows[:, 3 * HEAD : 4 * HEAD]], axis=0)
        seg = seg_rows_ref[pl.ds(2 * i + core, 1), :]
        allowed = jnp.concatenate([seg_cols_ref[j] == seg for j in key_blocks], axis=0)
        scores = dot_nt(pairs[:, :HEAD], queries) * (SCALE * LOG2E)
        scores = jnp.where(jnp.concatenate([allowed, allowed], axis=1), scores, MASKED)
        weights = jnp.exp2(scores - jnp.max(scores, axis=0, keepdims=True))
        probs = weights * (1.0 / jnp.sum(weights, axis=0, keepdims=True))
        attention = probs.astype(jnp.bfloat16)
        prob_grads = dot_nt(pairs[:, HEAD:], grads)
        delta = jnp.sum(attention.astype(jnp.float32) * prob_grads, axis=0, keepdims=True)
        score_grads = (probs * (prob_grads - delta)).astype(jnp.bfloat16)
        value_part = dot(attention, grads)
        key_part = dot(score_grads, queries)
        for t, j in enumerate(key_blocks):
            here = slice(t * BLOCK, (t + 1) * BLOCK)
            total_ref[at(j), :HEAD] += key_part[here]
            total_ref[at(j), HEAD:] += value_part[here]
        dq = (dot(keys_t, score_grads) * SCALE).astype(jnp.bfloat16).T
        slot = lax.rem(i - z + NZ, NZ)
        dq_ref[slot, :, :HEAD] = dq[:BLOCK]
        dq_ref[slot, :, HEAD:] = dq[BLOCK:]

    def linked(i, carry):
        key_blocks = [links_ref[2 * i + core, t] for t in range(LINKS)]
        for t, j in enumerate(key_blocks):
            here = slice(t * BLOCK, (t + 1) * BLOCK)
            near_ref[here, :] = pair_ref[at(j), :]
            near_t_ref[:, here] = keys_t_ref[:, at(j)]
        query_block(i, key_blocks, near_ref[...], near_t_ref[...])
        return carry

    @pl.when(core == 0)
    def _():
        query_block(0, list(range(BLOCKS)), pair_ref[...], keys_t_ref[...])

    lax.fori_loop(1 - core, NZ, linked, 0)

    moves = [(0, keep_ref), (NZ // 2, across_ref)]
    for k, ref in enumerate(ship_refs):
        up, down = k + 1, NZ - 1 - k
        moves.append((up + core * (down - up), ref))
        moves.append((down + core * (up - down), give_ref.at[k]))
    copies = [
        pltpu.make_async_copy(dq_ref.at[slot], ref, sems.at[n])
        for n, (slot, ref) in enumerate(moves)
    ]
    for copy in copies:
        copy.start()

    def store(i, carry):
        for ref, block in ((own_ref, 2 * i + core), (away_ref, 2 * i + 1 - core)):
            ref[i, :, :HEAD] = total_ref[at(block), :HEAD] * SCALE
            ref[i, :, HEAD:] = total_ref[at(block), HEAD:]
        return carry

    lax.fori_loop(0, NZ, store, 0)
    for copy in copies:
        copy.wait()


def attention_grads(links, place, rows, other, seg_cols, seg_rows):
    vmem = pl.BlockSpec(memory_space=pltpu.VMEM)
    smem = pl.BlockSpec(memory_space=pltpu.SMEM)
    return pl.pallas_call(
        attention_kernel,
        out_shape=(pltpu.HBM((BLOCK, 2 * HEAD), jnp.bfloat16),) * (SIDE + 2)
        + (pltpu.HBM((SIDE, BLOCK, 2 * HEAD), jnp.bfloat16),)
        + (
            jax.ShapeDtypeStruct((NZ, BLOCK, 2 * HEAD), jnp.float32),
            jax.ShapeDtypeStruct((NZ, BLOCK, 2 * HEAD), jnp.float32),
        ),
        in_specs=[smem, smem, vmem, vmem, vmem, vmem],
        out_specs=(pl.BlockSpec(memory_space=pltpu.HBM),) * (SIDE + 3) + (vmem, vmem),
        scratch_shapes=[
            pltpu.VMEM((BLOCKS * BLOCK, 2 * HEAD), jnp.bfloat16),
            pltpu.VMEM((HEAD, BLOCKS * BLOCK), jnp.bfloat16),
            pltpu.VMEM((BLOCKS * BLOCK, 2 * HEAD), jnp.float32),
            pltpu.VMEM((LINKS * BLOCK, 2 * HEAD), jnp.bfloat16),
            pltpu.VMEM((HEAD, LINKS * BLOCK), jnp.bfloat16),
            pltpu.VMEM((NZ, BLOCK, 2 * HEAD), jnp.bfloat16),
            pltpu.SemaphoreType.DMA((NZ,)),
        ],
        compiler_params=pltpu.CompilerParams(vmem_limit_bytes=32 * MIB),
        cost_estimate=pl.CostEstimate(
            flops=4_000_000_000, bytes_accessed=8 * MIB, transcendentals=2_500_000
        ),
    )(links, place, rows, other, seg_cols, seg_rows)


PARTS = tuple((shift, first) for shift in (0, -1, 1, 2) for first in (0, NX // 2))


AHEAD = 2


def weight_kernel(place_ref, grads_ref, *refs):
    count = len(PARTS)
    out_ref, held_ref, sems = refs[2 * count :]
    copies = []
    for p in range(count):
        for side in range(NC):
            target = held_ref.at[p, :, pl.ds(side * BLOCK, BLOCK), :]
            copies.append(pltpu.make_async_copy(refs[side * count + p], target, sems.at[p, side]))
    for copy in copies[: 2 * AHEAD]:
        copy.start()
    x, y, core = place_ref[0], place_ref[3], place_ref[2]
    total = None
    for p, (shift, first) in enumerate(PARTS):
        for copy in copies[2 * (p + AHEAD) : 2 * (p + AHEAD + 1)]:
            copy.start()
        copies[2 * p].wait()
        copies[2 * p + 1].wait()
        for s in range(NX // 2):
            source = (lax.rem(x - first - s + NX, NX) * NY + lax.rem(y + shift + NY, NY)) * NC
            grads = jnp.concatenate([grads_ref[source + core], grads_ref[source + 1 - core]], axis=0)
            part = dot(grads.T, held_ref[p, s])
            total = part if total is None else total + part
    out_ref[...] = total.T.astype(jnp.bfloat16)


def weight_grads_part(place, grads, own, other):
    half, rows, width = own[0].shape
    vmem = pl.BlockSpec(memory_space=pltpu.VMEM)
    return pl.pallas_call(
        weight_kernel,
        out_shape=jax.ShapeDtypeStruct((width, HEAD), jnp.bfloat16),
        in_specs=[pl.BlockSpec(memory_space=pltpu.SMEM), vmem]
        + [pl.BlockSpec(memory_space=pltpu.HBM)] * (2 * len(PARTS)),
        out_specs=vmem,
        scratch_shapes=[
            pltpu.VMEM((len(PARTS), half, NC * rows, width), jnp.bfloat16),
            pltpu.SemaphoreType.DMA((len(PARTS), NC)),
        ],
        compiler_params=pltpu.CompilerParams(vmem_limit_bytes=24 * MIB),
        cost_estimate=pl.CostEstimate(
            flops=1_100_000_000, bytes_accessed=9 * MIB, transcendentals=0
        ),
    )(place, grads, *placed(own, pltpu.HBM), *placed(other, pltpu.HBM))


def pack_kernel(queries_ref, grads_ref, keys_ref, values_ref, out_ref, sem):
    copies = []
    for i in range(NZ):
        heads = pl.ds(2 * HEAD * i, 2 * HEAD)
        shared = pl.ds(HEAD * (i * KV_HEADS // NZ), HEAD)
        for ref, source, first, size in (
            (queries_ref, heads, 0, 2), (grads_ref, heads, 2, 2), (keys_ref, shared, 4, 1), (values_ref, shared, 5, 1)
        ):
            target = out_ref.at[i, :, pl.ds(first * HEAD, size * HEAD)]
            copies.append(pltpu.make_async_copy(ref.at[:, source], target, sem.at[len(copies)]))
    for copy in copies:
        copy.start()
    for copy in copies:
        copy.wait()


def packed(queries, grads, keys, values):
    return pl.pallas_call(
        pack_kernel,
        out_shape=jax.ShapeDtypeStruct((NZ, BLOCK, 6 * HEAD), jnp.bfloat16),
        in_specs=[pl.BlockSpec(memory_space=pltpu.HBM)] * 4,
        out_specs=pl.BlockSpec(memory_space=pltpu.VMEM),
        scratch_shapes=[pltpu.SemaphoreType.DMA((4 * NZ,))],
        compiler_params=pltpu.CompilerParams(vmem_limit_bytes=16 * MIB),
        cost_estimate=pl.CostEstimate(flops=0, bytes_accessed=3 * MIB, transcendentals=0),
    )(*placed((queries, grads, keys, values), pltpu.HBM))


def pair_kernel(partials_ref, keys_ref, values_ref, chunks_ref):
    for g in range(KV_HEADS):
        pair = partials_ref[2 * g].astype(jnp.float32) + partials_ref[2 * g + 1].astype(jnp.float32)
        pair = pair.astype(jnp.bfloat16)
        for kind, ref in enumerate((keys_ref, values_ref)):
            part = pair[:, kind * HEAD : (kind + 1) * HEAD]
            ref[:, g * HEAD : (g + 1) * HEAD] = part
            for x in range(NX):
                chunks_ref[(x * NY + g) * NC + kind] = part


def pair_grads(partials):
    vmem = pl.BlockSpec(memory_space=pltpu.VMEM)
    out = jax.ShapeDtypeStruct((BLOCK, KV_HEADS * HEAD), jnp.bfloat16)
    return pl.pallas_call(
        pair_kernel,
        out_shape=(out, out, jax.ShapeDtypeStruct((NX * NY * NC, BLOCK, HEAD), jnp.bfloat16)),
        in_specs=[vmem],
        out_specs=(vmem, vmem, vmem),
        compiler_params=pltpu.CompilerParams(vmem_limit_bytes=16 * MIB),
        cost_estimate=pl.CostEstimate(flops=0, bytes_accessed=2 * MIB, transcendentals=0),
    )(partials)


def join_kernel(place_ref, keep_ref, across_ref, *refs):
    direct_refs, swapped_ref, out_ref = refs[:SIDE], refs[SIDE], refs[SIDE + 1]
    z, side = place_ref[1], 1 - 2 * place_ref[2]

    def put(source, value):
        column = lax.rem(source + NZ, NZ) * (2 * HEAD)
        out_ref[:, pl.ds(pl.multiple_of(column, 2 * HEAD), 2 * HEAD)] = value

    put(z, keep_ref[...])
    put(z + NZ // 2, across_ref[...])
    for k in range(SIDE):
        put(z - side * (k + 1), direct_refs[k][0])
        put(z + side * (k + 1), swapped_ref[k])


def joined(place, keep, across, direct, swapped):
    vmem = pl.BlockSpec(memory_space=pltpu.VMEM)
    return pl.pallas_call(
        join_kernel,
        out_shape=jax.ShapeDtypeStruct((BLOCK, NZ * 2 * HEAD), jnp.bfloat16),
        in_specs=[pl.BlockSpec(memory_space=pltpu.SMEM)] + [vmem] * (SIDE + 3),
        out_specs=vmem,
        compiler_params=pltpu.CompilerParams(vmem_limit_bytes=16 * MIB),
        cost_estimate=pl.CostEstimate(flops=0, bytes_accessed=MIB, transcendentals=0),
    )(place, keep, across, *direct, swapped)


def ring(size, shift):
    return [(i, (i + shift) % size) for i in range(size)]


def swap_cores(a):
    return lax.ppermute(a, "c", [(0, 1), (1, 0)])


def local(layer_input, queries, keys, values, output_grads, block_links, segment_ids):
    x, y, z, core = (lax.axis_index(axis) for axis in ("x", "y", "z", "c"))
    place = jnp.stack([x, z, core, y]).astype(jnp.int32)
    bf16 = jnp.bfloat16

    inputs = layer_input[0]
    width = inputs.shape[1] // NX
    pieces = [
        lax.dynamic_slice_in_dim(inputs, lax.rem(x + s, NX) * width, width, axis=1)
        for s in range(NX)
    ]
    pieces = [a if s == 0 else lax.ppermute(a, "x", ring(NX, s)) for s, a in enumerate(pieces)]
    half = NX // 2
    mine = (jnp.stack(pieces[:half]), jnp.stack(pieces[half:]))
    before, after = lax.ppermute(mine[0], "y", ring(NY, 1)), lax.ppermute(mine[1], "y", ring(NY, -1))

    outgoing = packed(queries[0], output_grads[0], keys[0], values[0])
    rows = lax.all_to_all(outgoing, "z", split_axis=0, concat_axis=0, tiled=True)
    seg_rows = segment_ids[0].reshape(BLOCKS, BLOCK)
    seg_cols = jnp.broadcast_to(seg_rows[:, :, None], (BLOCKS, BLOCK, BLOCK))
    rows, mine, before, after, seg_cols = lax.optimization_barrier(
        (rows, mine, before, after, seg_cols)
    )
    other = swap_cores(rows[..., 4 * HEAD :])
    before = (before, lax.ppermute(mine[1], "y", ring(NY, 1)))
    after = (lax.ppermute(mine[0], "y", ring(NY, -1)), after)
    keep, across, *ship, give, own, away = attention_grads(
        block_links[0], place, rows, other, seg_cols, seg_rows
    )
    keep, across, ship, give, own, away, mine, before, after = lax.optimization_barrier(
        (keep, across, ship, give, own, away, mine, before, after)
    )
    far = (
        lax.ppermute(before[0], "y", ring(NY, 1)),
        lax.ppermute(after[1], "y", ring(NY, -1)),
    )
    inputs_own = mine + before + after
    inputs_other = tuple(swap_cores(a) for a in inputs_own)

    pair = (own + swap_cores(away)).astype(bf16)
    pair = lax.all_to_all(pair, "z", split_axis=0, concat_axis=0, tiled=True)
    given = swap_cores(give)
    across, ship, given, pair, inputs_other, far = lax.optimization_barrier(
        (across, ship, given, pair, inputs_other, far)
    )
    far_other = tuple(swap_cores(a) for a in far)
    key_grads, value_grads, chunks = pair_grads(pair)

    grads = lax.all_to_all(chunks, ("x", "y", "c"), split_axis=0, concat_axis=0, tiled=True)
    direct = []
    for k in range(SIDE):
        hops = [((i, 0), ((i + k + 1) % NZ, 0)) for i in range(NZ)]
        hops += [((i, 1), ((i - k - 1) % NZ, 1)) for i in range(NZ)]
        hops = [tuple(a * NC + b for a, b in hop) for hop in hops]
        direct.append(lax.ppermute(jnp.stack([ship[k], given[k]]), ("z", "c"), hops))
    across = lax.ppermute(across, "z", ring(NZ, NZ // 2))
    grads, direct, across, far_other = lax.optimization_barrier((grads, direct, across, far_other))
    part = weight_grads_part(place, grads, inputs_own + far, inputs_other + far_other)

    swapped = swap_cores(jnp.stack([a[1] for a in direct]))
    query_grads = joined(place, keep, across, direct, swapped)
    part = part.reshape(NY * NZ * NC, -1, HEAD)
    part = lax.all_to_all(part, ("y", "z", "c"), split_axis=0, concat_axis=0, tiled=True)
    part = part.reshape(NY, NZ, NC, -1, HEAD).astype(jnp.float32)
    part = jnp.transpose(jnp.sum(part, axis=1), (1, 2, 0, 3))
    part = part.reshape(NC, -1, NY * HEAD)
    return query_grads[None], key_grads[None], value_grads[None], part[0], part[1]


def solution(mesh):
    chips = Mesh(mesh.devices.reshape(NX, NY, NZ, NC), ("x", "y", "z", "c"))
    dp, seq = ("x", "y"), ("z", "c")
    by_position = P(dp, seq, None)
    return jax.shard_map(
        local,
        mesh=chips,
        in_specs=(by_position,) * 5 + (P(dp, None, None), P(dp, None)),
        out_specs=(by_position,) * 3 + (P(dp + seq, None),) * 2,
        check_vma=False,
    )
```

```python
import math

import jax
import jax.numpy as jnp
from jax import lax
from jax.experimental import pallas as pl
from jax.experimental.pallas import tpu as pltpu
from jax.sharding import Mesh, PartitionSpec as P

NX, NY, NZ, NC = 4, 4, 8, 2
HEAD = 128
BLOCK = 128
BLOCKS = NZ * NC
LINKS = 8
KV_HEADS = 4
SIDE = NZ // 2 - 1
MIB = 1 << 20
SCALE = 1.0 / math.sqrt(HEAD)
LOG2E = math.log2(math.e)
MASKED = -1e30


def placed(arrays, space):
    return tuple(pltpu.with_memory_space_constraint(a, space) for a in arrays)


def dot(a, b):
    return lax.dot_general(
        a, b, (((1,), (0,)), ((), ())), preferred_element_type=jnp.float32
    )


def dot_nt(a, b):
    return lax.dot_general(
        a, b, (((1,), (1,)), ((), ())), preferred_element_type=jnp.float32
    )


def attention_kernel(
    links_ref, place_ref, rows_ref, other_ref, seg_cols_ref, seg_rows_ref, *refs
):
    (keep_ref, across_ref, *ship_refs, give_ref), refs = refs[: SIDE + 3], refs[SIDE + 3 :]
    own_ref, away_ref, pair_ref, keys_t_ref, total_ref, near_ref, near_t_ref, dq_ref, sems = refs
    z, core = place_ref[1], place_ref[2]

    def at(block):
        return pl.ds(pl.multiple_of(block * BLOCK, BLOCK), BLOCK)

    def load_pairs(i, carry):
        for block, pair in ((2 * i + core, rows_ref[i, :, 4 * HEAD:]), (2 * i + 1 - core, other_ref[i])):
            pair_ref[at(block), :] = pair
            keys_t_ref[:, at(block)] = pair[:, :HEAD].T
        return carry

    lax.fori_loop(0, NZ, load_pairs, 0)
    total_ref[...] = jnp.zeros_like(total_ref)

    def query_block(i, key_blocks, pairs, keys_t):
        rows = rows_ref[i]
        queries = jnp.concatenate([rows[:, :HEAD], rows[:, HEAD : 2 * HEAD]], axis=0)
        grads = jnp.concatenate([rows[:, 2 * HEAD : 3 * HEAD], rows[:, 3 * HEAD : 4 * HEAD]], axis=0)
        seg = seg_rows_ref[pl.ds(2 * i + core, 1), :]
        allowed = jnp.concatenate([seg_cols_ref[j] == seg for j in key_blocks], axis=0)
        scores = dot_nt(pairs[:, :HEAD], queries) * (SCALE * LOG2E)
        scores = jnp.where(jnp.concatenate([allowed, allowed], axis=1), scores, MASKED)
        weights = jnp.exp2(scores - jnp.max(scores, axis=0, keepdims=True))
        probs = weights * (1.0 / jnp.sum(weights, axis=0, keepdims=True))
        attention = probs.astype(jnp.bfloat16)
        prob_grads = dot_nt(pairs[:, HEAD:], grads)
        delta = jnp.sum(attention.astype(jnp.float32) * prob_grads, axis=0, keepdims=True)
        score_grads = (probs * (prob_grads - delta)).astype(jnp.bfloat16)
        value_part = dot(attention, grads)
        key_part = dot(score_grads, queries)
        for t, j in enumerate(key_blocks):
            here = slice(t * BLOCK, (t + 1) * BLOCK)
            total_ref[at(j), :HEAD] += key_part[here]
            total_ref[at(j), HEAD:] += value_part[here]
        dq = (dot(keys_t, score_grads) * SCALE).astype(jnp.bfloat16).T
        slot = lax.rem(i - z + NZ, NZ)
        dq_ref[slot, :, :HEAD] = dq[:BLOCK]
        dq_ref[slot, :, HEAD:] = dq[BLOCK:]

    def linked(i, carry):
        key_blocks = [links_ref[2 * i + core, t] for t in range(LINKS)]
        for t, j in enumerate(key_blocks):
            here = slice(t * BLOCK, (t + 1) * BLOCK)
            near_ref[here, :] = pair_ref[at(j), :]
            near_t_ref[:, here] = keys_t_ref[:, at(j)]
        query_block(i, key_blocks, near_ref[...], near_t_ref[...])
        return carry

    @pl.when(core == 0)
    def _():
        query_block(0, list(range(BLOCKS)), pair_ref[...], keys_t_ref[...])

    lax.fori_loop(1 - core, NZ, linked, 0)

    moves = [(0, keep_ref), (NZ // 2, across_ref)]
    for k, ref in enumerate(ship_refs):
        up, down = k + 1, NZ - 1 - k
        moves.append((up + core * (down - up), ref))
        moves.append((down + core * (up - down), give_ref.at[k]))
    copies = [
        pltpu.make_async_copy(dq_ref.at[slot], ref, sems.at[n])
        for n, (slot, ref) in enumerate(moves)
    ]
    for copy in copies:
        copy.start()

    def store(i, carry):
        for ref, block in ((own_ref, 2 * i + core), (away_ref, 2 * i + 1 - core)):
            ref[i, :, :HEAD] = total_ref[at(block), :HEAD] * SCALE
            ref[i, :, HEAD:] = total_ref[at(block), HEAD:]
        return carry

    lax.fori_loop(0, NZ, store, 0)
    for copy in copies:
        copy.wait()


def attention_grads(links, place, rows, other, seg_cols, seg_rows):
    vmem = pl.BlockSpec(memory_space=pltpu.VMEM)
    smem = pl.BlockSpec(memory_space=pltpu.SMEM)
    return pl.pallas_call(
        attention_kernel,
        out_shape=(pltpu.HBM((BLOCK, 2 * HEAD), jnp.bfloat16),) * (SIDE + 2)
        + (pltpu.HBM((SIDE, BLOCK, 2 * HEAD), jnp.bfloat16),)
        + (
            jax.ShapeDtypeStruct((NZ, BLOCK, 2 * HEAD), jnp.float32),
            jax.ShapeDtypeStruct((NZ, BLOCK, 2 * HEAD), jnp.float32),
        ),
        in_specs=[smem, smem, vmem, vmem, vmem, vmem],
        out_specs=(pl.BlockSpec(memory_space=pltpu.HBM),) * (SIDE + 3) + (vmem, vmem),
        scratch_shapes=[
            pltpu.VMEM((BLOCKS * BLOCK, 2 * HEAD), jnp.bfloat16),
            pltpu.VMEM((HEAD, BLOCKS * BLOCK), jnp.bfloat16),
            pltpu.VMEM((BLOCKS * BLOCK, 2 * HEAD), jnp.float32),
            pltpu.VMEM((LINKS * BLOCK, 2 * HEAD), jnp.bfloat16),
            pltpu.VMEM((HEAD, LINKS * BLOCK), jnp.bfloat16),
            pltpu.VMEM((NZ, BLOCK, 2 * HEAD), jnp.bfloat16),
            pltpu.SemaphoreType.DMA((NZ,)),
        ],
        compiler_params=pltpu.CompilerParams(vmem_limit_bytes=32 * MIB),
        cost_estimate=pl.CostEstimate(
            flops=4_000_000_000, bytes_accessed=8 * MIB, transcendentals=2_500_000
        ),
    )(links, place, rows, other, seg_cols, seg_rows)


PARTS = tuple((shift, first) for shift in (0, -1, 1, 2) for first in (0, NX // 2))


def weight_kernel(place_ref, grads_ref, *refs):
    count = len(PARTS)
    out_ref, held_ref, sems = refs[2 * count :]
    copies = []
    for p in range(count):
        for side in range(NC):
            target = held_ref.at[p, :, pl.ds(side * BLOCK, BLOCK), :]
            copies.append(pltpu.make_async_copy(refs[side * count + p], target, sems.at[p, side]))
    for copy in copies:
        copy.start()
    x, y, core = place_ref[0], place_ref[3], place_ref[2]
    total = None
    for p, (shift, first) in enumerate(PARTS):
        copies[2 * p].wait()
        copies[2 * p + 1].wait()
        for s in range(NX // 2):
            source = (lax.rem(x - first - s + NX, NX) * NY + lax.rem(y + shift + NY, NY)) * NC
            grads = jnp.concatenate([grads_ref[source + core], grads_ref[source + 1 - core]], axis=0)
            part = dot(grads.T, held_ref[p, s])
            total = part if total is None else total + part
    out_ref[...] = total.T.astype(jnp.bfloat16)


def weight_grads_part(place, grads, own, other):
    half, rows, width = own[0].shape
    vmem = pl.BlockSpec(memory_space=pltpu.VMEM)
    return pl.pallas_call(
        weight_kernel,
        out_shape=jax.ShapeDtypeStruct((width, HEAD), jnp.bfloat16),
        in_specs=[pl.BlockSpec(memory_space=pltpu.SMEM), vmem]
        + [pl.BlockSpec(memory_space=pltpu.HBM)] * (2 * len(PARTS)),
        out_specs=vmem,
        scratch_shapes=[
            pltpu.VMEM((len(PARTS), half, NC * rows, width), jnp.bfloat16),
            pltpu.SemaphoreType.DMA((len(PARTS), NC)),
        ],
        compiler_params=pltpu.CompilerParams(vmem_limit_bytes=24 * MIB),
        cost_estimate=pl.CostEstimate(
            flops=1_100_000_000, bytes_accessed=9 * MIB, transcendentals=0
        ),
    )(place, grads, *placed(own, pltpu.HBM), *placed(other, pltpu.HBM))


def pack_kernel(queries_ref, grads_ref, keys_ref, values_ref, out_ref, sem):
    copies = []
    for i in range(NZ):
        heads = pl.ds(2 * HEAD * i, 2 * HEAD)
        shared = pl.ds(HEAD * (i * KV_HEADS // NZ), HEAD)
        for ref, source, first, size in (
            (queries_ref, heads, 0, 2), (grads_ref, heads, 2, 2), (keys_ref, shared, 4, 1), (values_ref, shared, 5, 1)
        ):
            target = out_ref.at[i, :, pl.ds(first * HEAD, size * HEAD)]
            copies.append(pltpu.make_async_copy(ref.at[:, source], target, sem.at[len(copies)]))
    for copy in copies:
        copy.start()
    for copy in copies:
        copy.wait()


def packed(queries, grads, keys, values):
    return pl.pallas_call(
        pack_kernel,
        out_shape=jax.ShapeDtypeStruct((NZ, BLOCK, 6 * HEAD), jnp.bfloat16),
        in_specs=[pl.BlockSpec(memory_space=pltpu.HBM)] * 4,
        out_specs=pl.BlockSpec(memory_space=pltpu.VMEM),
        scratch_shapes=[pltpu.SemaphoreType.DMA((4 * NZ,))],
        compiler_params=pltpu.CompilerParams(vmem_limit_bytes=16 * MIB),
        cost_estimate=pl.CostEstimate(flops=0, bytes_accessed=3 * MIB, transcendentals=0),
    )(*placed((queries, grads, keys, values), pltpu.HBM))


def pair_kernel(partials_ref, keys_ref, values_ref, chunks_ref):
    for g in range(KV_HEADS):
        pair = partials_ref[2 * g].astype(jnp.float32) + partials_ref[2 * g + 1].astype(jnp.float32)
        pair = pair.astype(jnp.bfloat16)
        for kind, ref in enumerate((keys_ref, values_ref)):
            part = pair[:, kind * HEAD : (kind + 1) * HEAD]
            ref[:, g * HEAD : (g + 1) * HEAD] = part
            for x in range(NX):
                chunks_ref[(x * NY + g) * NC + kind] = part


def pair_grads(partials):
    vmem = pl.BlockSpec(memory_space=pltpu.VMEM)
    out = jax.ShapeDtypeStruct((BLOCK, KV_HEADS * HEAD), jnp.bfloat16)
    return pl.pallas_call(
        pair_kernel,
        out_shape=(out, out, jax.ShapeDtypeStruct((NX * NY * NC, BLOCK, HEAD), jnp.bfloat16)),
        in_specs=[vmem],
        out_specs=(vmem, vmem, vmem),
        compiler_params=pltpu.CompilerParams(vmem_limit_bytes=16 * MIB),
        cost_estimate=pl.CostEstimate(flops=0, bytes_accessed=2 * MIB, transcendentals=0),
    )(partials)


def join_kernel(place_ref, keep_ref, across_ref, *refs):
    direct_refs, swapped_ref, out_ref = refs[:SIDE], refs[SIDE], refs[SIDE + 1]
    z, side = place_ref[1], 1 - 2 * place_ref[2]

    def put(source, value):
        column = lax.rem(source + NZ, NZ) * (2 * HEAD)
        out_ref[:, pl.ds(pl.multiple_of(column, 2 * HEAD), 2 * HEAD)] = value

    put(z, keep_ref[...])
    put(z + NZ // 2, across_ref[...])
    for k in range(SIDE):
        put(z - side * (k + 1), direct_refs[k][0])
        put(z + side * (k + 1), swapped_ref[k])


def joined(place, keep, across, direct, swapped):
    vmem = pl.BlockSpec(memory_space=pltpu.VMEM)
    return pl.pallas_call(
        join_kernel,
        out_shape=jax.ShapeDtypeStruct((BLOCK, NZ * 2 * HEAD), jnp.bfloat16),
        in_specs=[pl.BlockSpec(memory_space=pltpu.SMEM)] + [vmem] * (SIDE + 3),
        out_specs=vmem,
        compiler_params=pltpu.CompilerParams(vmem_limit_bytes=16 * MIB),
        cost_estimate=pl.CostEstimate(flops=0, bytes_accessed=MIB, transcendentals=0),
    )(place, keep, across, *direct, swapped)


def ring(size, shift):
    return [(i, (i + shift) % size) for i in range(size)]


def swap_cores(a):
    return lax.ppermute(a, "c", [(0, 1), (1, 0)])


def local(layer_input, queries, keys, values, output_grads, block_links, segment_ids):
    x, y, z, core = (lax.axis_index(axis) for axis in ("x", "y", "z", "c"))
    place = jnp.stack([x, z, core, y]).astype(jnp.int32)
    bf16 = jnp.bfloat16

    inputs = layer_input[0]
    width = inputs.shape[1] // NX
    pieces = [
        lax.dynamic_slice_in_dim(inputs, lax.rem(x + s, NX) * width, width, axis=1)
        for s in range(NX)
    ]
    pieces = [a if s == 0 else lax.ppermute(a, "x", ring(NX, s)) for s, a in enumerate(pieces)]
    half = NX // 2
    mine = (jnp.stack(pieces[:half]), jnp.stack(pieces[half:]))
    before, after = (
        tuple(lax.ppermute(a, "y", ring(NY, shift)) for a in mine) for shift in (1, -1)
    )

    outgoing = packed(queries[0], output_grads[0], keys[0], values[0])
    rows = lax.all_to_all(outgoing, "z", split_axis=0, concat_axis=0, tiled=True)
    seg_rows = segment_ids[0].reshape(BLOCKS, BLOCK)
    seg_cols = jnp.broadcast_to(seg_rows[:, :, None], (BLOCKS, BLOCK, BLOCK))
    rows, mine, before, after, seg_cols = lax.optimization_barrier(
        (rows, mine, before, after, seg_cols)
    )
    other = swap_cores(rows[..., 4 * HEAD :])
    far = (
        lax.ppermute(before[0], "y", ring(NY, 1)),
        lax.ppermute(after[1], "y", ring(NY, -1)),
    )
    keep, across, *ship, give, own, away = attention_grads(
        block_links[0], place, rows, other, seg_cols, seg_rows
    )
    inputs_own = mine + before + after + far
    keep, across, ship, give, own, away, inputs_own = lax.optimization_barrier(
        (keep, across, ship, give, own, away, inputs_own)
    )
    inputs_other = tuple(swap_cores(a) for a in inputs_own)

    pair = (own + swap_cores(away)).astype(bf16)
    pair = lax.all_to_all(pair, "z", split_axis=0, concat_axis=0, tiled=True)
    given = swap_cores(give)
    across, ship, given, pair, inputs_other = lax.optimization_barrier(
        (across, ship, given, pair, inputs_other)
    )
    key_grads, value_grads, chunks = pair_grads(pair)

    grads = lax.all_to_all(chunks, ("x", "y", "c"), split_axis=0, concat_axis=0, tiled=True)
    direct = []
    for k in range(SIDE):
        hops = [((i, 0), ((i + k + 1) % NZ, 0)) for i in range(NZ)]
        hops += [((i, 1), ((i - k - 1) % NZ, 1)) for i in range(NZ)]
        hops = [tuple(a * NC + b for a, b in hop) for hop in hops]
        direct.append(lax.ppermute(jnp.stack([ship[k], given[k]]), ("z", "c"), hops))
    across = lax.ppermute(across, "z", ring(NZ, NZ // 2))
    grads, direct, across = lax.optimization_barrier((grads, direct, across))
    part = weight_grads_part(place, grads, inputs_own, inputs_other)

    swapped = swap_cores(jnp.stack([a[1] for a in direct]))
    query_grads = joined(place, keep, across, direct, swapped)
    part = part.reshape(NY * NZ * NC, -1, HEAD)
    part = lax.all_to_all(part, ("y", "z", "c"), split_axis=0, concat_axis=0, tiled=True)
    part = part.reshape(NY, NZ, NC, -1, HEAD).astype(jnp.float32)
    part = jnp.transpose(jnp.sum(part, axis=1), (1, 2, 0, 3))
    part = part.reshape(NC, -1, NY * HEAD)
    return query_grads[None], key_grads[None], value_grads[None], part[0], part[1]


def solution(mesh):
    chips = Mesh(mesh.devices.reshape(NX, NY, NZ, NC), ("x", "y", "z", "c"))
    dp, seq = ("x", "y"), ("z", "c")
    by_position = P(dp, seq, None)
    return jax.shard_map(
        local,
        mesh=chips,
        in_specs=(by_position,) * 5 + (P(dp, None, None), P(dp, None)),
        out_specs=(by_position,) * 3 + (P(dp + seq, None),) * 2,
        check_vma=False,
    )
```

```python
import math

import jax
import jax.numpy as jnp
from jax import lax
from jax.experimental import pallas as pl
from jax.experimental.pallas import tpu as pltpu
from jax.sharding import Mesh, PartitionSpec as P

NX, NY, NZ, NC = 4, 4, 8, 2
HEAD = 128
BLOCK = 128
BLOCKS = NZ * NC
LINKS = 8
KV_HEADS = 4
SIDE = NZ // 2 - 1
MIB = 1 << 20
SCALE = 1.0 / math.sqrt(HEAD)
LOG2E = math.log2(math.e)
MASKED = -1e30


def placed(arrays, space):
    return tuple(pltpu.with_memory_space_constraint(a, space) for a in arrays)


def dot(a, b):
    return lax.dot_general(
        a, b, (((1,), (0,)), ((), ())), preferred_element_type=jnp.float32
    )


def dot_nt(a, b):
    return lax.dot_general(
        a, b, (((1,), (1,)), ((), ())), preferred_element_type=jnp.float32
    )


def attention_kernel(
    links_ref, place_ref, rows_ref, other_ref, seg_cols_ref, seg_rows_ref, *refs
):
    (keep_ref, across_ref, *ship_refs, give_ref), refs = refs[: SIDE + 3], refs[SIDE + 3 :]
    own_ref, away_ref, pair_ref, keys_t_ref, total_ref, near_ref, near_t_ref, dq_ref, sems = refs
    z, core = place_ref[1], place_ref[2]

    def at(block):
        return pl.ds(pl.multiple_of(block * BLOCK, BLOCK), BLOCK)

    def load_pairs(i, carry):
        for block, pair in ((2 * i + core, rows_ref[i, :, 4 * HEAD:]), (2 * i + 1 - core, other_ref[i])):
            pair_ref[at(block), :] = pair
            keys_t_ref[:, at(block)] = pair[:, :HEAD].T
        return carry

    lax.fori_loop(0, NZ, load_pairs, 0)
    total_ref[...] = jnp.zeros_like(total_ref)

    def query_block(i, key_blocks, pairs, keys_t):
        rows = rows_ref[i]
        queries = jnp.concatenate([rows[:, :HEAD], rows[:, HEAD : 2 * HEAD]], axis=0)
        grads = jnp.concatenate([rows[:, 2 * HEAD : 3 * HEAD], rows[:, 3 * HEAD : 4 * HEAD]], axis=0)
        seg = seg_rows_ref[pl.ds(2 * i + core, 1), :]
        allowed = jnp.concatenate([seg_cols_ref[j] == seg for j in key_blocks], axis=0)
        scores = dot_nt(pairs[:, :HEAD], queries) * (SCALE * LOG2E)
        scores = jnp.where(jnp.concatenate([allowed, allowed], axis=1), scores, MASKED)
        weights = jnp.exp2(scores - jnp.max(scores, axis=0, keepdims=True))
        probs = weights * (1.0 / jnp.sum(weights, axis=0, keepdims=True))
        attention = probs.astype(jnp.bfloat16)
        prob_grads = dot_nt(pairs[:, HEAD:], grads)
        delta = jnp.sum(attention.astype(jnp.float32) * prob_grads, axis=0, keepdims=True)
        score_grads = (probs * (prob_grads - delta)).astype(jnp.bfloat16)
        value_part = dot(attention, grads)
        key_part = dot(score_grads, queries)
        for t, j in enumerate(key_blocks):
            here = slice(t * BLOCK, (t + 1) * BLOCK)
            total_ref[at(j), :HEAD] += key_part[here]
            total_ref[at(j), HEAD:] += value_part[here]
        dq = (dot(keys_t, score_grads) * SCALE).astype(jnp.bfloat16).T
        slot = lax.rem(i - z + NZ, NZ)
        dq_ref[slot, :, :HEAD] = dq[:BLOCK]
        dq_ref[slot, :, HEAD:] = dq[BLOCK:]

    def linked(i, carry):
        key_blocks = [links_ref[2 * i + core, t] for t in range(LINKS)]
        for t, j in enumerate(key_blocks):
            here = slice(t * BLOCK, (t + 1) * BLOCK)
            near_ref[here, :] = pair_ref[at(j), :]
            near_t_ref[:, here] = keys_t_ref[:, at(j)]
        query_block(i, key_blocks, near_ref[...], near_t_ref[...])
        return carry

    @pl.when(core == 0)
    def _():
        query_block(0, list(range(BLOCKS)), pair_ref[...], keys_t_ref[...])

    lax.fori_loop(1 - core, NZ, linked, 0)

    moves = [(0, keep_ref), (NZ // 2, across_ref)]
    for k, ref in enumerate(ship_refs):
        up, down = k + 1, NZ - 1 - k
        moves.append((up + core * (down - up), ref))
        moves.append((down + core * (up - down), give_ref.at[k]))
    copies = [
        pltpu.make_async_copy(dq_ref.at[slot], ref, sems.at[n])
        for n, (slot, ref) in enumerate(moves)
    ]
    for copy in copies:
        copy.start()

    def store(i, carry):
        for ref, block in ((own_ref, 2 * i + core), (away_ref, 2 * i + 1 - core)):
            ref[i, :, :HEAD] = total_ref[at(block), :HEAD] * SCALE
            ref[i, :, HEAD:] = total_ref[at(block), HEAD:]
        return carry

    lax.fori_loop(0, NZ, store, 0)
    for copy in copies:
        copy.wait()


def attention_grads(links, place, rows, other, seg_cols, seg_rows):
    vmem = pl.BlockSpec(memory_space=pltpu.VMEM)
    smem = pl.BlockSpec(memory_space=pltpu.SMEM)
    return pl.pallas_call(
        attention_kernel,
        out_shape=(pltpu.HBM((BLOCK, 2 * HEAD), jnp.bfloat16),) * (SIDE + 2)
        + (pltpu.HBM((SIDE, BLOCK, 2 * HEAD), jnp.bfloat16),)
        + (
            jax.ShapeDtypeStruct((NZ, BLOCK, 2 * HEAD), jnp.float32),
            jax.ShapeDtypeStruct((NZ, BLOCK, 2 * HEAD), jnp.float32),
        ),
        in_specs=[smem, smem, vmem, vmem, vmem, vmem],
        out_specs=(pl.BlockSpec(memory_space=pltpu.HBM),) * (SIDE + 3) + (vmem, vmem),
        scratch_shapes=[
            pltpu.VMEM((BLOCKS * BLOCK, 2 * HEAD), jnp.bfloat16),
            pltpu.VMEM((HEAD, BLOCKS * BLOCK), jnp.bfloat16),
            pltpu.VMEM((BLOCKS * BLOCK, 2 * HEAD), jnp.float32),
            pltpu.VMEM((LINKS * BLOCK, 2 * HEAD), jnp.bfloat16),
            pltpu.VMEM((HEAD, LINKS * BLOCK), jnp.bfloat16),
            pltpu.VMEM((NZ, BLOCK, 2 * HEAD), jnp.bfloat16),
            pltpu.SemaphoreType.DMA((NZ,)),
        ],
        compiler_params=pltpu.CompilerParams(vmem_limit_bytes=32 * MIB),
        cost_estimate=pl.CostEstimate(
            flops=4_000_000_000, bytes_accessed=8 * MIB, transcendentals=2_500_000
        ),
    )(links, place, rows, other, seg_cols, seg_rows)


PARTS = tuple((shift, first) for shift in (0, -1, 1, 2) for first in (0, NX // 2))


def weight_kernel(place_ref, grads_ref, *refs):
    count = len(PARTS)
    out_ref, held_ref, sems = refs[count:]
    copies = [pltpu.make_async_copy(refs[p], held_ref.at[p], sems.at[p]) for p in range(count)]
    for copy in copies:
        copy.start()
    x, y = place_ref[0], place_ref[3]
    total = None
    for p, (shift, first) in enumerate(PARTS):
        sources = [
            lax.rem(x - s + NX, NX) * NY + lax.rem(y + shift + NY, NY)
            for s in range(first, first + NX // 2)
        ]
        grads = jnp.concatenate([grads_ref[source] for source in sources], axis=0)
        copies[p].wait()
        part = dot(grads.T, held_ref[p].reshape(grads.shape[0], -1))
        total = part if total is None else total + part
    out_ref[...] = total.T.astype(jnp.bfloat16)


def weight_grads_part(place, grads, inputs):
    width = inputs[0].shape[-1]
    vmem = pl.BlockSpec(memory_space=pltpu.VMEM)
    return pl.pallas_call(
        weight_kernel,
        out_shape=jax.ShapeDtypeStruct((width, grads.shape[-1]), jnp.bfloat16),
        in_specs=[pl.BlockSpec(memory_space=pltpu.SMEM), vmem]
        + [pl.BlockSpec(memory_space=pltpu.HBM)] * len(PARTS),
        out_specs=vmem,
        scratch_shapes=[
            pltpu.VMEM((len(PARTS),) + inputs[0].shape, jnp.bfloat16),
            pltpu.SemaphoreType.DMA((len(PARTS),)),
        ],
        compiler_params=pltpu.CompilerParams(vmem_limit_bytes=24 * MIB),
        cost_estimate=pl.CostEstimate(
            flops=1_100_000_000, bytes_accessed=6 * MIB, transcendentals=0
        ),
    )(place, grads, *placed(inputs, pltpu.HBM))


def pack_kernel(queries_ref, grads_ref, keys_ref, values_ref, out_ref, sem):
    copies = []
    for i in range(NZ):
        heads = pl.ds(2 * HEAD * i, 2 * HEAD)
        shared = pl.ds(HEAD * (i * KV_HEADS // NZ), HEAD)
        for ref, source, first, size in (
            (queries_ref, heads, 0, 2), (grads_ref, heads, 2, 2), (keys_ref, shared, 4, 1), (values_ref, shared, 5, 1)
        ):
            target = out_ref.at[i, :, pl.ds(first * HEAD, size * HEAD)]
            copies.append(pltpu.make_async_copy(ref.at[:, source], target, sem.at[len(copies)]))
    for copy in copies:
        copy.start()
    for copy in copies:
        copy.wait()


def packed(queries, grads, keys, values):
    return pl.pallas_call(
        pack_kernel,
        out_shape=jax.ShapeDtypeStruct((NZ, BLOCK, 6 * HEAD), jnp.bfloat16),
        in_specs=[pl.BlockSpec(memory_space=pltpu.HBM)] * 4,
        out_specs=pl.BlockSpec(memory_space=pltpu.VMEM),
        scratch_shapes=[pltpu.SemaphoreType.DMA((4 * NZ,))],
        compiler_params=pltpu.CompilerParams(vmem_limit_bytes=16 * MIB),
        cost_estimate=pl.CostEstimate(flops=0, bytes_accessed=3 * MIB, transcendentals=0),
    )(*placed((queries, grads, keys, values), pltpu.HBM))


def pair_kernel(partials_ref, keys_ref, values_ref, chunks_ref):
    for g in range(KV_HEADS):
        pair = partials_ref[2 * g].astype(jnp.float32) + partials_ref[2 * g + 1].astype(jnp.float32)
        pair = pair.astype(jnp.bfloat16)
        for kind, ref in enumerate((keys_ref, values_ref)):
            ref[:, g * HEAD : (g + 1) * HEAD] = pair[:, kind * HEAD : (kind + 1) * HEAD]
        for x in range(NX):
            chunks_ref[x * NY + g] = pair


def pair_grads(partials):
    vmem = pl.BlockSpec(memory_space=pltpu.VMEM)
    out = jax.ShapeDtypeStruct((BLOCK, KV_HEADS * HEAD), jnp.bfloat16)
    return pl.pallas_call(
        pair_kernel,
        out_shape=(out, out, jax.ShapeDtypeStruct((NX * NY, BLOCK, 2 * HEAD), jnp.bfloat16)),
        in_specs=[vmem],
        out_specs=(vmem, vmem, vmem),
        compiler_params=pltpu.CompilerParams(vmem_limit_bytes=16 * MIB),
        cost_estimate=pl.CostEstimate(flops=0, bytes_accessed=2 * MIB, transcendentals=0),
    )(partials)


def sum_kernel(parts_ref, keys_ref, values_ref):
    count = NZ * NC
    for g in range(KV_HEADS):
        total = parts_ref[g * count].astype(jnp.float32)
        for i in range(1, count):
            total = total + parts_ref[g * count + i].astype(jnp.float32)
        keys_ref[:, g * HEAD : (g + 1) * HEAD] = total[:, :HEAD]
        values_ref[:, g * HEAD : (g + 1) * HEAD] = total[:, HEAD:]


def weight_sums(parts):
    vmem = pl.BlockSpec(memory_space=pltpu.VMEM)
    out = jax.ShapeDtypeStruct((parts.shape[1], KV_HEADS * HEAD), jnp.float32)
    return pl.pallas_call(
        sum_kernel,
        out_shape=(out, out),
        in_specs=[vmem],
        out_specs=(vmem, vmem),
        compiler_params=pltpu.CompilerParams(vmem_limit_bytes=16 * MIB),
        cost_estimate=pl.CostEstimate(flops=500_000, bytes_accessed=MIB, transcendentals=0),
    )(parts)


def join_kernel(place_ref, keep_ref, across_ref, *refs):
    direct_refs, swapped_ref, out_ref = refs[:SIDE], refs[SIDE], refs[SIDE + 1]
    z, side = place_ref[1], 1 - 2 * place_ref[2]

    def put(source, value):
        column = lax.rem(source + NZ, NZ) * (2 * HEAD)
        out_ref[:, pl.ds(pl.multiple_of(column, 2 * HEAD), 2 * HEAD)] = value

    put(z, keep_ref[...])
    put(z + NZ // 2, across_ref[...])
    for k in range(SIDE):
        put(z - side * (k + 1), direct_refs[k][0])
        put(z + side * (k + 1), swapped_ref[k])


def joined(place, keep, across, direct, swapped):
    vmem = pl.BlockSpec(memory_space=pltpu.VMEM)
    return pl.pallas_call(
        join_kernel,
        out_shape=jax.ShapeDtypeStruct((BLOCK, NZ * 2 * HEAD), jnp.bfloat16),
        in_specs=[pl.BlockSpec(memory_space=pltpu.SMEM)] + [vmem] * (SIDE + 3),
        out_specs=vmem,
        compiler_params=pltpu.CompilerParams(vmem_limit_bytes=16 * MIB),
        cost_estimate=pl.CostEstimate(flops=0, bytes_accessed=MIB, transcendentals=0),
    )(place, keep, across, *direct, swapped)


def ring(size, shift):
    return [(i, (i + shift) % size) for i in range(size)]


def swap_cores(a):
    return lax.ppermute(a, "c", [(0, 1), (1, 0)])


def local(layer_input, queries, keys, values, output_grads, block_links, segment_ids):
    x, y, z, core = (lax.axis_index(axis) for axis in ("x", "y", "z", "c"))
    place = jnp.stack([x, z, core, y]).astype(jnp.int32)
    bf16 = jnp.bfloat16

    inputs = layer_input[0]
    width = inputs.shape[1] // NX
    pieces = [
        lax.dynamic_slice_in_dim(inputs, lax.rem(x + s, NX) * width, width, axis=1)
        for s in range(NX)
    ]
    pieces = [a if s == 0 else lax.ppermute(a, "x", ring(NX, s)) for s, a in enumerate(pieces)]
    half = NX // 2
    mine = (jnp.stack(pieces[:half]), jnp.stack(pieces[half:]))
    before, after = (
        tuple(lax.ppermute(a, "y", ring(NY, shift)) for a in mine) for shift in (1, -1)
    )

    outgoing = packed(queries[0], output_grads[0], keys[0], values[0])
    rows = lax.all_to_all(outgoing, "z", split_axis=0, concat_axis=0, tiled=True)
    seg_rows = segment_ids[0].reshape(BLOCKS, BLOCK)
    seg_cols = jnp.broadcast_to(seg_rows[:, :, None], (BLOCKS, BLOCK, BLOCK))
    rows, mine, before, after, seg_cols = lax.optimization_barrier(
        (rows, mine, before, after, seg_cols)
    )
    other = swap_cores(rows[..., 4 * HEAD :])
    far = (
        lax.ppermute(before[0], "y", ring(NY, 1)),
        lax.ppermute(after[1], "y", ring(NY, -1)),
    )
    keep, across, *ship, give, own, away = attention_grads(
        block_links[0], place, rows, other, seg_cols, seg_rows
    )
    inputs = mine + before + after + far
    keep, across, ship, give, own, away, inputs = lax.optimization_barrier(
        (keep, across, ship, give, own, away, inputs)
    )

    away, given = lax.optimization_barrier((swap_cores(away), swap_cores(give)))
    pair = (own + away).astype(bf16)
    pair = lax.all_to_all(pair, "z", split_axis=0, concat_axis=0, tiled=True)
    across, ship, given, pair = lax.optimization_barrier((across, ship, given, pair))
    key_grads, value_grads, chunks = pair_grads(pair)

    grads = lax.all_to_all(chunks, ("x", "y"), split_axis=0, concat_axis=0, tiled=True)
    direct = []
    for k in range(SIDE):
        hops = [((i, 0), ((i + k + 1) % NZ, 0)) for i in range(NZ)]
        hops += [((i, 1), ((i - k - 1) % NZ, 1)) for i in range(NZ)]
        hops = [tuple(a * NC + b for a, b in hop) for hop in hops]
        direct.append(lax.ppermute(jnp.stack([ship[k], given[k]]), ("z", "c"), hops))
    across = lax.ppermute(across, "z", ring(NZ, NZ // 2))
    grads, direct, across = lax.optimization_barrier((grads, direct, across))
    part = weight_grads_part(place, grads, inputs)

    swapped = swap_cores(jnp.stack([a[1] for a in direct]))
    query_grads = joined(place, keep, across, direct, swapped)
    part = part.reshape(NY * NZ * NC, -1, 2 * HEAD)
    part = lax.all_to_all(part, ("y", "z", "c"), split_axis=0, concat_axis=0, tiled=True)
    key_weight_grads, value_weight_grads = weight_sums(part)
    return (
        query_grads[None],
        key_grads[None],
        value_grads[None],
        key_weight_grads,
        value_weight_grads,
    )


def solution(mesh):
    chips = Mesh(mesh.devices.reshape(NX, NY, NZ, NC), ("x", "y", "z", "c"))
    dp, seq = ("x", "y"), ("z", "c")
    by_position = P(dp, seq, None)
    return jax.shard_map(
        local,
        mesh=chips,
        in_specs=(by_position,) * 5 + (P(dp, None, None), P(dp, None)),
        out_specs=(by_position,) * 3 + (P(dp + seq, None),) * 2,
        check_vma=False,
    )
```

```python
import math

import jax
import jax.numpy as jnp
from jax import lax
from jax.experimental import pallas as pl
from jax.experimental.pallas import tpu as pltpu
from jax.sharding import Mesh, PartitionSpec as P

NX, NY, NZ, NC = 4, 4, 8, 2
HEAD = 128
BLOCK = 128
BLOCKS = NZ * NC
LINKS = 8
KV_HEADS = 4
SIDE = NZ // 2 - 1
MIB = 1 << 20
SCALE = 1.0 / math.sqrt(HEAD)
LOG2E = math.log2(math.e)
MASKED = -1e30


def placed(arrays, space):
    return tuple(pltpu.with_memory_space_constraint(a, space) for a in arrays)


def dot(a, b):
    return lax.dot_general(
        a, b, (((1,), (0,)), ((), ())), preferred_element_type=jnp.float32
    )


def dot_nt(a, b):
    return lax.dot_general(
        a, b, (((1,), (1,)), ((), ())), preferred_element_type=jnp.float32
    )


def attention_kernel(
    links_ref, place_ref, rows_ref, other_ref, seg_cols_ref, seg_rows_ref, *refs
):
    (keep_ref, across_ref, *ship_refs, give_ref), refs = refs[: SIDE + 3], refs[SIDE + 3 :]
    own_ref, away_ref, pair_ref, keys_t_ref, total_ref, dq_ref, *refs = refs
    even, odd = refs[:4], refs[4:8]
    score_ref, prob_ref, wide_ref, flat_ref, sems = refs[8:]
    z, core = place_ref[1], place_ref[2]

    def at(block):
        return pl.ds(pl.multiple_of(block * BLOCK, BLOCK), BLOCK)

    def load_pairs(i, carry):
        for block, pair in ((2 * i + core, rows_ref[i, :, 4 * HEAD:]), (2 * i + 1 - core, other_ref[i])):
            pair_ref[at(block), :] = pair
            keys_t_ref[:, at(block)] = pair[:, :HEAD].T
        return carry

    lax.fori_loop(0, NZ, load_pairs, 0)
    total_ref[...] = jnp.zeros_like(total_ref)

    def stacked(i, first):
        rows = rows_ref[i]
        return jnp.concatenate(
            [rows[:, first * HEAD : (first + 1) * HEAD], rows[:, (first + 1) * HEAD : (first + 2) * HEAD]],
            axis=0,
        )

    def softmax_part(i, key_blocks, pairs, score_ref, prob_ref, attention, score_grads):
        queries, grads = stacked(i, 0), stacked(i, 2)
        seg = seg_rows_ref[pl.ds(2 * i + core, 1), :]
        count = len(key_blocks)
        top = None
        for t, j in enumerate(key_blocks):
            here = pl.ds(t * BLOCK, BLOCK)
            allowed = seg_cols_ref[j] == seg
            s = dot_nt(pairs[here, :HEAD], queries) * (SCALE * LOG2E)
            s = jnp.where(jnp.concatenate([allowed, allowed], axis=1), s, MASKED)
            score_ref[here, :] = s
            part = jnp.max(s.reshape(BLOCK // 8, 8, -1), axis=0)
            top = part if top is None else jnp.maximum(top, part)
        top = jnp.max(top, axis=0, keepdims=True)
        norm = None
        for t in range(count):
            here = pl.ds(t * BLOCK, BLOCK)
            e = jnp.exp2(score_ref[here, :] - top)
            score_ref[here, :] = e
            part = jnp.sum(e.reshape(BLOCK // 8, 8, -1), axis=0)
            norm = part if norm is None else norm + part
            yield
        inverse = 1.0 / jnp.sum(norm, axis=0, keepdims=True)
        delta = None
        for t in range(count):
            here = pl.ds(t * BLOCK, BLOCK)
            a = (score_ref[here, :] * inverse).astype(jnp.bfloat16)
            attention[here, :] = a
            g = dot_nt(pairs[here, HEAD:], grads)
            prob_ref[here, :] = g
            part = jnp.sum((a.astype(jnp.float32) * g).reshape(BLOCK // 8, 8, -1), axis=0)
            delta = part if delta is None else delta + part
        delta = jnp.sum(delta, axis=0, keepdims=True)
        for t in range(count):
            here = pl.ds(t * BLOCK, BLOCK)
            ds = (score_ref[here, :] * inverse) * (prob_ref[here, :] - delta)
            score_grads[here, :] = ds.astype(jnp.bfloat16)
            yield

    def product_part(i, key_blocks, keys_t, attention, score_grads):
        queries, grads = stacked(i, 0), stacked(i, 2)
        count = len(key_blocks)
        step = 4
        dq = (dot(keys_t[...], score_grads[...]) * SCALE).astype(jnp.bfloat16).T
        slot = lax.rem(i - z + NZ, NZ)
        dq_ref[slot, :, :HEAD] = dq[:BLOCK]
        dq_ref[slot, :, HEAD:] = dq[BLOCK:]
        yield
        for held, other, columns in (
            (attention, grads, slice(HEAD, 2 * HEAD)), (score_grads, queries, slice(0, HEAD))
        ):
            for t in range(0, count, step):
                part = dot(held[pl.ds(t * BLOCK, step * BLOCK), :], other)
                for u in range(step):
                    total_ref[at(key_blocks[t + u]), columns] += part[u * BLOCK : (u + 1) * BLOCK]
                yield

    def run(*parts):
        parts = list(parts)
        while parts:
            for part in list(parts):
                if next(part, parts) is parts:
                    parts.remove(part)

    def linked(i):
        return [links_ref[2 * i + core, t] for t in range(LINKS)]

    def first_part(i, held):
        key_blocks, (near, near_t, attention, score_grads) = linked(i), held
        for t, j in enumerate(key_blocks):
            here = pl.ds(t * BLOCK, BLOCK)
            near[here, :] = pair_ref[at(j), :]
            near_t[:, here] = keys_t_ref[:, at(j)]
        return softmax_part(i, key_blocks, near, score_ref, prob_ref, attention, score_grads)

    def second_part(i, held):
        return product_part(i, linked(i), *held[1:])

    @pl.when(core == 0)
    def _():
        key_blocks = list(range(BLOCKS))
        attention, score_grads = flat_ref.at[0], flat_ref.at[1]
        run(softmax_part(0, key_blocks, pair_ref, wide_ref.at[0], wide_ref.at[1], attention, score_grads))
        run(first_part(1, odd), product_part(0, key_blocks, keys_t_ref, attention, score_grads))

    @pl.when(core == 1)
    def _():
        run(first_part(0, even))
        run(first_part(1, odd), second_part(0, even))

    def two(h, carry):
        run(first_part(2 * h, even), second_part(2 * h - 1, odd))
        run(first_part(2 * h + 1, odd), second_part(2 * h, even))
        return carry

    lax.fori_loop(1, NZ // 2, two, 0)
    run(second_part(NZ - 1, odd))

    moves = [(0, keep_ref), (NZ // 2, across_ref)]
    for k, ref in enumerate(ship_refs):
        up, down = k + 1, NZ - 1 - k
        moves.append((up + core * (down - up), ref))
        moves.append((down + core * (up - down), give_ref.at[k]))
    copies = [
        pltpu.make_async_copy(dq_ref.at[slot], ref, sems.at[n])
        for n, (slot, ref) in enumerate(moves)
    ]
    for copy in copies:
        copy.start()

    def store(i, carry):
        for ref, block in ((own_ref, 2 * i + core), (away_ref, 2 * i + 1 - core)):
            ref[i, :, :HEAD] = total_ref[at(block), :HEAD] * SCALE
            ref[i, :, HEAD:] = total_ref[at(block), HEAD:]
        return carry

    lax.fori_loop(0, NZ, store, 0)
    for copy in copies:
        copy.wait()


def attention_grads(links, place, rows, other, seg_cols, seg_rows):
    vmem = pl.BlockSpec(memory_space=pltpu.VMEM)
    smem = pl.BlockSpec(memory_space=pltpu.SMEM)
    return pl.pallas_call(
        attention_kernel,
        out_shape=(pltpu.HBM((BLOCK, 2 * HEAD), jnp.bfloat16),) * (SIDE + 2)
        + (pltpu.HBM((SIDE, BLOCK, 2 * HEAD), jnp.bfloat16),)
        + (
            jax.ShapeDtypeStruct((NZ, BLOCK, 2 * HEAD), jnp.float32),
            jax.ShapeDtypeStruct((NZ, BLOCK, 2 * HEAD), jnp.float32),
        ),
        in_specs=[smem, smem, vmem, vmem, vmem, vmem],
        out_specs=(pl.BlockSpec(memory_space=pltpu.HBM),) * (SIDE + 3) + (vmem, vmem),
        scratch_shapes=[
            pltpu.VMEM((BLOCKS * BLOCK, 2 * HEAD), jnp.bfloat16),
            pltpu.VMEM((HEAD, BLOCKS * BLOCK), jnp.bfloat16),
            pltpu.VMEM((BLOCKS * BLOCK, 2 * HEAD), jnp.float32),
            pltpu.VMEM((NZ, BLOCK, 2 * HEAD), jnp.bfloat16),
        ]
        + [
            pltpu.VMEM((LINKS * BLOCK, 2 * HEAD), jnp.bfloat16),
            pltpu.VMEM((HEAD, LINKS * BLOCK), jnp.bfloat16),
            pltpu.VMEM((LINKS * BLOCK, 2 * HEAD), jnp.bfloat16),
            pltpu.VMEM((LINKS * BLOCK, 2 * HEAD), jnp.bfloat16),
        ]
        * 2
        + [
            pltpu.VMEM((LINKS * BLOCK, 2 * HEAD), jnp.float32),
            pltpu.VMEM((LINKS * BLOCK, 2 * HEAD), jnp.float32),
            pltpu.VMEM((2, BLOCKS * BLOCK, 2 * HEAD), jnp.float32),
            pltpu.VMEM((2, BLOCKS * BLOCK, 2 * HEAD), jnp.bfloat16),
            pltpu.SemaphoreType.DMA((NZ,)),
        ],
        compiler_params=pltpu.CompilerParams(vmem_limit_bytes=32 * MIB),
        cost_estimate=pl.CostEstimate(
            flops=1_000, bytes_accessed=1_000, transcendentals=0
        ),
    )(links, place, rows, other, seg_cols, seg_rows)


PARTS = tuple((shift, first) for shift in (0, -1, 1, 2) for first in (0, NX // 2))


def weight_kernel(place_ref, grads_ref, *refs):
    count = len(PARTS)
    out_ref, held_ref, sems = refs[2 * count :]
    copies = []
    for p in range(count):
        for side in range(NC):
            target = held_ref.at[p, :, pl.ds(side * BLOCK, BLOCK), :]
            copies.append(pltpu.make_async_copy(refs[side * count + p], target, sems.at[p, side]))
    for copy in copies:
        copy.start()
    x, y, core = place_ref[0], place_ref[3], place_ref[2]
    total = None
    for p, (shift, first) in enumerate(PARTS):
        copies[2 * p].wait()
        copies[2 * p + 1].wait()
        for s in range(NX // 2):
            source = (lax.rem(x - first - s + NX, NX) * NY + lax.rem(y + shift + NY, NY)) * NC
            grads = jnp.concatenate([grads_ref[source + core], grads_ref[source + 1 - core]], axis=1)
            part = dot(grads, held_ref[p, s])
            total = part if total is None else total + part
    out_ref[...] = total.T.astype(jnp.bfloat16)


def weight_grads_part(place, grads, own, other):
    half, rows, width = own[0].shape
    vmem = pl.BlockSpec(memory_space=pltpu.VMEM)
    return pl.pallas_call(
        weight_kernel,
        out_shape=jax.ShapeDtypeStruct((width, HEAD), jnp.bfloat16),
        in_specs=[pl.BlockSpec(memory_space=pltpu.SMEM), vmem]
        + [pl.BlockSpec(memory_space=pltpu.HBM)] * (2 * len(PARTS)),
        out_specs=vmem,
        scratch_shapes=[
            pltpu.VMEM((len(PARTS), half, NC * rows, width), jnp.bfloat16),
            pltpu.SemaphoreType.DMA((len(PARTS), NC)),
        ],
        compiler_params=pltpu.CompilerParams(vmem_limit_bytes=24 * MIB),
        cost_estimate=pl.CostEstimate(
            flops=1_100_000_000, bytes_accessed=9 * MIB, transcendentals=0
        ),
    )(place, grads, *placed(own, pltpu.HBM), *placed(other, pltpu.HBM))


def pack_kernel(queries_ref, grads_ref, keys_ref, values_ref, out_ref, sem):
    copies = []
    for i in range(NZ):
        heads = pl.ds(2 * HEAD * i, 2 * HEAD)
        shared = pl.ds(HEAD * (i * KV_HEADS // NZ), HEAD)
        for ref, source, first, size in (
            (queries_ref, heads, 0, 2), (grads_ref, heads, 2, 2), (keys_ref, shared, 4, 1), (values_ref, shared, 5, 1)
        ):
            target = out_ref.at[i, :, pl.ds(first * HEAD, size * HEAD)]
            copies.append(pltpu.make_async_copy(ref.at[:, source], target, sem.at[len(copies)]))
    for copy in copies:
        copy.start()
    for copy in copies:
        copy.wait()


def packed(queries, grads, keys, values):
    return pl.pallas_call(
        pack_kernel,
        out_shape=jax.ShapeDtypeStruct((NZ, BLOCK, 6 * HEAD), jnp.bfloat16),
        in_specs=[pl.BlockSpec(memory_space=pltpu.HBM)] * 4,
        out_specs=pl.BlockSpec(memory_space=pltpu.VMEM),
        scratch_shapes=[pltpu.SemaphoreType.DMA((4 * NZ,))],
        compiler_params=pltpu.CompilerParams(vmem_limit_bytes=16 * MIB),
        cost_estimate=pl.CostEstimate(flops=0, bytes_accessed=3 * MIB, transcendentals=0),
    )(*placed((queries, grads, keys, values), pltpu.HBM))


def pair_kernel(partials_ref, keys_ref, values_ref, chunks_ref):
    for g in range(KV_HEADS):
        pair = partials_ref[2 * g].astype(jnp.float32) + partials_ref[2 * g + 1].astype(jnp.float32)
        pair = pair.astype(jnp.bfloat16)
        for kind, ref in enumerate((keys_ref, values_ref)):
            part = pair[:, kind * HEAD : (kind + 1) * HEAD]
            ref[:, g * HEAD : (g + 1) * HEAD] = part
            part = part.T
            for x in range(NX):
                chunks_ref[(x * NY + g) * NC + kind] = part


def pair_grads(partials):
    vmem = pl.BlockSpec(memory_space=pltpu.VMEM)
    out = jax.ShapeDtypeStruct((BLOCK, KV_HEADS * HEAD), jnp.bfloat16)
    return pl.pallas_call(
        pair_kernel,
        out_shape=(out, out, jax.ShapeDtypeStruct((NX * NY * NC, HEAD, BLOCK), jnp.bfloat16)),
        in_specs=[vmem],
        out_specs=(vmem, vmem, vmem),
        compiler_params=pltpu.CompilerParams(vmem_limit_bytes=16 * MIB),
        cost_estimate=pl.CostEstimate(flops=0, bytes_accessed=2 * MIB, transcendentals=0),
    )(partials)


def join_kernel(place_ref, keep_ref, across_ref, *refs):
    direct_refs, swapped_ref, out_ref = refs[:SIDE], refs[SIDE], refs[SIDE + 1]
    z, side = place_ref[1], 1 - 2 * place_ref[2]

    def put(source, value):
        column = lax.rem(source + NZ, NZ) * (2 * HEAD)
        out_ref[:, pl.ds(pl.multiple_of(column, 2 * HEAD), 2 * HEAD)] = value

    put(z, keep_ref[...])
    put(z + NZ // 2, across_ref[...])
    for k in range(SIDE):
        put(z - side * (k + 1), direct_refs[k][0])
        put(z + side * (k + 1), swapped_ref[k])


def joined(place, keep, across, direct, swapped):
    vmem = pl.BlockSpec(memory_space=pltpu.VMEM)
    return pl.pallas_call(
        join_kernel,
        out_shape=jax.ShapeDtypeStruct((BLOCK, NZ * 2 * HEAD), jnp.bfloat16),
        in_specs=[pl.BlockSpec(memory_space=pltpu.SMEM)] + [vmem] * (SIDE + 3),
        out_specs=vmem,
        compiler_params=pltpu.CompilerParams(vmem_limit_bytes=16 * MIB),
        cost_estimate=pl.CostEstimate(flops=0, bytes_accessed=MIB, transcendentals=0),
    )(place, keep, across, *direct, swapped)


def ring(size, shift):
    return [(i, (i + shift) % size) for i in range(size)]


def swap_cores(a):
    return lax.ppermute(a, "c", [(0, 1), (1, 0)])


def local(layer_input, queries, keys, values, output_grads, block_links, segment_ids):
    x, y, z, core = (lax.axis_index(axis) for axis in ("x", "y", "z", "c"))
    place = jnp.stack([x, z, core, y]).astype(jnp.int32)
    bf16 = jnp.bfloat16

    inputs = layer_input[0]
    width = inputs.shape[1] // NX
    pieces = [
        lax.dynamic_slice_in_dim(inputs, lax.rem(x + s, NX) * width, width, axis=1)
        for s in range(NX)
    ]
    pieces = [a if s == 0 else lax.ppermute(a, "x", ring(NX, s)) for s, a in enumerate(pieces)]
    half = NX // 2
    mine = (jnp.stack(pieces[:half]), jnp.stack(pieces[half:]))
    before, after = (
        tuple(lax.ppermute(a, "y", ring(NY, shift)) for a in mine) for shift in (1, -1)
    )

    far = (
        lax.ppermute(before[0], "y", ring(NY, 1)),
        lax.ppermute(after[1], "y", ring(NY, -1)),
    )

    outgoing = packed(queries[0], output_grads[0], keys[0], values[0])
    rows = lax.all_to_all(outgoing, "z", split_axis=0, concat_axis=0, tiled=True)
    seg_rows = segment_ids[0].reshape(BLOCKS, BLOCK)
    seg_cols = jnp.broadcast_to(seg_rows[:, :, None], (BLOCKS, BLOCK, BLOCK))
    rows, mine, before, after, seg_cols = lax.optimization_barrier(
        (rows, mine, before, after, seg_cols)
    )
    other = swap_cores(rows[..., 4 * HEAD :])
    keep, across, *ship, give, own, away = attention_grads(
        block_links[0], place, rows, other, seg_cols, seg_rows
    )
    inputs_own = mine + before + after + far
    keep, across, ship, give, own, away, inputs_own = lax.optimization_barrier(
        (keep, across, ship, give, own, away, inputs_own)
    )
    inputs_other = tuple(swap_cores(a) for a in inputs_own)

    pair = (own + swap_cores(away)).astype(bf16)
    pair = lax.all_to_all(pair, "z", split_axis=0, concat_axis=0, tiled=True)
    given = swap_cores(give)
    across, ship, given, pair, inputs_other = lax.optimization_barrier(
        (across, ship, given, pair, inputs_other)
    )
    key_grads, value_grads, chunks = pair_grads(pair)

    grads = lax.all_to_all(chunks, ("x", "y", "c"), split_axis=0, concat_axis=0, tiled=True)
    direct = []
    for k in range(SIDE):
        hops = [((i, 0), ((i + k + 1) % NZ, 0)) for i in range(NZ)]
        hops += [((i, 1), ((i - k - 1) % NZ, 1)) for i in range(NZ)]
        hops = [tuple(a * NC + b for a, b in hop) for hop in hops]
        direct.append(lax.ppermute(jnp.stack([ship[k], given[k]]), ("z", "c"), hops))
    across = lax.ppermute(across, "z", ring(NZ, NZ // 2))
    grads, direct, across = lax.optimization_barrier((grads, direct, across))
    part = weight_grads_part(place, grads, inputs_own, inputs_other)

    swapped = swap_cores(jnp.stack([a[1] for a in direct]))
    query_grads = joined(place, keep, across, direct, swapped)
    part = part.reshape(NY * NZ * NC, -1, HEAD)
    part = lax.all_to_all(part, ("y", "z", "c"), split_axis=0, concat_axis=0, tiled=True)
    part = part.reshape(NY, NZ, NC, -1, HEAD).astype(jnp.float32)
    part = jnp.transpose(jnp.sum(part, axis=1), (1, 2, 0, 3))
    part = part.reshape(NC, -1, NY * HEAD)
    return query_grads[None], key_grads[None], value_grads[None], part[0], part[1]


def solution(mesh):
    chips = Mesh(mesh.devices.reshape(NX, NY, NZ, NC), ("x", "y", "z", "c"))
    dp, seq = ("x", "y"), ("z", "c")
    by_position = P(dp, seq, None)
    return jax.shard_map(
        local,
        mesh=chips,
        in_specs=(by_position,) * 5 + (P(dp, None, None), P(dp, None)),
        out_specs=(by_position,) * 3 + (P(dp + seq, None),) * 2,
        check_vma=False,
    )
```

```python
import math

import jax
import jax.numpy as jnp
from jax import lax
from jax.experimental import pallas as pl
from jax.experimental.pallas import tpu as pltpu
from jax.sharding import Mesh, PartitionSpec as P

NX, NY, NZ, NC = 4, 4, 8, 2
HEAD = 128
BLOCK = 128
BLOCKS = NZ * NC
LINKS = 8
KV_HEADS = 4
SIDE = NZ // 2 - 1
MIB = 1 << 20
SCALE = 1.0 / math.sqrt(HEAD)
LOG2E = math.log2(math.e)
MASKED = -1e30


def placed(arrays, space):
    return tuple(pltpu.with_memory_space_constraint(a, space) for a in arrays)


def dot(a, b):
    return lax.dot_general(
        a, b, (((1,), (0,)), ((), ())), preferred_element_type=jnp.float32
    )


def dot_nt(a, b):
    return lax.dot_general(
        a, b, (((1,), (1,)), ((), ())), preferred_element_type=jnp.float32
    )


def attention_kernel(
    links_ref, place_ref, rows_ref, other_ref, seg_cols_ref, seg_rows_ref, *refs
):
    (keep_ref, across_ref, *ship_refs, give_ref), refs = refs[: SIDE + 3], refs[SIDE + 3 :]
    own_ref, away_ref, pair_ref, keys_t_ref, total_ref, dq_ref, *refs = refs
    even, odd = refs[:4], refs[4:8]
    score_ref, prob_ref, wide_ref, flat_ref, sems = refs[8:]
    z, core = place_ref[1], place_ref[2]

    def at(block):
        return pl.ds(pl.multiple_of(block * BLOCK, BLOCK), BLOCK)

    def load_pairs(i, carry):
        for block, pair in ((2 * i + core, rows_ref[i, :, 4 * HEAD:]), (2 * i + 1 - core, other_ref[i])):
            pair_ref[at(block), :] = pair
            keys_t_ref[:, at(block)] = pair[:, :HEAD].T
        return carry

    lax.fori_loop(0, NZ, load_pairs, 0)
    total_ref[...] = jnp.zeros_like(total_ref)

    def stacked(i, first):
        rows = rows_ref[i]
        return jnp.concatenate(
            [rows[:, first * HEAD : (first + 1) * HEAD], rows[:, (first + 1) * HEAD : (first + 2) * HEAD]],
            axis=0,
        )

    def softmax_part(i, key_blocks, pairs, score_ref, prob_ref, attention, score_grads):
        queries, grads = stacked(i, 0), stacked(i, 2)
        seg = seg_rows_ref[pl.ds(2 * i + core, 1), :]
        count = len(key_blocks)
        top = None
        for t, j in enumerate(key_blocks):
            here = pl.ds(t * BLOCK, BLOCK)
            allowed = seg_cols_ref[j] == seg
            s = dot_nt(pairs[here, :HEAD], queries) * (SCALE * LOG2E)
            s = jnp.where(jnp.concatenate([allowed, allowed], axis=1), s, MASKED)
            score_ref[here, :] = s
            part = jnp.max(s.reshape(BLOCK // 8, 8, -1), axis=0)
            top = part if top is None else jnp.maximum(top, part)
        top = jnp.max(top, axis=0, keepdims=True)
        norm = None
        for t in range(count):
            here = pl.ds(t * BLOCK, BLOCK)
            e = jnp.exp2(score_ref[here, :] - top)
            score_ref[here, :] = e
            part = jnp.sum(e.reshape(BLOCK // 8, 8, -1), axis=0)
            norm = part if norm is None else norm + part
            yield
        inverse = 1.0 / jnp.sum(norm, axis=0, keepdims=True)
        delta = None
        for t in range(count):
            here = pl.ds(t * BLOCK, BLOCK)
            a = (score_ref[here, :] * inverse).astype(jnp.bfloat16)
            attention[here, :] = a
            g = dot_nt(pairs[here, HEAD:], grads)
            prob_ref[here, :] = g
            part = jnp.sum((a.astype(jnp.float32) * g).reshape(BLOCK // 8, 8, -1), axis=0)
            delta = part if delta is None else delta + part
        delta = jnp.sum(delta, axis=0, keepdims=True)
        for t in range(count):
            here = pl.ds(t * BLOCK, BLOCK)
            ds = (score_ref[here, :] * inverse) * (prob_ref[here, :] - delta)
            score_grads[here, :] = ds.astype(jnp.bfloat16)
            yield

    def product_part(i, key_blocks, keys_t, attention, score_grads):
        queries, grads = stacked(i, 0), stacked(i, 2)
        count = len(key_blocks)
        step = 4
        dq = (dot(keys_t[...], score_grads[...]) * SCALE).astype(jnp.bfloat16).T
        slot = lax.rem(i - z + NZ, NZ)
        dq_ref[slot, :, :HEAD] = dq[:BLOCK]
        dq_ref[slot, :, HEAD:] = dq[BLOCK:]
        yield
        for held, other, columns in (
            (attention, grads, slice(HEAD, 2 * HEAD)), (score_grads, queries, slice(0, HEAD))
        ):
            for t in range(0, count, step):
                part = dot(held[pl.ds(t * BLOCK, step * BLOCK), :], other)
                for u in range(step):
                    total_ref[at(key_blocks[t + u]), columns] += part[u * BLOCK : (u + 1) * BLOCK]
                yield

    def run(*parts):
        parts = list(parts)
        while parts:
            for part in list(parts):
                if next(part, parts) is parts:
                    parts.remove(part)

    def linked(i):
        return [links_ref[2 * i + core, t] for t in range(LINKS)]

    def first_part(i, held):
        key_blocks, (near, near_t, attention, score_grads) = linked(i), held
        for t, j in enumerate(key_blocks):
            here = pl.ds(t * BLOCK, BLOCK)
            near[here, :] = pair_ref[at(j), :]
            near_t[:, here] = keys_t_ref[:, at(j)]
        return softmax_part(i, key_blocks, near, score_ref, prob_ref, attention, score_grads)

    def second_part(i, held):
        return product_part(i, linked(i), *held[1:])

    @pl.when(core == 0)
    def _():
        key_blocks = list(range(BLOCKS))
        attention, score_grads = flat_ref.at[0], flat_ref.at[1]
        run(softmax_part(0, key_blocks, pair_ref, wide_ref.at[0], wide_ref.at[1], attention, score_grads))
        run(first_part(1, odd), product_part(0, key_blocks, keys_t_ref, attention, score_grads))

    @pl.when(core == 1)
    def _():
        run(first_part(0, even))
        run(first_part(1, odd), second_part(0, even))

    def two(h, carry):
        run(first_part(2 * h, even), second_part(2 * h - 1, odd))
        run(first_part(2 * h + 1, odd), second_part(2 * h, even))
        return carry

    lax.fori_loop(1, NZ // 2, two, 0)
    run(second_part(NZ - 1, odd))

    moves = [(0, keep_ref), (NZ // 2, across_ref)]
    for k, ref in enumerate(ship_refs):
        up, down = k + 1, NZ - 1 - k
        moves.append((up + core * (down - up), ref))
        moves.append((down + core * (up - down), give_ref.at[k]))
    copies = [
        pltpu.make_async_copy(dq_ref.at[slot], ref, sems.at[n])
        for n, (slot, ref) in enumerate(moves)
    ]
    for copy in copies:
        copy.start()

    def store(i, carry):
        for ref, block in ((own_ref, 2 * i + core), (away_ref, 2 * i + 1 - core)):
            ref[i, :, :HEAD] = (total_ref[at(block), :HEAD] * SCALE).astype(ref.dtype)
            ref[i, :, HEAD:] = total_ref[at(block), HEAD:].astype(ref.dtype)
        return carry

    lax.fori_loop(0, NZ, store, 0)
    for copy in copies:
        copy.wait()


def attention_grads(links, place, rows, other, seg_cols, seg_rows):
    vmem = pl.BlockSpec(memory_space=pltpu.VMEM)
    smem = pl.BlockSpec(memory_space=pltpu.SMEM)
    return pl.pallas_call(
        attention_kernel,
        out_shape=(pltpu.HBM((BLOCK, 2 * HEAD), jnp.bfloat16),) * (SIDE + 2)
        + (pltpu.HBM((SIDE, BLOCK, 2 * HEAD), jnp.bfloat16),)
        + (
            jax.ShapeDtypeStruct((NZ, BLOCK, 2 * HEAD), jnp.float32),
            jax.ShapeDtypeStruct((NZ, BLOCK, 2 * HEAD), jnp.bfloat16),
        ),
        in_specs=[smem, smem, vmem, vmem, vmem, vmem],
        out_specs=(pl.BlockSpec(memory_space=pltpu.HBM),) * (SIDE + 3) + (vmem, vmem),
        scratch_shapes=[
            pltpu.VMEM((BLOCKS * BLOCK, 2 * HEAD), jnp.bfloat16),
            pltpu.VMEM((HEAD, BLOCKS * BLOCK), jnp.bfloat16),
            pltpu.VMEM((BLOCKS * BLOCK, 2 * HEAD), jnp.float32),
            pltpu.VMEM((NZ, BLOCK, 2 * HEAD), jnp.bfloat16),
        ]
        + [
            pltpu.VMEM((LINKS * BLOCK, 2 * HEAD), jnp.bfloat16),
            pltpu.VMEM((HEAD, LINKS * BLOCK), jnp.bfloat16),
            pltpu.VMEM((LINKS * BLOCK, 2 * HEAD), jnp.bfloat16),
            pltpu.VMEM((LINKS * BLOCK, 2 * HEAD), jnp.bfloat16),
        ]
        * 2
        + [
            pltpu.VMEM((LINKS * BLOCK, 2 * HEAD), jnp.float32),
            pltpu.VMEM((LINKS * BLOCK, 2 * HEAD), jnp.float32),
            pltpu.VMEM((2, BLOCKS * BLOCK, 2 * HEAD), jnp.float32),
            pltpu.VMEM((2, BLOCKS * BLOCK, 2 * HEAD), jnp.bfloat16),
            pltpu.SemaphoreType.DMA((NZ,)),
        ],
        compiler_params=pltpu.CompilerParams(vmem_limit_bytes=32 * MIB),
        cost_estimate=pl.CostEstimate(
            flops=1_000, bytes_accessed=1_000, transcendentals=0
        ),
    )(links, place, rows, other, seg_cols, seg_rows)


PARTS = tuple((shift, first) for shift in (0, -1, 1, 2) for first in (0, NX // 2))


def weight_kernel(place_ref, grads_ref, *refs):
    count = len(PARTS)
    out_ref, held_ref, sems = refs[2 * count :]
    copies = []
    for p in range(count):
        for side in range(NC):
            target = held_ref.at[p, :, pl.ds(side * BLOCK, BLOCK), :]
            copies.append(pltpu.make_async_copy(refs[side * count + p], target, sems.at[p, side]))
    for copy in copies:
        copy.start()
    x, y, core = place_ref[0], place_ref[3], place_ref[2]
    total = None
    for p, (shift, first) in enumerate(PARTS):
        copies[2 * p].wait()
        copies[2 * p + 1].wait()
        for s in range(NX // 2):
            source = (lax.rem(x - first - s + NX, NX) * NY + lax.rem(y + shift + NY, NY)) * NC
            grads = jnp.concatenate([grads_ref[source + core], grads_ref[source + 1 - core]], axis=1)
            part = dot(grads, held_ref[p, s])
            total = part if total is None else total + part
    out_ref[...] = total.T.astype(jnp.bfloat16)


def weight_grads_part(place, grads, own, other):
    half, rows, width = own[0].shape
    vmem = pl.BlockSpec(memory_space=pltpu.VMEM)
    return pl.pallas_call(
        weight_kernel,
        out_shape=jax.ShapeDtypeStruct((width, HEAD), jnp.bfloat16),
        in_specs=[pl.BlockSpec(memory_space=pltpu.SMEM), vmem]
        + [pl.BlockSpec(memory_space=pltpu.HBM)] * (2 * len(PARTS)),
        out_specs=vmem,
        scratch_shapes=[
            pltpu.VMEM((len(PARTS), half, NC * rows, width), jnp.bfloat16),
            pltpu.SemaphoreType.DMA((len(PARTS), NC)),
        ],
        compiler_params=pltpu.CompilerParams(vmem_limit_bytes=24 * MIB),
        cost_estimate=pl.CostEstimate(
            flops=1_100_000_000, bytes_accessed=9 * MIB, transcendentals=0
        ),
    )(place, grads, *placed(own, pltpu.HBM), *placed(other, pltpu.HBM))


def pack_kernel(queries_ref, grads_ref, keys_ref, values_ref, out_ref, *refs):
    q_ref, g_ref, k_ref, v_ref, sem, store_sem = refs
    loads = [
        pltpu.make_async_copy(a, b, sem.at[n])
        for n, (a, b) in enumerate(((queries_ref, q_ref), (grads_ref, g_ref), (keys_ref, k_ref), (values_ref, v_ref)))
    ]
    for copy in loads:
        copy.start()
    stores = []
    for load, ref, first, size, shared in (
        (loads[0], q_ref, 0, 2, 1), (loads[1], g_ref, 2, 2, 1), (loads[2], k_ref, 4, 1, 2), (loads[3], v_ref, 5, 1, 2)
    ):
        load.wait()
        for i in range(NZ):
            source = ref.at[:, pl.ds(size * HEAD * (i // shared), size * HEAD)]
            copy = pltpu.make_async_copy(source, out_ref.at[i, :, pl.ds(first * HEAD, size * HEAD)], store_sem.at[len(stores)])
            copy.start()
            stores.append(copy)
    for copy in stores:
        copy.wait()


def packed(queries, grads, keys, values):
    return pl.pallas_call(
        pack_kernel,
        out_shape=pltpu.HBM((NZ, BLOCK, 6 * HEAD), jnp.bfloat16),
        in_specs=[pl.BlockSpec(memory_space=pltpu.HBM)] * 4,
        out_specs=pl.BlockSpec(memory_space=pltpu.HBM),
        scratch_shapes=[pltpu.VMEM(a.shape, a.dtype) for a in (queries, grads, keys, values)]
        + [pltpu.SemaphoreType.DMA((4,)), pltpu.SemaphoreType.DMA((4 * NZ,))],
        compiler_params=pltpu.CompilerParams(vmem_limit_bytes=16 * MIB),
        cost_estimate=pl.CostEstimate(flops=0, bytes_accessed=3 * MIB, transcendentals=0),
    )(*placed((queries, grads, keys, values), pltpu.HBM))


def pair_kernel(partials_ref, keys_ref, values_ref, chunks_ref):
    for g in range(KV_HEADS):
        pair = partials_ref[2 * g].astype(jnp.float32) + partials_ref[2 * g + 1].astype(jnp.float32)
        pair = pair.astype(jnp.bfloat16)
        for kind, ref in enumerate((keys_ref, values_ref)):
            part = pair[:, kind * HEAD : (kind + 1) * HEAD]
            ref[:, g * HEAD : (g + 1) * HEAD] = part
            part = part.T
            for x in range(NX):
                chunks_ref[(x * NY + g) * NC + kind] = part


def pair_grads(partials):
    vmem = pl.BlockSpec(memory_space=pltpu.VMEM)
    out = jax.ShapeDtypeStruct((BLOCK, KV_HEADS * HEAD), jnp.bfloat16)
    return pl.pallas_call(
        pair_kernel,
        out_shape=(out, out, jax.ShapeDtypeStruct((NX * NY * NC, HEAD, BLOCK), jnp.bfloat16)),
        in_specs=[vmem],
        out_specs=(vmem, vmem, vmem),
        compiler_params=pltpu.CompilerParams(vmem_limit_bytes=16 * MIB),
        cost_estimate=pl.CostEstimate(flops=0, bytes_accessed=2 * MIB, transcendentals=0),
    )(partials)


def join_kernel(place_ref, keep_ref, across_ref, *refs):
    direct_refs, swapped_ref, out_ref = refs[:SIDE], refs[SIDE], refs[SIDE + 1]
    z, side = place_ref[1], 1 - 2 * place_ref[2]

    def put(source, value):
        column = lax.rem(source + NZ, NZ) * (2 * HEAD)
        out_ref[:, pl.ds(pl.multiple_of(column, 2 * HEAD), 2 * HEAD)] = value

    put(z, keep_ref[...])
    put(z + NZ // 2, across_ref[...])
    for k in range(SIDE):
        put(z - side * (k + 1), direct_refs[k][0])
        put(z + side * (k + 1), swapped_ref[k])


def joined(place, keep, across, direct, swapped):
    vmem = pl.BlockSpec(memory_space=pltpu.VMEM)
    return pl.pallas_call(
        join_kernel,
        out_shape=jax.ShapeDtypeStruct((BLOCK, NZ * 2 * HEAD), jnp.bfloat16),
        in_specs=[pl.BlockSpec(memory_space=pltpu.SMEM)] + [vmem] * (SIDE + 3),
        out_specs=vmem,
        compiler_params=pltpu.CompilerParams(vmem_limit_bytes=16 * MIB),
        cost_estimate=pl.CostEstimate(flops=0, bytes_accessed=MIB, transcendentals=0),
    )(place, keep, across, *direct, swapped)


def ring(size, shift):
    return [(i, (i + shift) % size) for i in range(size)]


def swap_cores(a):
    return lax.ppermute(a, "c", [(0, 1), (1, 0)])


def local(layer_input, queries, keys, values, output_grads, block_links, segment_ids):
    x, y, z, core = (lax.axis_index(axis) for axis in ("x", "y", "z", "c"))
    place = jnp.stack([x, z, core, y]).astype(jnp.int32)
    bf16 = jnp.bfloat16

    inputs = layer_input[0]
    width = inputs.shape[1] // NX
    pieces = [
        lax.dynamic_slice_in_dim(inputs, lax.rem(x + s, NX) * width, width, axis=1)
        for s in range(NX)
    ]
    pieces = [a if s == 0 else lax.ppermute(a, "x", ring(NX, s)) for s, a in enumerate(pieces)]
    groups = [pieces[0], pieces[1], jnp.stack(pieces[2:])]
    before, after = (
        [lax.ppermute(a, "y", ring(NY, shift)) for a in groups] for shift in (1, -1)
    )
    mine, before, after = (
        (jnp.stack(a[:2]), a[2]) for a in (groups, before, after)
    )
    far = (
        lax.ppermute(after[0], "y", ring(NY, -1)),
        lax.ppermute(before[1], "y", ring(NY, 1)),
    )

    outgoing = packed(queries[0], output_grads[0], keys[0], values[0])
    rows = lax.all_to_all(outgoing, "z", split_axis=0, concat_axis=0, tiled=True)
    seg_rows = segment_ids[0].reshape(BLOCKS, BLOCK)
    seg_cols = jnp.broadcast_to(seg_rows[:, :, None], (BLOCKS, BLOCK, BLOCK))
    rows, mine, before, after, seg_cols = lax.optimization_barrier(
        (rows, mine, before, after, seg_cols)
    )
    other = swap_cores(rows[..., 4 * HEAD :])
    keep, across, *ship, give, own, away = attention_grads(
        block_links[0], place, rows, other, seg_cols, seg_rows
    )
    inputs_own = mine + before + after + far
    keep, across, ship, give, own, away, inputs_own = lax.optimization_barrier(
        (keep, across, ship, give, own, away, inputs_own)
    )
    inputs_other = tuple(swap_cores(a) for a in inputs_own)

    pair = (own + swap_cores(away).astype(jnp.float32)).astype(bf16)
    pair = lax.all_to_all(pair, "z", split_axis=0, concat_axis=0, tiled=True)
    given = swap_cores(give)
    across, ship, given, pair, inputs_other = lax.optimization_barrier(
        (across, ship, given, pair, inputs_other)
    )
    key_grads, value_grads, chunks = pair_grads(pair)

    grads = lax.all_to_all(chunks, ("x", "y", "c"), split_axis=0, concat_axis=0, tiled=True)
    direct = []
    for k in range(SIDE):
        hops = [((i, 0), ((i + k + 1) % NZ, 0)) for i in range(NZ)]
        hops += [((i, 1), ((i - k - 1) % NZ, 1)) for i in range(NZ)]
        hops = [tuple(a * NC + b for a, b in hop) for hop in hops]
        direct.append(lax.ppermute(jnp.stack([ship[k], given[k]]), ("z", "c"), hops))
    across = lax.ppermute(across, "z", ring(NZ, NZ // 2))
    grads, direct, across = lax.optimization_barrier((grads, direct, across))
    part = weight_grads_part(place, grads, inputs_own, inputs_other)

    swapped = swap_cores(jnp.stack([a[1] for a in direct]))
    query_grads = joined(place, keep, across, direct, swapped)
    part = part.reshape(NY * NZ * NC, -1, HEAD)
    part = lax.all_to_all(part, ("y", "z", "c"), split_axis=0, concat_axis=0, tiled=True)
    part = part.reshape(NY, NZ, NC, -1, HEAD).astype(jnp.float32)
    part = jnp.transpose(jnp.sum(part, axis=1), (1, 2, 0, 3))
    part = part.reshape(NC, -1, NY * HEAD)
    return query_grads[None], key_grads[None], value_grads[None], part[0], part[1]


def solution(mesh):
    chips = Mesh(mesh.devices.reshape(NX, NY, NZ, NC), ("x", "y", "z", "c"))
    dp, seq = ("x", "y"), ("z", "c")
    by_position = P(dp, seq, None)
    return jax.shard_map(
        local,
        mesh=chips,
        in_specs=(by_position,) * 5 + (P(dp, None, None), P(dp, None)),
        out_specs=(by_position,) * 3 + (P(dp + seq, None),) * 2,
        check_vma=False,
    )
```

```python
import math

import jax
import jax.numpy as jnp
from jax import lax
from jax.experimental import pallas as pl
from jax.experimental.pallas import tpu as pltpu
from jax.sharding import Mesh, PartitionSpec as P

NX, NY, NZ, NC = 4, 4, 8, 2
HEAD = 128
BLOCK = 128
BLOCKS = NZ * NC
LINKS = 8
KV_HEADS = 4
SIDE = NZ // 2 - 1
MIB = 1 << 20
SCALE = 1.0 / math.sqrt(HEAD)
LOG2E = math.log2(math.e)
MASKED = -1e30


def placed(arrays, space):
    return tuple(pltpu.with_memory_space_constraint(a, space) for a in arrays)


def dot(a, b):
    return lax.dot_general(
        a, b, (((1,), (0,)), ((), ())), preferred_element_type=jnp.float32
    )


def dot_nt(a, b):
    return lax.dot_general(
        a, b, (((1,), (1,)), ((), ())), preferred_element_type=jnp.float32
    )


def attention_kernel(
    links_ref, place_ref, rows_ref, other_ref, seg_cols_ref, seg_rows_ref, *refs
):
    (keep_ref, across_ref, *ship_refs, give_ref), refs = refs[: SIDE + 3], refs[SIDE + 3 :]
    own_ref, away_ref, pair_ref, keys_t_ref, total_ref, dq_ref, *refs = refs
    even, odd = refs[:4], refs[4:8]
    score_ref, prob_ref, wide_ref, flat_ref, sems = refs[8:]
    z, core = place_ref[1], place_ref[2]

    def at(block):
        return pl.ds(pl.multiple_of(block * BLOCK, BLOCK), BLOCK)

    def load_pairs(i, carry):
        for block, pair in ((2 * i + core, rows_ref[i, :, 4 * HEAD:]), (2 * i + 1 - core, other_ref[i])):
            pair_ref[at(block), :] = pair
            keys_t_ref[:, at(block)] = pair[:, :HEAD].T
        return carry

    lax.fori_loop(0, NZ, load_pairs, 0)
    total_ref[...] = jnp.zeros_like(total_ref)

    def stacked(i, first):
        rows = rows_ref[i]
        return jnp.concatenate(
            [rows[:, first * HEAD : (first + 1) * HEAD], rows[:, (first + 1) * HEAD : (first + 2) * HEAD]],
            axis=0,
        )

    def softmax_part(i, key_blocks, pairs, score_ref, prob_ref, attention, score_grads):
        queries, grads = stacked(i, 0), stacked(i, 2)
        seg = seg_rows_ref[pl.ds(2 * i + core, 1), :]
        count = len(key_blocks)
        top = None
        for t, j in enumerate(key_blocks):
            here = pl.ds(t * BLOCK, BLOCK)
            allowed = seg_cols_ref[j] == seg
            s = dot_nt(pairs[here, :HEAD], queries) * (SCALE * LOG2E)
            s = jnp.where(jnp.concatenate([allowed, allowed], axis=1), s, MASKED)
            score_ref[here, :] = s
            part = jnp.max(s.reshape(BLOCK // 8, 8, -1), axis=0)
            top = part if top is None else jnp.maximum(top, part)
        top = jnp.max(top, axis=0, keepdims=True)
        norm = None
        for t in range(count):
            here = pl.ds(t * BLOCK, BLOCK)
            e = jnp.exp2(score_ref[here, :] - top)
            score_ref[here, :] = e
            part = jnp.sum(e.reshape(BLOCK // 8, 8, -1), axis=0)
            norm = part if norm is None else norm + part
            yield
        inverse = 1.0 / jnp.sum(norm, axis=0, keepdims=True)
        delta = None
        for t in range(count):
            here = pl.ds(t * BLOCK, BLOCK)
            a = (score_ref[here, :] * inverse).astype(jnp.bfloat16)
            attention[here, :] = a
            g = dot_nt(pairs[here, HEAD:], grads)
            prob_ref[here, :] = g
            part = jnp.sum((a.astype(jnp.float32) * g).reshape(BLOCK // 8, 8, -1), axis=0)
            delta = part if delta is None else delta + part
        delta = jnp.sum(delta, axis=0, keepdims=True)
        for t in range(count):
            here = pl.ds(t * BLOCK, BLOCK)
            ds = (score_ref[here, :] * inverse) * (prob_ref[here, :] - delta)
            score_grads[here, :] = ds.astype(jnp.bfloat16)
            yield

    def product_part(i, key_blocks, keys_t, attention, score_grads):
        queries, grads = stacked(i, 0), stacked(i, 2)
        count = len(key_blocks)
        step = 4
        dq = (dot(keys_t[...], score_grads[...]) * SCALE).astype(jnp.bfloat16).T
        slot = lax.rem(i - z + NZ, NZ)
        dq_ref[slot, :, :HEAD] = dq[:BLOCK]
        dq_ref[slot, :, HEAD:] = dq[BLOCK:]
        yield
        for held, other, columns in (
            (attention, grads, slice(HEAD, 2 * HEAD)), (score_grads, queries, slice(0, HEAD))
        ):
            for t in range(0, count, step):
                part = dot(held[pl.ds(t * BLOCK, step * BLOCK), :], other)
                for u in range(step):
                    total_ref[at(key_blocks[t + u]), columns] += part[u * BLOCK : (u + 1) * BLOCK]
                yield

    def run(*parts):
        parts = list(parts)
        while parts:
            for part in list(parts):
                if next(part, parts) is parts:
                    parts.remove(part)

    def linked(i):
        return [links_ref[2 * i + core, t] for t in range(LINKS)]

    def first_part(i, held):
        key_blocks, (near, near_t, attention, score_grads) = linked(i), held
        for t, j in enumerate(key_blocks):
            here = pl.ds(t * BLOCK, BLOCK)
            near[here, :] = pair_ref[at(j), :]
            near_t[:, here] = keys_t_ref[:, at(j)]
        return softmax_part(i, key_blocks, near, score_ref, prob_ref, attention, score_grads)

    def second_part(i, held):
        return product_part(i, linked(i), *held[1:])

    @pl.when(core == 0)
    def _():
        key_blocks = list(range(BLOCKS))
        attention, score_grads = flat_ref.at[0], flat_ref.at[1]
        run(softmax_part(0, key_blocks, pair_ref, wide_ref.at[0], wide_ref.at[1], attention, score_grads))
        run(first_part(1, odd), product_part(0, key_blocks, keys_t_ref, attention, score_grads))

    @pl.when(core == 1)
    def _():
        run(first_part(0, even))
        run(first_part(1, odd), second_part(0, even))

    def two(h, carry):
        run(first_part(2 * h, even), second_part(2 * h - 1, odd))
        run(first_part(2 * h + 1, odd), second_part(2 * h, even))
        return carry

    lax.fori_loop(1, NZ // 2, two, 0)
    run(second_part(NZ - 1, odd))

    moves = [(0, keep_ref), (NZ // 2, across_ref)]
    for k, ref in enumerate(ship_refs):
        up, down = k + 1, NZ - 1 - k
        moves.append((up + core * (down - up), ref))
        moves.append((down + core * (up - down), give_ref.at[k]))
    copies = [
        pltpu.make_async_copy(dq_ref.at[slot], ref, sems.at[n])
        for n, (slot, ref) in enumerate(moves)
    ]
    for copy in copies:
        copy.start()

    def store(i, carry):
        for ref, block in ((own_ref, 2 * i + core), (away_ref, 2 * i + 1 - core)):
            ref[i, :, :HEAD] = (total_ref[at(block), :HEAD] * SCALE).astype(ref.dtype)
            ref[i, :, HEAD:] = total_ref[at(block), HEAD:].astype(ref.dtype)
        return carry

    lax.fori_loop(0, NZ, store, 0)
    for copy in copies:
        copy.wait()


def attention_grads(links, place, rows, other, seg_cols, seg_rows):
    vmem = pl.BlockSpec(memory_space=pltpu.VMEM)
    smem = pl.BlockSpec(memory_space=pltpu.SMEM)
    return pl.pallas_call(
        attention_kernel,
        out_shape=(pltpu.HBM((BLOCK, 2 * HEAD), jnp.bfloat16),) * (SIDE + 2)
        + (pltpu.HBM((SIDE, BLOCK, 2 * HEAD), jnp.bfloat16),)
        + (
            jax.ShapeDtypeStruct((NZ, BLOCK, 2 * HEAD), jnp.float32),
            jax.ShapeDtypeStruct((NZ, BLOCK, 2 * HEAD), jnp.bfloat16),
        ),
        in_specs=[smem, smem, vmem, vmem, vmem, vmem],
        out_specs=(pl.BlockSpec(memory_space=pltpu.HBM),) * (SIDE + 3) + (vmem, vmem),
        scratch_shapes=[
            pltpu.VMEM((BLOCKS * BLOCK, 2 * HEAD), jnp.bfloat16),
            pltpu.VMEM((HEAD, BLOCKS * BLOCK), jnp.bfloat16),
            pltpu.VMEM((BLOCKS * BLOCK, 2 * HEAD), jnp.float32),
            pltpu.VMEM((NZ, BLOCK, 2 * HEAD), jnp.bfloat16),
        ]
        + [
            pltpu.VMEM((LINKS * BLOCK, 2 * HEAD), jnp.bfloat16),
            pltpu.VMEM((HEAD, LINKS * BLOCK), jnp.bfloat16),
            pltpu.VMEM((LINKS * BLOCK, 2 * HEAD), jnp.bfloat16),
            pltpu.VMEM((LINKS * BLOCK, 2 * HEAD), jnp.bfloat16),
        ]
        * 2
        + [
            pltpu.VMEM((LINKS * BLOCK, 2 * HEAD), jnp.float32),
            pltpu.VMEM((LINKS * BLOCK, 2 * HEAD), jnp.float32),
            pltpu.VMEM((2, BLOCKS * BLOCK, 2 * HEAD), jnp.float32),
            pltpu.VMEM((2, BLOCKS * BLOCK, 2 * HEAD), jnp.bfloat16),
            pltpu.SemaphoreType.DMA((NZ,)),
        ],
        compiler_params=pltpu.CompilerParams(vmem_limit_bytes=32 * MIB),
        cost_estimate=pl.CostEstimate(
            flops=1_000, bytes_accessed=1_000, transcendentals=0
        ),
    )(links, place, rows, other, seg_cols, seg_rows)


PARTS = tuple((shift, first) for shift in (0, -1, 1, 2) for first in (0, NX // 2))


def weight_kernel(place_ref, grads_ref, *refs):
    count = len(PARTS)
    out_ref, held_ref, sems = refs[2 * count :]
    copies = []
    for p in range(count):
        for side in range(NC):
            target = held_ref.at[p, :, pl.ds(side * BLOCK, BLOCK), :]
            copies.append(pltpu.make_async_copy(refs[side * count + p], target, sems.at[p, side]))
    for copy in copies:
        copy.start()
    x, y, core = place_ref[0], place_ref[3], place_ref[2]
    total = None
    for p, (shift, first) in enumerate(PARTS):
        copies[2 * p].wait()
        copies[2 * p + 1].wait()
        for s in range(NX // 2):
            source = (lax.rem(x - first - s + NX, NX) * NY + lax.rem(y + shift + NY, NY)) * NC
            grads = jnp.concatenate([grads_ref[source + core], grads_ref[source + 1 - core]], axis=1)
            part = dot(grads, held_ref[p, s])
            total = part if total is None else total + part
    out_ref[...] = total.T.astype(jnp.bfloat16)


def weight_grads_part(place, grads, own, other):
    half, rows, width = own[0].shape
    vmem = pl.BlockSpec(memory_space=pltpu.VMEM)
    return pl.pallas_call(
        weight_kernel,
        out_shape=jax.ShapeDtypeStruct((width, HEAD), jnp.bfloat16),
        in_specs=[pl.BlockSpec(memory_space=pltpu.SMEM), vmem]
        + [pl.BlockSpec(memory_space=pltpu.HBM)] * (2 * len(PARTS)),
        out_specs=vmem,
        scratch_shapes=[
            pltpu.VMEM((len(PARTS), half, NC * rows, width), jnp.bfloat16),
            pltpu.SemaphoreType.DMA((len(PARTS), NC)),
        ],
        compiler_params=pltpu.CompilerParams(vmem_limit_bytes=24 * MIB),
        cost_estimate=pl.CostEstimate(
            flops=1_100_000_000, bytes_accessed=9 * MIB, transcendentals=0
        ),
    )(place, grads, *placed(own, pltpu.HBM), *placed(other, pltpu.HBM))


def pack_kernel(queries_ref, grads_ref, keys_ref, values_ref, out_ref, *refs):
    q_ref, g_ref, k_ref, v_ref, sem, store_sem = refs
    loads = [
        pltpu.make_async_copy(a, b, sem.at[n])
        for n, (a, b) in enumerate(((queries_ref, q_ref), (grads_ref, g_ref), (keys_ref, k_ref), (values_ref, v_ref)))
    ]
    for copy in loads:
        copy.start()
    stores = []
    for load, ref, first, size, shared in (
        (loads[0], q_ref, 0, 2, 1), (loads[1], g_ref, 2, 2, 1), (loads[2], k_ref, 4, 1, 2), (loads[3], v_ref, 5, 1, 2)
    ):
        load.wait()
        for i in range(NZ):
            source = ref.at[:, pl.ds(size * HEAD * (i // shared), size * HEAD)]
            copy = pltpu.make_async_copy(source, out_ref.at[i, :, pl.ds(first * HEAD, size * HEAD)], store_sem.at[len(stores)])
            copy.start()
            stores.append(copy)
    for copy in stores:
        copy.wait()


def packed(queries, grads, keys, values):
    return pl.pallas_call(
        pack_kernel,
        out_shape=pltpu.HBM((NZ, BLOCK, 6 * HEAD), jnp.bfloat16),
        in_specs=[pl.BlockSpec(memory_space=pltpu.HBM)] * 4,
        out_specs=pl.BlockSpec(memory_space=pltpu.HBM),
        scratch_shapes=[pltpu.VMEM(a.shape, a.dtype) for a in (queries, grads, keys, values)]
        + [pltpu.SemaphoreType.DMA((4,)), pltpu.SemaphoreType.DMA((4 * NZ,))],
        compiler_params=pltpu.CompilerParams(vmem_limit_bytes=16 * MIB),
        cost_estimate=pl.CostEstimate(flops=0, bytes_accessed=3 * MIB, transcendentals=0),
    )(*placed((queries, grads, keys, values), pltpu.HBM))


def pair_kernel(partials_ref, keys_ref, values_ref, chunks_ref):
    for g in range(KV_HEADS):
        pair = partials_ref[2 * g].astype(jnp.float32) + partials_ref[2 * g + 1].astype(jnp.float32)
        pair = pair.astype(jnp.bfloat16)
        for kind, ref in enumerate((keys_ref, values_ref)):
            part = pair[:, kind * HEAD : (kind + 1) * HEAD]
            ref[:, g * HEAD : (g + 1) * HEAD] = part
            part = part.T
            for x in range(NX):
                chunks_ref[(x * NY + g) * NC + kind] = part


def pair_grads(partials):
    vmem = pl.BlockSpec(memory_space=pltpu.VMEM)
    out = jax.ShapeDtypeStruct((BLOCK, KV_HEADS * HEAD), jnp.bfloat16)
    return pl.pallas_call(
        pair_kernel,
        out_shape=(out, out, jax.ShapeDtypeStruct((NX * NY * NC, HEAD, BLOCK), jnp.bfloat16)),
        in_specs=[vmem],
        out_specs=(vmem, vmem, vmem),
        compiler_params=pltpu.CompilerParams(vmem_limit_bytes=16 * MIB),
        cost_estimate=pl.CostEstimate(flops=0, bytes_accessed=2 * MIB, transcendentals=0),
    )(partials)


def join_kernel(place_ref, keep_ref, across_ref, *refs):
    direct_refs, swapped_ref, out_ref = refs[:SIDE], refs[SIDE], refs[SIDE + 1]
    z, side = place_ref[1], 1 - 2 * place_ref[2]

    def put(source, value):
        column = lax.rem(source + NZ, NZ) * (2 * HEAD)
        out_ref[:, pl.ds(pl.multiple_of(column, 2 * HEAD), 2 * HEAD)] = value

    put(z, keep_ref[...])
    put(z + NZ // 2, across_ref[...])
    for k in range(SIDE):
        put(z - side * (k + 1), direct_refs[k][0])
        put(z + side * (k + 1), swapped_ref[k])


def joined(place, keep, across, direct, swapped):
    vmem = pl.BlockSpec(memory_space=pltpu.VMEM)
    return pl.pallas_call(
        join_kernel,
        out_shape=jax.ShapeDtypeStruct((BLOCK, NZ * 2 * HEAD), jnp.bfloat16),
        in_specs=[pl.BlockSpec(memory_space=pltpu.SMEM)] + [vmem] * (SIDE + 3),
        out_specs=vmem,
        compiler_params=pltpu.CompilerParams(vmem_limit_bytes=16 * MIB),
        cost_estimate=pl.CostEstimate(flops=0, bytes_accessed=MIB, transcendentals=0),
    )(place, keep, across, *direct, swapped)


def ring(size, shift):
    return [(i, (i + shift) % size) for i in range(size)]


def swap_cores(a):
    return lax.ppermute(a, "c", [(0, 1), (1, 0)])


def local(layer_input, queries, keys, values, output_grads, block_links, segment_ids):
    x, y, z, core = (lax.axis_index(axis) for axis in ("x", "y", "z", "c"))
    place = jnp.stack([x, z, core, y]).astype(jnp.int32)
    bf16 = jnp.bfloat16

    inputs = layer_input[0]
    width = inputs.shape[1] // NX
    pieces = [
        lax.dynamic_slice_in_dim(inputs, lax.rem(x + s, NX) * width, width, axis=1)
        for s in range(NX)
    ]
    near = lax.ppermute(pieces[1], "x", ring(NX, 1))
    near, later = lax.optimization_barrier((near, pieces[2:]))
    pieces = [pieces[0], near] + [
        lax.ppermute(a, "x", ring(NX, s)) for s, a in enumerate(later, 2)
    ]
    half = NX // 2
    mine = (jnp.stack(pieces[:half]), jnp.stack(pieces[half:]))
    before, after = zip(
        *[[lax.ppermute(a, "y", ring(NY, shift)) for shift in (1, -1)] for a in mine]
    )
    far = (
        lax.ppermute(before[0], "y", ring(NY, 1)),
        lax.ppermute(after[1], "y", ring(NY, -1)),
    )

    outgoing = packed(queries[0], output_grads[0], keys[0], values[0])
    rows = lax.all_to_all(outgoing, "z", split_axis=0, concat_axis=0, tiled=True)
    seg_rows = segment_ids[0].reshape(BLOCKS, BLOCK)
    seg_cols = jnp.broadcast_to(seg_rows[:, :, None], (BLOCKS, BLOCK, BLOCK))
    rows, mine, before, after, seg_cols = lax.optimization_barrier(
        (rows, mine, before, after, seg_cols)
    )
    other = swap_cores(rows[..., 4 * HEAD :])
    keep, across, *ship, give, own, away = attention_grads(
        block_links[0], place, rows, other, seg_cols, seg_rows
    )
    inputs_own = mine + before + after + far
    keep, across, ship, give, own, away, inputs_own = lax.optimization_barrier(
        (keep, across, ship, give, own, away, inputs_own)
    )
    inputs_other = tuple(swap_cores(a) for a in inputs_own)

    pair = (own + swap_cores(away).astype(jnp.float32)).astype(bf16)
    pair = lax.all_to_all(pair, "z", split_axis=0, concat_axis=0, tiled=True)
    given = swap_cores(give)
    across, ship, given, pair, inputs_other = lax.optimization_barrier(
        (across, ship, given, pair, inputs_other)
    )
    key_grads, value_grads, chunks = pair_grads(pair)

    grads = lax.all_to_all(chunks, ("x", "y", "c"), split_axis=0, concat_axis=0, tiled=True)
    direct = []
    for k in range(SIDE):
        hops = [((i, 0), ((i + k + 1) % NZ, 0)) for i in range(NZ)]
        hops += [((i, 1), ((i - k - 1) % NZ, 1)) for i in range(NZ)]
        hops = [tuple(a * NC + b for a, b in hop) for hop in hops]
        direct.append(lax.ppermute(jnp.stack([ship[k], given[k]]), ("z", "c"), hops))
    across = lax.ppermute(across, "z", ring(NZ, NZ // 2))
    grads, direct, across = lax.optimization_barrier((grads, direct, across))
    part = weight_grads_part(place, grads, inputs_own, inputs_other)

    swapped = swap_cores(jnp.stack([a[1] for a in direct]))
    query_grads = joined(place, keep, across, direct, swapped)
    part = part.reshape(NY * NZ * NC, -1, HEAD)
    part = lax.all_to_all(part, ("y", "z", "c"), split_axis=0, concat_axis=0, tiled=True)
    part = part.reshape(NY, NZ, NC, -1, HEAD).astype(jnp.float32)
    part = jnp.transpose(jnp.sum(part, axis=1), (1, 2, 0, 3))
    part = part.reshape(NC, -1, NY * HEAD)
    return query_grads[None], key_grads[None], value_grads[None], part[0], part[1]


def solution(mesh):
    chips = Mesh(mesh.devices.reshape(NX, NY, NZ, NC), ("x", "y", "z", "c"))
    dp, seq = ("x", "y"), ("z", "c")
    by_position = P(dp, seq, None)
    return jax.shard_map(
        local,
        mesh=chips,
        in_specs=(by_position,) * 5 + (P(dp, None, None), P(dp, None)),
        out_specs=(by_position,) * 3 + (P(dp + seq, None),) * 2,
        check_vma=False,
    )
```

```python
import math

import jax
import jax.numpy as jnp
from jax import lax
from jax.experimental import pallas as pl
from jax.experimental.pallas import tpu as pltpu
from jax.sharding import Mesh, PartitionSpec as P

NX, NY, NZ, NC = 4, 4, 8, 2
HEAD = 128
BLOCK = 128
BLOCKS = NZ * NC
LINKS = 8
KV_HEADS = 4
SIDE = NZ // 2 - 1
MIB = 1 << 20
SCALE = 1.0 / math.sqrt(HEAD)
LOG2E = math.log2(math.e)
MASKED = -1e30


def placed(arrays, space):
    return tuple(pltpu.with_memory_space_constraint(a, space) for a in arrays)


def dot(a, b):
    return lax.dot_general(
        a, b, (((1,), (0,)), ((), ())), preferred_element_type=jnp.float32
    )


def dot_nt(a, b):
    return lax.dot_general(
        a, b, (((1,), (1,)), ((), ())), preferred_element_type=jnp.float32
    )


def attention_kernel(
    links_ref, place_ref, rows_ref, other_ref, seg_cols_ref, seg_rows_ref, *refs
):
    (keep_ref, across_ref, *ship_refs, give_ref), refs = refs[: SIDE + 3], refs[SIDE + 3 :]
    own_ref, away_ref, pair_ref, keys_t_ref, total_ref, dq_ref, *refs = refs
    even, odd = refs[:4], refs[4:8]
    score_ref, prob_ref, wide_ref, flat_ref, sems = refs[8:]
    z, core = place_ref[1], place_ref[2]

    def at(block):
        return pl.ds(pl.multiple_of(block * BLOCK, BLOCK), BLOCK)

    def load_pairs(i, carry):
        for block, pair in ((2 * i + core, rows_ref[i, :, 4 * HEAD:]), (2 * i + 1 - core, other_ref[i])):
            pair_ref[at(block), :] = pair
            keys_t_ref[:, at(block)] = pair[:, :HEAD].T
        return carry

    lax.fori_loop(0, NZ, load_pairs, 0, unroll=True)
    total_ref[...] = jnp.zeros_like(total_ref)

    def stacked(i, first):
        rows = rows_ref[i]
        return jnp.concatenate(
            [rows[:, first * HEAD : (first + 1) * HEAD], rows[:, (first + 1) * HEAD : (first + 2) * HEAD]],
            axis=0,
        )

    def softmax_part(i, key_blocks, pairs, score_ref, prob_ref, attention, score_grads):
        queries, grads = stacked(i, 0), stacked(i, 2)
        seg = seg_rows_ref[pl.ds(2 * i + core, 1), :]
        count = len(key_blocks)
        top = None
        for t, j in enumerate(key_blocks):
            here = pl.ds(t * BLOCK, BLOCK)
            allowed = seg_cols_ref[j] == seg
            s = dot_nt(pairs[here, :HEAD], queries) * (SCALE * LOG2E)
            s = jnp.where(jnp.concatenate([allowed, allowed], axis=1), s, MASKED)
            score_ref[here, :] = s
            part = jnp.max(s.reshape(BLOCK // 8, 8, -1), axis=0)
            top = part if top is None else jnp.maximum(top, part)
        top = jnp.max(top, axis=0, keepdims=True)
        norm = None
        for t in range(count):
            here = pl.ds(t * BLOCK, BLOCK)
            e = jnp.exp2(score_ref[here, :] - top)
            score_ref[here, :] = e
            part = jnp.sum(e.reshape(BLOCK // 8, 8, -1), axis=0)
            norm = part if norm is None else norm + part
            yield
        inverse = 1.0 / jnp.sum(norm, axis=0, keepdims=True)
        delta = None
        for t in range(count):
            here = pl.ds(t * BLOCK, BLOCK)
            a = (score_ref[here, :] * inverse).astype(jnp.bfloat16)
            attention[here, :] = a
            g = dot_nt(pairs[here, HEAD:], grads)
            prob_ref[here, :] = g
            part = jnp.sum((a.astype(jnp.float32) * g).reshape(BLOCK // 8, 8, -1), axis=0)
            delta = part if delta is None else delta + part
        delta = jnp.sum(delta, axis=0, keepdims=True)
        for t in range(count):
            here = pl.ds(t * BLOCK, BLOCK)
            ds = (score_ref[here, :] * inverse) * (prob_ref[here, :] - delta)
            score_grads[here, :] = ds.astype(jnp.bfloat16)
            yield

    def product_part(i, key_blocks, keys_t, attention, score_grads):
        queries, grads = stacked(i, 0), stacked(i, 2)
        count = len(key_blocks)
        step = 4
        dq = (dot(keys_t[...], score_grads[...]) * SCALE).astype(jnp.bfloat16).T
        slot = lax.rem(i - z + NZ, NZ)
        dq_ref[slot, :, :HEAD] = dq[:BLOCK]
        dq_ref[slot, :, HEAD:] = dq[BLOCK:]
        yield
        for held, other, columns in (
            (attention, grads, slice(HEAD, 2 * HEAD)), (score_grads, queries, slice(0, HEAD))
        ):
            for t in range(0, count, step):
                part = dot(held[pl.ds(t * BLOCK, step * BLOCK), :], other)
                for u in range(step):
                    total_ref[at(key_blocks[t + u]), columns] += part[u * BLOCK : (u + 1) * BLOCK]
                yield

    def run(*parts):
        parts = list(parts)
        while parts:
            for part in list(parts):
                if next(part, parts) is parts:
                    parts.remove(part)

    def linked(i):
        return [links_ref[2 * i + core, t] for t in range(LINKS)]

    def first_part(i, held):
        key_blocks, (near, near_t, attention, score_grads) = linked(i), held
        for t, j in enumerate(key_blocks):
            here = pl.ds(t * BLOCK, BLOCK)
            near[here, :] = pair_ref[at(j), :]
            near_t[:, here] = keys_t_ref[:, at(j)]
        return softmax_part(i, key_blocks, near, score_ref, prob_ref, attention, score_grads)

    def second_part(i, held):
        return product_part(i, linked(i), *held[1:])

    @pl.when(core == 0)
    def _():
        key_blocks = list(range(BLOCKS))
        attention, score_grads = flat_ref.at[0], flat_ref.at[1]
        run(softmax_part(0, key_blocks, pair_ref, wide_ref.at[0], wide_ref.at[1], attention, score_grads))
        run(first_part(1, odd), product_part(0, key_blocks, keys_t_ref, attention, score_grads))

    @pl.when(core == 1)
    def _():
        run(first_part(0, even))
        run(first_part(1, odd), second_part(0, even))

    def two(h, carry):
        run(first_part(2 * h, even), second_part(2 * h - 1, odd))
        run(first_part(2 * h + 1, odd), second_part(2 * h, even))
        return carry

    lax.fori_loop(1, NZ // 2, two, 0)
    run(second_part(NZ - 1, odd))

    moves = [(0, keep_ref), (NZ // 2, across_ref)]
    for k, ref in enumerate(ship_refs):
        up, down = k + 1, NZ - 1 - k
        moves.append((up + core * (down - up), ref))
        moves.append((down + core * (up - down), give_ref.at[k]))
    copies = [
        pltpu.make_async_copy(dq_ref.at[slot], ref, sems.at[n])
        for n, (slot, ref) in enumerate(moves)
    ]
    for copy in copies:
        copy.start()

    def store(i, carry):
        for ref, block in ((own_ref, 2 * i + core), (away_ref, 2 * i + 1 - core)):
            ref[i, :, :HEAD] = (total_ref[at(block), :HEAD] * SCALE).astype(ref.dtype)
            ref[i, :, HEAD:] = total_ref[at(block), HEAD:].astype(ref.dtype)
        return carry

    lax.fori_loop(0, NZ, store, 0, unroll=True)
    for copy in copies:
        copy.wait()


def attention_grads(links, place, rows, other, seg_cols, seg_rows):
    vmem = pl.BlockSpec(memory_space=pltpu.VMEM)
    smem = pl.BlockSpec(memory_space=pltpu.SMEM)
    return pl.pallas_call(
        attention_kernel,
        out_shape=(pltpu.HBM((BLOCK, 2 * HEAD), jnp.bfloat16),) * (SIDE + 2)
        + (pltpu.HBM((SIDE, BLOCK, 2 * HEAD), jnp.bfloat16),)
        + (
            jax.ShapeDtypeStruct((NZ, BLOCK, 2 * HEAD), jnp.float32),
            jax.ShapeDtypeStruct((NZ, BLOCK, 2 * HEAD), jnp.bfloat16),
        ),
        in_specs=[smem, smem, vmem, vmem, vmem, vmem],
        out_specs=(pl.BlockSpec(memory_space=pltpu.HBM),) * (SIDE + 3) + (vmem, vmem),
        scratch_shapes=[
            pltpu.VMEM((BLOCKS * BLOCK, 2 * HEAD), jnp.bfloat16),
            pltpu.VMEM((HEAD, BLOCKS * BLOCK), jnp.bfloat16),
            pltpu.VMEM((BLOCKS * BLOCK, 2 * HEAD), jnp.float32),
            pltpu.VMEM((NZ, BLOCK, 2 * HEAD), jnp.bfloat16),
        ]
        + [
            pltpu.VMEM((LINKS * BLOCK, 2 * HEAD), jnp.bfloat16),
            pltpu.VMEM((HEAD, LINKS * BLOCK), jnp.bfloat16),
            pltpu.VMEM((LINKS * BLOCK, 2 * HEAD), jnp.bfloat16),
            pltpu.VMEM((LINKS * BLOCK, 2 * HEAD), jnp.bfloat16),
        ]
        * 2
        + [
            pltpu.VMEM((LINKS * BLOCK, 2 * HEAD), jnp.float32),
            pltpu.VMEM((LINKS * BLOCK, 2 * HEAD), jnp.float32),
            pltpu.VMEM((2, BLOCKS * BLOCK, 2 * HEAD), jnp.float32),
            pltpu.VMEM((2, BLOCKS * BLOCK, 2 * HEAD), jnp.bfloat16),
            pltpu.SemaphoreType.DMA((NZ,)),
        ],
        compiler_params=pltpu.CompilerParams(vmem_limit_bytes=32 * MIB),
        cost_estimate=pl.CostEstimate(
            flops=1_000, bytes_accessed=1_000, transcendentals=0
        ),
    )(links, place, rows, other, seg_cols, seg_rows)


PARTS = tuple((shift, first) for shift in (0, -1, 1, 2) for first in (0, NX // 2))


def weight_kernel(place_ref, grads_ref, *refs):
    count = len(PARTS)
    out_ref, held_ref, sems = refs[2 * count :]
    copies = []
    for p in range(count):
        for side in range(NC):
            target = held_ref.at[p, :, pl.ds(side * BLOCK, BLOCK), :]
            copies.append(pltpu.make_async_copy(refs[side * count + p], target, sems.at[p, side]))
    for copy in copies:
        copy.start()
    x, y, core = place_ref[0], place_ref[3], place_ref[2]
    total = None
    for p, (shift, first) in enumerate(PARTS):
        copies[2 * p].wait()
        copies[2 * p + 1].wait()
        for s in range(NX // 2):
            source = (lax.rem(x - first - s + NX, NX) * NY + lax.rem(y + shift + NY, NY)) * NC
            grads = jnp.concatenate([grads_ref[source + core], grads_ref[source + 1 - core]], axis=1)
            part = dot(grads, held_ref[p, s])
            total = part if total is None else total + part
    out_ref[...] = total.T.astype(jnp.bfloat16)


def weight_grads_part(place, grads, own, other):
    half, rows, width = own[0].shape
    vmem = pl.BlockSpec(memory_space=pltpu.VMEM)
    return pl.pallas_call(
        weight_kernel,
        out_shape=jax.ShapeDtypeStruct((width, HEAD), jnp.bfloat16),
        in_specs=[pl.BlockSpec(memory_space=pltpu.SMEM), vmem]
        + [pl.BlockSpec(memory_space=pltpu.HBM)] * (2 * len(PARTS)),
        out_specs=vmem,
        scratch_shapes=[
            pltpu.VMEM((len(PARTS), half, NC * rows, width), jnp.bfloat16),
            pltpu.SemaphoreType.DMA((len(PARTS), NC)),
        ],
        compiler_params=pltpu.CompilerParams(vmem_limit_bytes=24 * MIB),
        cost_estimate=pl.CostEstimate(
            flops=1_100_000_000, bytes_accessed=9 * MIB, transcendentals=0
        ),
    )(place, grads, *placed(own, pltpu.HBM), *placed(other, pltpu.HBM))


def pack_kernel(queries_ref, grads_ref, keys_ref, values_ref, out_ref, *refs):
    q_ref, g_ref, k_ref, v_ref, sem, store_sem = refs
    loads = [
        pltpu.make_async_copy(a, b, sem.at[n])
        for n, (a, b) in enumerate(((queries_ref, q_ref), (grads_ref, g_ref), (keys_ref, k_ref), (values_ref, v_ref)))
    ]
    for copy in loads:
        copy.start()
    stores = []
    for load, ref, first, size, shared in (
        (loads[0], q_ref, 0, 2, 1), (loads[1], g_ref, 2, 2, 1), (loads[2], k_ref, 4, 1, 2), (loads[3], v_ref, 5, 1, 2)
    ):
        load.wait()
        for i in range(NZ):
            source = ref.at[:, pl.ds(size * HEAD * (i // shared), size * HEAD)]
            copy = pltpu.make_async_copy(source, out_ref.at[i, :, pl.ds(first * HEAD, size * HEAD)], store_sem.at[len(stores)])
            copy.start()
            stores.append(copy)
    for copy in stores:
        copy.wait()


def packed(queries, grads, keys, values):
    return pl.pallas_call(
        pack_kernel,
        out_shape=pltpu.HBM((NZ, BLOCK, 6 * HEAD), jnp.bfloat16),
        in_specs=[pl.BlockSpec(memory_space=pltpu.HBM)] * 4,
        out_specs=pl.BlockSpec(memory_space=pltpu.HBM),
        scratch_shapes=[pltpu.VMEM(a.shape, a.dtype) for a in (queries, grads, keys, values)]
        + [pltpu.SemaphoreType.DMA((4,)), pltpu.SemaphoreType.DMA((4 * NZ,))],
        compiler_params=pltpu.CompilerParams(vmem_limit_bytes=16 * MIB),
        cost_estimate=pl.CostEstimate(flops=0, bytes_accessed=3 * MIB, transcendentals=0),
    )(*placed((queries, grads, keys, values), pltpu.HBM))


def pair_kernel(partials_ref, keys_ref, values_ref, chunks_ref):
    for g in range(KV_HEADS):
        pair = partials_ref[2 * g].astype(jnp.float32) + partials_ref[2 * g + 1].astype(jnp.float32)
        pair = pair.astype(jnp.bfloat16)
        for kind, ref in enumerate((keys_ref, values_ref)):
            part = pair[:, kind * HEAD : (kind + 1) * HEAD]
            ref[:, g * HEAD : (g + 1) * HEAD] = part
            part = part.T
            for x in range(NX):
                chunks_ref[(x * NY + g) * NC + kind] = part


def pair_grads(partials):
    vmem = pl.BlockSpec(memory_space=pltpu.VMEM)
    out = jax.ShapeDtypeStruct((BLOCK, KV_HEADS * HEAD), jnp.bfloat16)
    return pl.pallas_call(
        pair_kernel,
        out_shape=(out, out, jax.ShapeDtypeStruct((NX * NY * NC, HEAD, BLOCK), jnp.bfloat16)),
        in_specs=[vmem],
        out_specs=(vmem, vmem, vmem),
        compiler_params=pltpu.CompilerParams(vmem_limit_bytes=16 * MIB),
        cost_estimate=pl.CostEstimate(flops=0, bytes_accessed=2 * MIB, transcendentals=0),
    )(partials)


def join_kernel(place_ref, keep_ref, across_ref, *refs):
    direct_refs, swapped_ref, out_ref = refs[:SIDE], refs[SIDE], refs[SIDE + 1]
    z, side = place_ref[1], 1 - 2 * place_ref[2]

    def put(source, value):
        column = lax.rem(source + NZ, NZ) * (2 * HEAD)
        out_ref[:, pl.ds(pl.multiple_of(column, 2 * HEAD), 2 * HEAD)] = value

    put(z, keep_ref[...])
    put(z + NZ // 2, across_ref[...])
    for k in range(SIDE):
        put(z - side * (k + 1), direct_refs[k][0])
        put(z + side * (k + 1), swapped_ref[k])


def joined(place, keep, across, direct, swapped):
    vmem = pl.BlockSpec(memory_space=pltpu.VMEM)
    return pl.pallas_call(
        join_kernel,
        out_shape=jax.ShapeDtypeStruct((BLOCK, NZ * 2 * HEAD), jnp.bfloat16),
        in_specs=[pl.BlockSpec(memory_space=pltpu.SMEM)] + [vmem] * (SIDE + 3),
        out_specs=vmem,
        compiler_params=pltpu.CompilerParams(vmem_limit_bytes=16 * MIB),
        cost_estimate=pl.CostEstimate(flops=0, bytes_accessed=MIB, transcendentals=0),
    )(place, keep, across, *direct, swapped)


def ring(size, shift):
    return [(i, (i + shift) % size) for i in range(size)]


def swap_cores(a):
    return lax.ppermute(a, "c", [(0, 1), (1, 0)])


def local(layer_input, queries, keys, values, output_grads, block_links, segment_ids):
    x, y, z, core = (lax.axis_index(axis) for axis in ("x", "y", "z", "c"))
    place = jnp.stack([x, z, core, y]).astype(jnp.int32)
    bf16 = jnp.bfloat16

    inputs = layer_input[0]
    width = inputs.shape[1] // NX
    pieces = [
        lax.dynamic_slice_in_dim(inputs, lax.rem(x + s, NX) * width, width, axis=1)
        for s in range(NX)
    ]
    near = lax.ppermute(pieces[1], "x", ring(NX, 1))
    near, later = lax.optimization_barrier((near, pieces[2:]))
    pieces = [pieces[0], near] + [
        lax.ppermute(a, "x", ring(NX, s)) for s, a in enumerate(later, 2)
    ]
    half = NX // 2
    mine = (jnp.stack(pieces[:half]), jnp.stack(pieces[half:]))
    before, after = zip(
        *[[lax.ppermute(a, "y", ring(NY, shift)) for shift in (1, -1)] for a in mine]
    )
    far = (
        lax.ppermute(before[0], "y", ring(NY, 1)),
        lax.ppermute(after[1], "y", ring(NY, -1)),
    )

    outgoing = packed(queries[0], output_grads[0], keys[0], values[0])
    rows = lax.all_to_all(outgoing, "z", split_axis=0, concat_axis=0, tiled=True)
    seg_rows = segment_ids[0].reshape(BLOCKS, BLOCK)
    seg_cols = jnp.broadcast_to(seg_rows[:, :, None], (BLOCKS, BLOCK, BLOCK))
    rows, mine, before, after, seg_cols = lax.optimization_barrier(
        (rows, mine, before, after, seg_cols)
    )
    other = swap_cores(rows[..., 4 * HEAD :])
    keep, across, *ship, give, own, away = attention_grads(
        block_links[0], place, rows, other, seg_cols, seg_rows
    )
    inputs_own = mine + before + after + far
    keep, across, ship, give, own, away, inputs_own = lax.optimization_barrier(
        (keep, across, ship, give, own, away, inputs_own)
    )
    inputs_other = tuple(swap_cores(a) for a in inputs_own)

    pair = (own + swap_cores(away).astype(jnp.float32)).astype(bf16)
    pair = lax.all_to_all(pair, "z", split_axis=0, concat_axis=0, tiled=True)
    given = swap_cores(give)
    across, ship, given, pair, inputs_other = lax.optimization_barrier(
        (across, ship, given, pair, inputs_other)
    )
    key_grads, value_grads, chunks = pair_grads(pair)

    grads = lax.all_to_all(chunks, ("x", "y", "c"), split_axis=0, concat_axis=0, tiled=True)
    direct = []
    for k in range(SIDE):
        hops = [((i, 0), ((i + k + 1) % NZ, 0)) for i in range(NZ)]
        hops += [((i, 1), ((i - k - 1) % NZ, 1)) for i in range(NZ)]
        hops = [tuple(a * NC + b for a, b in hop) for hop in hops]
        direct.append(lax.ppermute(jnp.stack([ship[k], given[k]]), ("z", "c"), hops))
    across = lax.ppermute(across, "z", ring(NZ, NZ // 2))
    grads, direct, across = lax.optimization_barrier((grads, direct, across))
    part = weight_grads_part(place, grads, inputs_own, inputs_other)

    swapped = swap_cores(jnp.stack([a[1] for a in direct]))
    query_grads = joined(place, keep, across, direct, swapped)
    part = part.reshape(NY * NZ * NC, -1, HEAD)
    part = lax.all_to_all(part, ("y", "z", "c"), split_axis=0, concat_axis=0, tiled=True)
    part = part.reshape(NY, NZ, NC, -1, HEAD).astype(jnp.float32)
    part = jnp.transpose(jnp.sum(part, axis=1), (1, 2, 0, 3))
    part = part.reshape(NC, -1, NY * HEAD)
    return query_grads[None], key_grads[None], value_grads[None], part[0], part[1]


def solution(mesh):
    chips = Mesh(mesh.devices.reshape(NX, NY, NZ, NC), ("x", "y", "z", "c"))
    dp, seq = ("x", "y"), ("z", "c")
    by_position = P(dp, seq, None)
    return jax.shard_map(
        local,
        mesh=chips,
        in_specs=(by_position,) * 5 + (P(dp, None, None), P(dp, None)),
        out_specs=(by_position,) * 3 + (P(dp + seq, None),) * 2,
        check_vma=False,
    )
```

```python
import math

import jax
import jax.numpy as jnp
from jax import lax
from jax.experimental import pallas as pl
from jax.experimental.pallas import tpu as pltpu
from jax.sharding import Mesh, PartitionSpec as P

NX, NY, NZ, NC = 4, 4, 8, 2
HEAD = 128
BLOCK = 128
BLOCKS = NZ * NC
LINKS = 8
KV_HEADS = 4
SIDE = NZ // 2 - 1
MIB = 1 << 20
SCALE = 1.0 / math.sqrt(HEAD)
LOG2E = math.log2(math.e)
MASKED = -1e30


def placed(arrays, space):
    return tuple(pltpu.with_memory_space_constraint(a, space) for a in arrays)


def dot(a, b):
    return lax.dot_general(
        a, b, (((1,), (0,)), ((), ())), preferred_element_type=jnp.float32
    )


def dot_nt(a, b):
    return lax.dot_general(
        a, b, (((1,), (1,)), ((), ())), preferred_element_type=jnp.float32
    )


def attention_kernel(
    links_ref, place_ref, rows_ref, other_ref, seg_cols_ref, seg_rows_ref, *refs
):
    (keep_ref, across_ref, *ship_refs, give_ref), refs = refs[: SIDE + 3], refs[SIDE + 3 :]
    own_ref, away_ref, pair_ref, keys_t_ref, total_ref, dq_ref, *refs = refs
    even, odd = refs[:4], refs[4:8]
    score_ref, prob_ref, wide_ref, flat_ref, sems = refs[8:]
    z, core = place_ref[1], place_ref[2]

    def at(block):
        return pl.ds(pl.multiple_of(block * BLOCK, BLOCK), BLOCK)

    def load_pairs(i, carry):
        for block, pair in ((2 * i + core, rows_ref[i, :, 4 * HEAD:]), (2 * i + 1 - core, other_ref[i])):
            pair_ref[at(block), :] = pair
            keys_t_ref[:, at(block)] = pair[:, :HEAD].T
        return carry

    lax.fori_loop(0, NZ, load_pairs, 0)
    total_ref[...] = jnp.zeros_like(total_ref)

    def stacked(i, first):
        rows = rows_ref[i]
        return jnp.concatenate(
            [rows[:, first * HEAD : (first + 1) * HEAD], rows[:, (first + 1) * HEAD : (first + 2) * HEAD]],
            axis=0,
        )

    def softmax_part(i, key_blocks, pairs, score_ref, prob_ref, attention, score_grads):
        queries, grads = stacked(i, 0), stacked(i, 2)
        seg = seg_rows_ref[pl.ds(2 * i + core, 1), :]
        count = len(key_blocks)
        top = None
        for t, j in enumerate(key_blocks):
            here = pl.ds(t * BLOCK, BLOCK)
            allowed = seg_cols_ref[j] == seg
            s = dot_nt(pairs[here, :HEAD], queries) * (SCALE * LOG2E)
            s = jnp.where(jnp.concatenate([allowed, allowed], axis=1), s, MASKED)
            score_ref[here, :] = s
            part = jnp.max(s.reshape(BLOCK // 8, 8, -1), axis=0)
            top = part if top is None else jnp.maximum(top, part)
        top = jnp.max(top, axis=0, keepdims=True)
        norm = None
        for t in range(count):
            here = pl.ds(t * BLOCK, BLOCK)
            e = jnp.exp2(score_ref[here, :] - top)
            score_ref[here, :] = e
            part = jnp.sum(e.reshape(BLOCK // 8, 8, -1), axis=0)
            norm = part if norm is None else norm + part
            yield
        inverse = 1.0 / jnp.sum(norm, axis=0, keepdims=True)
        delta = None
        for t in range(count):
            here = pl.ds(t * BLOCK, BLOCK)
            a = (score_ref[here, :] * inverse).astype(jnp.bfloat16)
            attention[here, :] = a
            g = dot_nt(pairs[here, HEAD:], grads)
            prob_ref[here, :] = g
            part = jnp.sum((a.astype(jnp.float32) * g).reshape(BLOCK // 8, 8, -1), axis=0)
            delta = part if delta is None else delta + part
        delta = jnp.sum(delta, axis=0, keepdims=True)
        for t in range(count):
            here = pl.ds(t * BLOCK, BLOCK)
            ds = (score_ref[here, :] * inverse) * (prob_ref[here, :] - delta)
            score_grads[here, :] = ds.astype(jnp.bfloat16)
            yield

    def product_part(i, key_blocks, keys_t, attention, score_grads):
        queries, grads = stacked(i, 0), stacked(i, 2)
        count = len(key_blocks)
        step = 4
        dq = (dot(keys_t[...], score_grads[...]) * SCALE).astype(jnp.bfloat16).T
        slot = lax.rem(i - z + NZ, NZ)
        dq_ref[slot, :, :HEAD] = dq[:BLOCK]
        dq_ref[slot, :, HEAD:] = dq[BLOCK:]
        yield
        for held, other, columns in (
            (attention, grads, slice(HEAD, 2 * HEAD)), (score_grads, queries, slice(0, HEAD))
        ):
            for t in range(0, count, step):
                part = dot(held[pl.ds(t * BLOCK, step * BLOCK), :], other)
                for u in range(step):
                    total_ref[at(key_blocks[t + u]), columns] += part[u * BLOCK : (u + 1) * BLOCK]
                yield

    def run(*parts):
        parts = list(parts)
        while parts:
            for part in list(parts):
                if next(part, parts) is parts:
                    parts.remove(part)

    def linked(i):
        return [links_ref[2 * i + core, t] for t in range(LINKS)]

    def first_part(i, held):
        key_blocks, (near, near_t, attention, score_grads) = linked(i), held
        for t, j in enumerate(key_blocks):
            here = pl.ds(t * BLOCK, BLOCK)
            near[here, :] = pair_ref[at(j), :]
            near_t[:, here] = keys_t_ref[:, at(j)]
        return softmax_part(i, key_blocks, near, score_ref, prob_ref, attention, score_grads)

    def second_part(i, held):
        return product_part(i, linked(i), *held[1:])

    @pl.when(core == 0)
    def _():
        key_blocks = list(range(BLOCKS))
        attention, score_grads = flat_ref.at[0], flat_ref.at[1]
        run(softmax_part(0, key_blocks, pair_ref, wide_ref.at[0], wide_ref.at[1], attention, score_grads))
        run(first_part(1, odd), product_part(0, key_blocks, keys_t_ref, attention, score_grads))

    @pl.when(core == 1)
    def _():
        run(first_part(0, even))
        run(first_part(1, odd), second_part(0, even))

    def two(h, carry):
        run(first_part(2 * h, even), second_part(2 * h - 1, odd))
        run(first_part(2 * h + 1, odd), second_part(2 * h, even))
        return carry

    lax.fori_loop(1, NZ // 2, two, 0)
    run(second_part(NZ - 1, odd))

    moves = [(0, keep_ref), (NZ // 2, across_ref)]
    for k, ref in enumerate(ship_refs):
        up, down = k + 1, NZ - 1 - k
        moves.append((up + core * (down - up), ref))
        moves.append((down + core * (up - down), give_ref.at[k]))
    copies = [
        pltpu.make_async_copy(dq_ref.at[slot], ref, sems.at[n])
        for n, (slot, ref) in enumerate(moves)
    ]
    for copy in copies:
        copy.start()

    def store(i, carry):
        for ref, block in ((own_ref, 2 * i + core), (away_ref, 2 * i + 1 - core)):
            ref[i, :, :HEAD] = (total_ref[at(block), :HEAD] * SCALE).astype(ref.dtype)
            ref[i, :, HEAD:] = total_ref[at(block), HEAD:].astype(ref.dtype)
        return carry

    lax.fori_loop(0, NZ, store, 0)
    for copy in copies:
        copy.wait()


def attention_grads(links, place, rows, other, seg_cols, seg_rows):
    vmem = pl.BlockSpec(memory_space=pltpu.VMEM)
    smem = pl.BlockSpec(memory_space=pltpu.SMEM)
    return pl.pallas_call(
        attention_kernel,
        out_shape=(pltpu.HBM((BLOCK, 2 * HEAD), jnp.bfloat16),) * (SIDE + 2)
        + (pltpu.HBM((SIDE, BLOCK, 2 * HEAD), jnp.bfloat16),)
        + (
            jax.ShapeDtypeStruct((NZ, BLOCK, 2 * HEAD), jnp.float32),
            jax.ShapeDtypeStruct((NZ, BLOCK, 2 * HEAD), jnp.bfloat16),
        ),
        in_specs=[smem, smem, vmem, vmem, vmem, vmem],
        out_specs=(pl.BlockSpec(memory_space=pltpu.HBM),) * (SIDE + 3) + (vmem, vmem),
        scratch_shapes=[
            pltpu.VMEM((BLOCKS * BLOCK, 2 * HEAD), jnp.bfloat16),
            pltpu.VMEM((HEAD, BLOCKS * BLOCK), jnp.bfloat16),
            pltpu.VMEM((BLOCKS * BLOCK, 2 * HEAD), jnp.float32),
            pltpu.VMEM((NZ, BLOCK, 2 * HEAD), jnp.bfloat16),
        ]
        + [
            pltpu.VMEM((LINKS * BLOCK, 2 * HEAD), jnp.bfloat16),
            pltpu.VMEM((HEAD, LINKS * BLOCK), jnp.bfloat16),
            pltpu.VMEM((LINKS * BLOCK, 2 * HEAD), jnp.bfloat16),
            pltpu.VMEM((LINKS * BLOCK, 2 * HEAD), jnp.bfloat16),
        ]
        * 2
        + [
            pltpu.VMEM((LINKS * BLOCK, 2 * HEAD), jnp.float32),
            pltpu.VMEM((LINKS * BLOCK, 2 * HEAD), jnp.float32),
            pltpu.VMEM((2, BLOCKS * BLOCK, 2 * HEAD), jnp.float32),
            pltpu.VMEM((2, BLOCKS * BLOCK, 2 * HEAD), jnp.bfloat16),
            pltpu.SemaphoreType.DMA((NZ,)),
        ],
        compiler_params=pltpu.CompilerParams(vmem_limit_bytes=32 * MIB),
        cost_estimate=pl.CostEstimate(
            flops=1_000, bytes_accessed=1_000, transcendentals=0
        ),
    )(links, place, rows, other, seg_cols, seg_rows)


PARTS = tuple((shift, first) for shift in (0, -1, 1, 2) for first in (0, NX // 2))


def weight_kernel(place_ref, grads_ref, *refs):
    count = len(PARTS)
    out_ref, held_ref, sems = refs[2 * count :]
    copies = []
    for p in range(count):
        for side in range(NC):
            target = held_ref.at[p, :, pl.ds(side * BLOCK, BLOCK), :]
            copies.append(pltpu.make_async_copy(refs[side * count + p], target, sems.at[p, side]))
    for copy in copies:
        copy.start()
    x, y, core = place_ref[0], place_ref[3], place_ref[2]
    total = None
    for p, (shift, first) in enumerate(PARTS):
        copies[2 * p].wait()
        copies[2 * p + 1].wait()
        for s in range(NX // 2):
            source = (lax.rem(x - first - s + NX, NX) * NY + lax.rem(y + shift + NY, NY)) * NC
            grads = jnp.concatenate([grads_ref[source + core], grads_ref[source + 1 - core]], axis=1)
            part = dot(grads, held_ref[p, s])
            total = part if total is None else total + part
    out_ref[...] = total.T.astype(jnp.bfloat16)


def weight_grads_part(place, grads, own, other):
    half, rows, width = own[0].shape
    vmem = pl.BlockSpec(memory_space=pltpu.VMEM)
    return pl.pallas_call(
        weight_kernel,
        out_shape=jax.ShapeDtypeStruct((width, HEAD), jnp.bfloat16),
        in_specs=[pl.BlockSpec(memory_space=pltpu.SMEM), vmem]
        + [pl.BlockSpec(memory_space=pltpu.HBM)] * (2 * len(PARTS)),
        out_specs=vmem,
        scratch_shapes=[
            pltpu.VMEM((len(PARTS), half, NC * rows, width), jnp.bfloat16),
            pltpu.SemaphoreType.DMA((len(PARTS), NC)),
        ],
        compiler_params=pltpu.CompilerParams(vmem_limit_bytes=24 * MIB),
        cost_estimate=pl.CostEstimate(
            flops=1_100_000_000, bytes_accessed=9 * MIB, transcendentals=0
        ),
    )(place, grads, *placed(own, pltpu.HBM), *placed(other, pltpu.HBM))


def pack_kernel(queries_ref, grads_ref, keys_ref, values_ref, out_ref, *refs):
    q_ref, g_ref, k_ref, v_ref, sem, store_sem = refs
    loads = [
        pltpu.make_async_copy(a, b, sem.at[n])
        for n, (a, b) in enumerate(((queries_ref, q_ref), (grads_ref, g_ref), (keys_ref, k_ref), (values_ref, v_ref)))
    ]
    for copy in loads:
        copy.start()
    stores = []
    for load, ref, first, size, shared in (
        (loads[0], q_ref, 0, 2, 1), (loads[1], g_ref, 2, 2, 1), (loads[2], k_ref, 4, 1, 2), (loads[3], v_ref, 5, 1, 2)
    ):
        load.wait()
        for i in range(NZ):
            source = ref.at[:, pl.ds(size * HEAD * (i // shared), size * HEAD)]
            copy = pltpu.make_async_copy(source, out_ref.at[i, :, pl.ds(first * HEAD, size * HEAD)], store_sem.at[len(stores)])
            copy.start()
            stores.append(copy)
    for copy in stores:
        copy.wait()


def packed(queries, grads, keys, values):
    return pl.pallas_call(
        pack_kernel,
        out_shape=pltpu.HBM((NZ, BLOCK, 6 * HEAD), jnp.bfloat16),
        in_specs=[pl.BlockSpec(memory_space=pltpu.HBM)] * 4,
        out_specs=pl.BlockSpec(memory_space=pltpu.HBM),
        scratch_shapes=[pltpu.VMEM(a.shape, a.dtype) for a in (queries, grads, keys, values)]
        + [pltpu.SemaphoreType.DMA((4,)), pltpu.SemaphoreType.DMA((4 * NZ,))],
        compiler_params=pltpu.CompilerParams(vmem_limit_bytes=16 * MIB),
        cost_estimate=pl.CostEstimate(flops=0, bytes_accessed=3 * MIB, transcendentals=0),
    )(*placed((queries, grads, keys, values), pltpu.HBM))


def pair_kernel(partials_ref, keys_ref, values_ref, chunks_ref):
    for g in range(KV_HEADS):
        pair = partials_ref[2 * g].astype(jnp.float32) + partials_ref[2 * g + 1].astype(jnp.float32)
        pair = pair.astype(jnp.bfloat16)
        for kind, ref in enumerate((keys_ref, values_ref)):
            part = pair[:, kind * HEAD : (kind + 1) * HEAD]
            ref[:, g * HEAD : (g + 1) * HEAD] = part
            part = part.T
            for x in range(NX):
                chunks_ref[(x * NY + g) * NC + kind] = part


def pair_grads(partials):
    vmem = pl.BlockSpec(memory_space=pltpu.VMEM)
    out = jax.ShapeDtypeStruct((BLOCK, KV_HEADS * HEAD), jnp.bfloat16)
    return pl.pallas_call(
        pair_kernel,
        out_shape=(out, out, jax.ShapeDtypeStruct((NX * NY * NC, HEAD, BLOCK), jnp.bfloat16)),
        in_specs=[vmem],
        out_specs=(vmem, vmem, vmem),
        compiler_params=pltpu.CompilerParams(vmem_limit_bytes=16 * MIB),
        cost_estimate=pl.CostEstimate(flops=0, bytes_accessed=2 * MIB, transcendentals=0),
    )(partials)


def join_kernel(place_ref, keep_ref, across_ref, *refs):
    direct_refs, swapped_ref, out_ref = refs[:SIDE], refs[SIDE], refs[SIDE + 1]
    z, side = place_ref[1], 1 - 2 * place_ref[2]

    def put(source, value):
        column = lax.rem(source + NZ, NZ) * (2 * HEAD)
        out_ref[:, pl.ds(pl.multiple_of(column, 2 * HEAD), 2 * HEAD)] = value

    put(z, keep_ref[...])
    put(z + NZ // 2, across_ref[...])
    for k in range(SIDE):
        put(z - side * (k + 1), direct_refs[k][0])
        put(z + side * (k + 1), swapped_ref[k])


def joined(place, keep, across, direct, swapped):
    vmem = pl.BlockSpec(memory_space=pltpu.VMEM)
    return pl.pallas_call(
        join_kernel,
        out_shape=jax.ShapeDtypeStruct((BLOCK, NZ * 2 * HEAD), jnp.bfloat16),
        in_specs=[pl.BlockSpec(memory_space=pltpu.SMEM)] + [vmem] * (SIDE + 3),
        out_specs=vmem,
        compiler_params=pltpu.CompilerParams(vmem_limit_bytes=16 * MIB),
        cost_estimate=pl.CostEstimate(flops=0, bytes_accessed=MIB, transcendentals=0),
    )(place, keep, across, *direct, swapped)


def ring(size, shift):
    return [(i, (i + shift) % size) for i in range(size)]


def swap_cores(a):
    return lax.ppermute(a, "c", [(0, 1), (1, 0)])


def local(layer_input, queries, keys, values, output_grads, block_links, segment_ids):
    x, y, z, core = (lax.axis_index(axis) for axis in ("x", "y", "z", "c"))
    place = jnp.stack([x, z, core, y]).astype(jnp.int32)
    bf16 = jnp.bfloat16

    inputs = layer_input[0]
    width = inputs.shape[1] // NX
    pieces = [
        lax.dynamic_slice_in_dim(inputs, lax.rem(x + s, NX) * width, width, axis=1)
        for s in range(NX)
    ]
    near = lax.ppermute(pieces[1], "x", ring(NX, 1))
    near, later = lax.optimization_barrier((near, pieces[2:]))
    pieces = [pieces[0], near] + [
        lax.ppermute(a, "x", ring(NX, s)) for s, a in enumerate(later, 2)
    ]
    half = NX // 2
    mine = (jnp.stack(pieces[:half]), jnp.stack(pieces[half:]))
    before, after = zip(
        *[[lax.ppermute(a, "y", ring(NY, shift)) for shift in (1, -1)] for a in mine]
    )
    far_low = lax.ppermute(before[0], "y", ring(NY, 1))

    outgoing = packed(queries[0], output_grads[0], keys[0], values[0])
    rows = lax.all_to_all(outgoing, "z", split_axis=0, concat_axis=0, tiled=True)
    seg_rows = segment_ids[0].reshape(BLOCKS, BLOCK)
    seg_cols = jnp.broadcast_to(seg_rows[:, :, None], (BLOCKS, BLOCK, BLOCK))
    rows, mine, before, after, seg_cols = lax.optimization_barrier(
        (rows, mine, before, after, seg_cols)
    )
    other = swap_cores(rows[..., 4 * HEAD :])
    keep, across, *ship, give, own, away = attention_grads(
        block_links[0], place, rows, other, seg_cols, seg_rows
    )
    inputs_own = mine + before + after + (far_low,)
    keep, across, ship, give, own, away, inputs_own = lax.optimization_barrier(
        (keep, across, ship, give, own, away, inputs_own)
    )
    far_high = lax.ppermute(inputs_own[5], "y", ring(NY, -1))
    inputs_own = tuple(inputs_own) + (far_high,)
    inputs_other = tuple(swap_cores(a) for a in inputs_own)

    pair = (own + swap_cores(away).astype(jnp.float32)).astype(bf16)
    pair = lax.all_to_all(pair, "z", split_axis=0, concat_axis=0, tiled=True)
    given = swap_cores(give)
    across, ship, given, pair, inputs_other = lax.optimization_barrier(
        (across, ship, given, pair, inputs_other)
    )
    key_grads, value_grads, chunks = pair_grads(pair)

    grads = lax.all_to_all(chunks, ("x", "y", "c"), split_axis=0, concat_axis=0, tiled=True)
    direct = []
    for k in range(SIDE):
        hops = [((i, 0), ((i + k + 1) % NZ, 0)) for i in range(NZ)]
        hops += [((i, 1), ((i - k - 1) % NZ, 1)) for i in range(NZ)]
        hops = [tuple(a * NC + b for a, b in hop) for hop in hops]
        direct.append(lax.ppermute(jnp.stack([ship[k], given[k]]), ("z", "c"), hops))
    across = lax.ppermute(across, "z", ring(NZ, NZ // 2))
    grads, direct, across = lax.optimization_barrier((grads, direct, across))
    part = weight_grads_part(place, grads, inputs_own, inputs_other)

    swapped = swap_cores(jnp.stack([a[1] for a in direct]))
    query_grads = joined(place, keep, across, direct, swapped)
    part = part.reshape(NY * NZ * NC, -1, HEAD)
    part = lax.all_to_all(part, ("y", "z", "c"), split_axis=0, concat_axis=0, tiled=True)
    part = part.reshape(NY, NZ, NC, -1, HEAD).astype(jnp.float32)
    part = jnp.transpose(jnp.sum(part, axis=1), (1, 2, 0, 3))
    part = part.reshape(NC, -1, NY * HEAD)
    return query_grads[None], key_grads[None], value_grads[None], part[0], part[1]


def solution(mesh):
    chips = Mesh(mesh.devices.reshape(NX, NY, NZ, NC), ("x", "y", "z", "c"))
    dp, seq = ("x", "y"), ("z", "c")
    by_position = P(dp, seq, None)
    return jax.shard_map(
        local,
        mesh=chips,
        in_specs=(by_position,) * 5 + (P(dp, None, None), P(dp, None)),
        out_specs=(by_position,) * 3 + (P(dp + seq, None),) * 2,
        check_vma=False,
    )
```
